32 devices in a mesh: clip: 8 (over y, x, core), tm: 4 (over z).
Axes of the slice: x: 2, y: 2, z: 4, core: 2. Of those that a mesh axis runs over, the one named last changes fastest.
Arguments:
- tokens: bfloat16 [2, 16, 2048, 1024], P(None, 'tm', 'clip'), may hold values from -6 to 6
- segments: int32 [2, 2048], P(None, 'clip'), may hold values from 0 to 3, as said below
- assignment: int32 [2, 32], P(None, 'clip'), may hold values from 0 to 31, as said below
- actions: int32 [2, 32, 16], P(None, None, 'tm'), may hold values from 0 to 7
- norm_gain: bfloat16 [3, 1024], P(None, 'clip'), may hold values from 0.099609375 to 1.8984375
- norm_bias: bfloat16 [3, 1024], P(None, 'clip'), may hold values from -1.75 to 1.75
- space_in_weight: bfloat16 [1024, 3072], P('clip'), may hold values from -0.1875 to 0.1875
- space_out_weight: bfloat16 [1024, 1024], P('clip'), may hold values from -1.5 to 1.5
- time_in_weight: bfloat16 [1024, 3072], P('clip'), may hold values from -0.1875 to 0.1875
- time_out_weight: bfloat16 [1024, 1024], P('clip'), may hold values from -0.5 to 0.5
- hidden_weight: bfloat16 [1024, 4096], P('clip'), may hold values from -0.1875 to 0.1875
- hidden_bias: bfloat16 [4096], P('clip'), may hold values from -3 to 3
- output_weight: bfloat16 [4096, 1024], P('clip'), may hold values from -0.09375 to 0.09375
- output_bias: bfloat16 [1024], P('clip'), may hold values from -3 to 3
- action_table: bfloat16 [8, 1024], P(None, 'clip'), may hold values from -3 to 3
- out_grad: float32 [2, 16, 2048, 1024], P(None, 'tm', 'clip'), may hold values from -6 to 6
Outputs:
- block_out: bfloat16 [2, 16, 2048, 1024], P(None, 'tm', 'clip')
- tokens_grad: float32 [2, 16, 2048, 1024], P(None, 'tm', 'clip')
- norm_gain_grad: float32 [3, 1024], P(None, 'clip')
- norm_bias_grad: float32 [3, 1024], P(None, 'clip')
- space_in_grad: float32 [1024, 3072], P('clip')
- space_out_grad: float32 [1024, 1024], P('clip')
- time_in_grad: float32 [1024, 3072], P('clip')
- time_out_grad: float32 [1024, 1024], P('clip')
- hidden_grad: float32 [1024, 4096], P('clip')
- hidden_bias_grad: float32 [4096], P('clip')
- output_grad: float32 [4096, 1024], P('clip')
- output_bias_grad: float32 [1024], P('clip')
- action_table_grad: float32 [8, 1024], P(None, 'clip')
The draws below stay inside these ranges and needn't reach their ends.
Inputs may be any that keep to these rules, and one draw needn't show every extreme that they name: `segments`: on every clip index and micro-batch the 256 positions hold first some clips of 256 positions, then clips of 64 positions, numbered upward from 0 in that order; every frame uses the same numbering. `assignment`: each row is a permutation of the 32 clip numbers; numbers of local clips that a clip index does not use are read by nobody.
All inputs are finite; a program needn't handle non-finite values.
Results may differ from the reference program's by a relative error of at most 0.018.
Values may be sent and summed in bfloat16 or wider, within the bound.
No kernel may reach another device: no remote copies, remote signals or barrier semaphores. Data moves between devices by JAX's collectives and lax.ppermute only.
A program may use at most 512 MiB of HBM per device.

```python
import jax
import jax.numpy as jnp
from jax import lax

D = 1024
HEADS = 16
HEAD_DIM = 64
FF = 4096
NACT = 8
MICRO = 2
BIG = 256
SMALL = 64
SLOTS = 256
FRAMES = 16
SLOTS_ALL = 2048
MAXSEG = 4
CLIPS = 32
N_CLIP = 8


def draw_segments(key, part):
    key = jax.random.fold_in(key, 11)
    device_count = SLOTS_ALL // SLOTS
    count_key = jax.random.fold_in(key, 1)
    pick_key = jax.random.fold_in(key, 2)
    big_count = jax.random.randint(count_key, (MICRO, device_count), 0, SLOTS // BIG + 1)
    empty_device = jax.random.randint(pick_key, (MICRO, 1), 0, device_count)
    big_count = jnp.where(jnp.arange(device_count)[None, :] == empty_device, 0, big_count)
    position = jnp.arange(SLOTS)[None, None, :]
    big_edge = big_count[:, :, None] * BIG
    labels = jnp.where(position < big_edge, position // BIG, big_count[:, :, None] + (position - big_edge) // SMALL)
    return labels.reshape(MICRO, SLOTS_ALL).astype(jnp.int32)


def draw_assignment(key, part):
    key = jax.random.fold_in(key, 23)
    perm_rows = [jax.random.permutation(jax.random.fold_in(key, micro_index), CLIPS) for micro_index in range(MICRO)]
    return jnp.stack(perm_rows).astype(jnp.int32)


def place_ends(drawn, own_key, low, top_value):
    extent = drawn.shape
    spot = [jax.random.randint(jax.random.fold_in(own_key, axis), (), 0, extent[axis]) for axis in range(len(extent))]
    drawn = drawn.at[tuple(spot)].set(low)
    longest = extent.index(max(extent))
    spot[longest] = (spot[longest] + 1) % extent[longest]
    return drawn.at[tuple(spot)].set(top_value)


def level_of(own_key, shape, pieces, least, largest):
    def one(axis_at, shards_of):
        draws = jax.random.uniform(jax.random.fold_in(jax.random.fold_in(own_key, 6), axis_at), (shards_of,), jnp.float32, least / len(pieces), largest / len(pieces))
        return jnp.repeat(jnp.exp(draws), shape[axis_at] // shards_of).reshape((-1,) + (1,) * (len(shape) - axis_at - 1))

    loudness = one(*pieces[0])
    for cut in pieces[1:]:
        loudness = loudness * one(*cut)
    return loudness


def gaussian(own_key, extent, scale, limit, cuts=(), kind=jnp.bfloat16):
    values = scale * jax.random.normal(own_key, extent, jnp.float32)
    if cuts:
        values = values * level_of(own_key, extent, cuts, -0.22, 0.18)
    return jnp.clip(values, -limit, limit).astype(kind)


def setup_inputs(seed: int = 0) -> dict:
    splits = jax.random.split(jax.random.key(seed), 17)
    return {
        "tokens": gaussian(splits[0], (MICRO, FRAMES, SLOTS_ALL, D), 1.0, 6.0, ((1, 4), (2, 8))),
        "segments": draw_segments(jax.random.fold_in(splits[16], 71), 0),
        "assignment": draw_assignment(jax.random.fold_in(splits[16], 71), 0),
        "actions": place_ends(jax.random.randint(splits[3], (MICRO, CLIPS, FRAMES), 0, NACT), jax.random.fold_in(splits[3], 1), 0, NACT - 1).astype(jnp.int32),
        "norm_gain": jnp.clip(1.0 + 0.18 * jax.random.normal(splits[4], (3, D), jnp.float32), 0.099609375, 1.8984375).astype(jnp.bfloat16),
        "norm_bias": gaussian(splits[5], (3, D), 0.3, 1.75, ((1, 8),)),
        "space_in_weight": gaussian(splits[6], (D, 3 * D), D ** -0.5, 0.1875, ((0, 8),)),
        "space_out_weight": gaussian(splits[7], (D, D), (D // 64) ** -0.5, 1.5, ((0, 8),)),
        "time_in_weight": gaussian(splits[8], (D, 3 * D), D ** -0.5, 0.1875, ((0, 8),)),
        "time_out_weight": gaussian(splits[9], (D, D), (D // 8) ** -0.5, 0.5, ((0, 8),)),
        "hidden_weight": gaussian(splits[10], (D, FF), D ** -0.5, 0.1875, ((0, 8),)),
        "hidden_bias": gaussian(splits[11], (FF,), 0.5, 3.0, ((0, 8),)),
        "output_weight": gaussian(splits[12], (FF, D), FF ** -0.5, 0.09375, ((0, 8),)),
        "output_bias": gaussian(splits[13], (D,), 0.5, 3.0, ((0, 8),)),
        "action_table": gaussian(splits[14], (NACT, D), 0.5, 3.0, ((1, 8),)),
        "out_grad": gaussian(splits[15], (MICRO, FRAMES, SLOTS_ALL, D), 1.0, 6.0, ((1, 4), (2, 8)), jnp.float32),
    }


@jax.custom_vjp
def low(v):
    return lax.optimization_barrier(v.astype(jnp.bfloat16)).astype(jnp.float32)

@jax.custom_vjp
def low_back(v):
    return v

def low_keep(v):
    return (low(v), None)

def low_pass(kept, grad):
    return (grad,)

def back_keep(v):
    return (v, None)

def back_low(kept, grad):
    return (low(grad),)
low.defvjp(low_keep, low_pass)
low_back.defvjp(back_keep, back_low)

def layer_norm(values, norm_gains, shifts):
    centered = values - lax.optimization_barrier(jnp.mean(values, axis=-1, keepdims=True))
    spread = lax.optimization_barrier(jnp.mean(centered * centered, axis=-1, keepdims=True))
    return centered * lax.rsqrt(spread + 1e-05) * norm_gains + shifts

def project(left, right):
    return jnp.einsum('fsd,de->fse', left, right, precision=lax.Precision.HIGHEST)

def softmax_rows(scores):
    row_top = lax.optimization_barrier(jnp.max(scores, axis=-1, keepdims=True))
    raised = jnp.exp(scores - row_top)
    return raised / lax.optimization_barrier(jnp.sum(raised, axis=-1, keepdims=True))

def space_block(portions):
    queries, key_rows, value_rows, labels = portions
    score_scale = queries.shape[-1] ** (-0.5)
    raw_scores = low_back(jnp.einsum('qhe,khe->hqk', queries, key_rows, precision=lax.Precision.HIGHEST) * score_scale)
    same_clip = labels[:, None] == labels[None, :]
    scores = jnp.where(same_clip[None], raw_scores, -1e+30)
    attn_probs = low(softmax_rows(scores))
    return jnp.einsum('hqk,khe->qhe', attn_probs, value_rows, precision=lax.Precision.HIGHEST)

def time_attention(queries, key_rows, value_rows):
    score_scale = queries.shape[-1] ** (-0.5)
    raw_scores = low_back(jnp.einsum('qshe,kshe->shqk', queries, key_rows, precision=lax.Precision.HIGHEST) * score_scale)
    frame_order = jnp.arange(queries.shape[0])
    causal = frame_order[:, None] >= frame_order[None, :]
    scores = jnp.where(causal[None, None], raw_scores, -1e+30)
    attn_probs = low(softmax_rows(scores))
    return jnp.einsum('shqk,kshe->qshe', attn_probs, value_rows, precision=lax.Precision.HIGHEST)

def reference(tokens, segments, assignment, actions, norm_gain, norm_bias, space_in_weight, space_out_weight, time_in_weight, time_out_weight, hidden_weight, hidden_bias, output_weight, output_bias, action_table, out_grad):
    owner_rows = (jnp.arange(SLOTS_ALL) // SLOTS).astype(jnp.int32)
    action_list = []
    for micro_index in range(MICRO):
        flat_index = (owner_rows * MAXSEG + segments[micro_index]).astype(jnp.int32)
        clip_ids = assignment[micro_index][flat_index]
        action_list.append(jnp.transpose(actions[micro_index][clip_ids]))
    action_ids = jnp.stack(action_list)

    def forward(inputs, gain_rows, shift_rows, space_in, space_out, time_in, time_out, hidden_full, hidden_shift, output_full, output_shift, table_full):
        results = []
        for micro_index in range(MICRO):
            embedded = inputs[micro_index] + table_full[action_ids[micro_index]]
            norm_one = low(layer_norm(embedded, gain_rows[0], shift_rows[0]))
            space_packed = low(low_back(project(norm_one, space_in)))
            block_shape = (FRAMES * N_CLIP, SLOTS, HEADS, HEAD_DIM)
            space_parts = [space_packed[..., part_index * D:(part_index + 1) * D].reshape(block_shape) for part_index in range(3)]
            label_rows = jnp.broadcast_to(segments[micro_index].reshape(1, N_CLIP, SLOTS), (FRAMES, N_CLIP, SLOTS)).reshape(FRAMES * N_CLIP, SLOTS)
            space_mixed = lax.map(jax.checkpoint(space_block), (space_parts[0], space_parts[1], space_parts[2], label_rows))
            space_mixed = low(low_back(space_mixed.reshape(FRAMES, SLOTS_ALL, D)))
            after_space = embedded + low_back(project(space_mixed, space_out))
            norm_two = low(layer_norm(after_space, gain_rows[1], shift_rows[1]))
            time_packed = low(low_back(project(norm_two, time_in)))
            head_shape = (FRAMES, SLOTS_ALL, HEADS, HEAD_DIM)
            time_parts = [time_packed[..., part_index * D:(part_index + 1) * D].reshape(head_shape) for part_index in range(3)]
            time_mixed = time_attention(time_parts[0], time_parts[1], time_parts[2])
            time_mixed = low(low_back(time_mixed.reshape(FRAMES, SLOTS_ALL, D)))
            after_time = after_space + low_back(project(time_mixed, time_out))
            norm_three = low(layer_norm(after_time, gain_rows[2], shift_rows[2]))
            pre_act = low_back(project(norm_three, hidden_full) + hidden_shift)
            activation = low(jax.nn.gelu(pre_act, approximate=True))
            branch = low_back(project(activation, output_full) + output_shift)
            results.append(after_time + branch)
        return jnp.stack(results)
    float_args = (tokens.astype(jnp.float32), norm_gain.astype(jnp.float32), norm_bias.astype(jnp.float32), space_in_weight.astype(jnp.float32), space_out_weight.astype(jnp.float32), time_in_weight.astype(jnp.float32), time_out_weight.astype(jnp.float32), hidden_weight.astype(jnp.float32), hidden_bias.astype(jnp.float32), output_weight.astype(jnp.float32), output_bias.astype(jnp.float32), action_table.astype(jnp.float32))
    result, pullback = jax.vjp(forward, *float_args)
    grads = pullback(out_grad)
    return (result.astype(jnp.bfloat16), grads[0], grads[1], grads[2], grads[3], grads[4], grads[5], grads[6], grads[7], grads[8], grads[9], grads[10], grads[11])
```

```python
import functools

import jax
import jax.numpy as jnp
from jax import lax
from jax.experimental import pallas as pl
from jax.experimental.pallas import tpu as pltpu
from jax.sharding import PartitionSpec as P

HEADS = 16
HEAD = 64
EPS = 1e-05
MASKED = -1e30
ROWS = 256
CHUNK = 1024
VMEM_LIMIT = 62 * 1024 * 1024

bf16 = jnp.bfloat16
f32 = jnp.float32

NN = (((1,), (0,)), ((), ()))
NT = (((1,), (1,)), ((), ()))
TN = (((0,), (0,)), ((), ()))


def dot(left, right, form=NN):
    return lax.dot_general(left, right, form, preferred_element_type=f32)


def standardize(values):
    centered = values - jnp.mean(values, axis=-1, keepdims=True)
    rate = lax.rsqrt(jnp.mean(centered * centered, axis=-1, keepdims=True) + EPS)
    return centered * rate, rate


def norm_back(hat, rate, gain, grad):
    scaled = grad * gain
    return rate * (
        scaled
        - jnp.mean(scaled, axis=-1, keepdims=True)
        - hat * jnp.mean(scaled * hat, axis=-1, keepdims=True)
    )


def add_row(ref, row, first):
    @pl.when(first)
    def _():
        ref[...] = row

    @pl.when(jnp.logical_not(first))
    def _():
        ref[...] += row


def column_sum(values):
    return jnp.sum(values, axis=0, keepdims=True)


def pair_slices(pair):
    lane = pair * 128
    return slice(lane, lane + 128), slice(1024 + lane, 1024 + lane + 128), slice(2048 + lane, 2048 + lane + 128)


def attend(qkv_ref, key_mask, query_mask, mixed_t, lse_ref):
    blank = jnp.zeros((HEAD, ROWS), bf16)
    for pair in range(HEADS // 2):
        q_at, k_at, v_at = pair_slices(pair)
        q_t = (qkv_ref[:, q_at] * jnp.asarray(HEAD**-0.5, bf16)).T
        v_t = qkv_ref[:, v_at].T
        keys = jnp.concatenate([qkv_ref[:, k_at], key_mask], axis=1)
        for part in range(2):
            head = pair * 2 + part
            half = slice(part * HEAD, (part + 1) * HEAD)
            parts = [q_t[half], blank] if part == 0 else [blank, q_t[half]]
            scores = dot(keys, jnp.concatenate(parts + [query_mask], axis=0))
            top = jnp.max(scores, axis=0, keepdims=True)
            raised = jnp.exp(scores - top)
            total = jnp.sum(raised, axis=0, keepdims=True)
            mixed = dot(v_t[half], raised.astype(bf16))
            mixed_t[head * HEAD : (head + 1) * HEAD, :] = (mixed * (1.0 / total)).astype(bf16)
            lse_ref[head : head + 1, :] = top + jnp.log(total)


def attend_back(qkv_ref, key_mask, query_mask, lse_ref, grad_ref, grad_t, mixed_t, out_ref, query_t):
    blank = jnp.zeros((HEAD, ROWS), bf16)
    scale = jnp.asarray(HEAD**-0.5, bf16)
    low_half = lax.broadcasted_iota(jnp.int32, (ROWS, 128), 1) < HEAD
    for pair in range(HEADS // 2):
        q_at, k_at, v_at = pair_slices(pair)
        queries = qkv_ref[:, q_at] * scale
        keys = qkv_ref[:, k_at]
        values = qkv_ref[:, v_at]
        grads = grad_ref[:, q_at]
        q_t = queries.T
        k_t = (keys * scale).T
        keys_masked = jnp.concatenate([keys, key_mask], axis=1)
        grad_keys = grad_values = None
        for part in range(2):
            head = pair * 2 + part
            half = slice(part * HEAD, (part + 1) * HEAD)
            at = slice(head * HEAD, (head + 1) * HEAD)
            parts = [q_t[half], blank] if part == 0 else [blank, q_t[half]]
            scores = dot(keys_masked, jnp.concatenate(parts + [query_mask], axis=0))
            probs = jnp.exp(scores - lse_ref[head : head + 1, :])
            head_grad = grad_t[at, :]
            grad_parts = [head_grad, blank] if part == 0 else [blank, head_grad]
            grad_probs = dot(values, jnp.concatenate(grad_parts, axis=0))
            along = jnp.sum(head_grad.astype(f32) * mixed_t[at, :].astype(f32), axis=0, keepdims=True)
            grad_scores = (probs * (grad_probs - along)).astype(bf16)
            keep = low_half if part == 0 else jnp.logical_not(low_half)
            zero = jnp.zeros_like(queries)
            gv = dot(probs.astype(bf16), jnp.where(keep, grads, zero))
            gk = dot(grad_scores, jnp.where(keep, queries, zero))
            grad_values = gv if grad_values is None else grad_values + gv
            grad_keys = gk if grad_keys is None else grad_keys + gk
            query_t[at, :] = dot(k_t[half], grad_scores).astype(bf16)
        out_ref[:, k_at] = grad_keys.astype(bf16)
        out_ref[:, v_at] = grad_values.astype(bf16)
    for quarter in range(4):
        at = slice(quarter * 256, (quarter + 1) * 256)
        out_ref[:, at] = query_t[at, :].T


def block_of(weights, index):
    own = 1024 // weights.shape[0]
    return weights[:, index * own : (index + 1) * own, :].reshape(1024, 1024)


def piece_at(place, step, count, rows):
    return pl.ds(pl.multiple_of(lax.rem(place[0] + step, count) * rows, rows), rows)


def stacked(refs):
    parts = [ref[...].reshape(-1, ref.shape[-1]) for ref in refs]
    return parts[0] if len(parts) == 1 else jnp.concatenate(parts, axis=0)


def unstack(refs, values):
    rows = values.shape[0] // len(refs)
    for index, ref in enumerate(refs):
        ref[...] = values[index * rows : (index + 1) * rows].reshape(ref.shape)


def space_forward(
    place, tok, hot, kmask, qmask, gain, bias, table, weights,
    norm_out, qkv_out, mix_out, lse_out, *rest,
):
    after_out, (mixed_t, after) = rest[:-2], rest[-2:]
    embedded = tok[...].astype(f32) + dot(hot[...], table[...])
    hat, _ = standardize(embedded)
    normed = (hat * gain[0:1, :] + bias[0:1, :]).astype(bf16)
    norm_out[...] = normed
    for part in range(3):
        qkv_out[:, part * 1024 : (part + 1) * 1024] = dot(normed, block_of(weights, part)).astype(bf16)
    attend(qkv_out, kmask[...], qmask[...], mixed_t, lse_out)
    mixed = mixed_t[...].T
    mix_out[...] = mixed
    after[...] = (embedded + dot(mixed, block_of(weights, 3))).astype(bf16)
    count = len(after_out)
    for step in range(count):
        after_out[step][...] = after[piece_at(place, step, count, ROWS // count), :]


def grad_into_norm(gqkv, weights):
    total = None
    for part in range(3):
        piece = dot(gqkv[:, part * 1024 : (part + 1) * 1024], block_of(weights, part), NT)
        total = piece if total is None else total + piece
    return total


def space_backward(count, *refs):
    grads, refs = refs[:count], refs[count:]
    (
        place, tok, hot, kmask, qmask, gain, table, weights, qkv, mix, lse,
        gqkv_out, gas_out, tok_out, gain_out, bias_out, table_out, grad_t, mixed_t, query_t, grad_rows,
    ) = refs
    first = pl.program_id(0) == 0
    for step in range(count):
        gas_out[piece_at(place, step, count, ROWS // count), :] = grads[step][...]
    upstream = gas_out[...]
    mixed_t[...] = mix[...].T
    grad_rows[...] = dot(upstream, block_of(weights, 3), NT).astype(bf16)
    grad_t[...] = grad_rows[...].T
    attend_back(qkv, kmask[...], qmask[...], lse, grad_rows, grad_t, mixed_t, gqkv_out, query_t)
    grad_norm = grad_into_norm(gqkv_out, weights)
    embedded = tok[...].astype(f32) + dot(hot[...], table[...])
    hat, rate = standardize(embedded)
    add_row(gain_out, column_sum(grad_norm * hat), first)
    add_row(bias_out, column_sum(grad_norm), first)
    total = upstream.astype(f32) + norm_back(hat, rate, gain[0:1, :], grad_norm)
    tok_out[...] = total
    add_row(table_out, dot(hot[...], total.astype(bf16), TN), first)


def time_forward(count, *refs):
    x, refs = refs[:count], refs[count:]
    kmask, qmask, gain, bias, weights, norm_out, qkv_out, mix_out, lse_out, after_out, mixed_t = refs
    after_space = stacked(x).astype(f32)
    hat, _ = standardize(after_space)
    normed = (hat * gain[1:2, :] + bias[1:2, :]).astype(bf16)
    norm_out[...] = normed
    for part in range(3):
        qkv_out[:, part * 1024 : (part + 1) * 1024] = dot(normed, block_of(weights, part)).astype(bf16)
    attend(qkv_out, kmask[...], qmask[...], mixed_t, lse_out)
    mixed = mixed_t[...].T
    mix_out[...] = mixed
    after_out[...] = after_space + dot(mixed, block_of(weights, 3))


def feed_forward(count, *refs):
    grad, refs = refs[:count], refs[count:]
    x, gain, bias, hidden_bias, out_bias, weights = refs[:6]
    norm_out, act_out, gpre_out, gat_out, branch_out, gain_out, bias_out, hb_out, ob_out = refs[6:15]
    block_out = refs[15:]
    first = pl.program_id(0) == 0
    after_time = x[...]
    hat, rate = standardize(after_time)
    normed = (hat * gain[2:3, :] + bias[2:3, :]).astype(bf16)
    norm_out[...] = normed
    branch = stacked(grad)
    branch_out[...] = branch
    clips = weights.shape[0]
    own = 1024 // clips
    per_chunk = clips // 4
    result = None
    grad_norm = None
    for chunk in range(4):
        at = slice(chunk * 1024, (chunk + 1) * 1024)
        w_hidden = block_of(weights, chunk)
        w_down = weights[chunk * per_chunk : (chunk + 1) * per_chunk, 4 * own :, :].reshape(1024, 1024)
        u = dot(normed, w_hidden) + hidden_bias[0:1, at]
        c0 = 0.7978845608028654
        square = u * u
        t = jnp.tanh(u * (c0 + (c0 * 0.044715) * square))
        half_plus = 0.5 + 0.5 * t
        act = (u * half_plus).astype(bf16)
        act_out[:, at] = act
        down = dot(act, w_down)
        result = down if result is None else result + down
        slope = half_plus + (0.5 * u) * (1.0 - t * t) * (c0 + (3.0 * c0 * 0.044715) * square)
        gpre = (dot(branch, w_down, NT) * slope).astype(bf16)
        gpre_out[:, at] = gpre
        back = dot(gpre, w_hidden, NT)
        grad_norm = back if grad_norm is None else grad_norm + back
    block = (after_time + result + out_bias[0:1, :]).astype(bf16)
    unstack(block_out, block)
    upstream = branch.astype(f32)
    gat_out[...] = (upstream + norm_back(hat, rate, gain[2:3, :], grad_norm)).astype(bf16)
    add_row(gain_out, column_sum(grad_norm * hat), first)
    add_row(bias_out, column_sum(grad_norm), first)
    add_row(ob_out, column_sum(upstream), first)
    add_row(hb_out, column_sum(gpre_out[...].astype(f32)), first)


def time_backward(count, *refs):
    x, refs = refs[:count], refs[count:]
    gat, kmask, qmask, gain, weights, qkv, mix, lse, gqkv_out, gain_out, bias_out = refs[:11]
    gas_out = refs[11 : 11 + count]
    grad_t, mixed_t, query_t, grad_rows = refs[11 + count :]
    first = pl.program_id(0) == 0
    upstream = gat[...]
    mixed_t[...] = mix[...].T
    grad_rows[...] = dot(upstream, block_of(weights, 3), NT).astype(bf16)
    grad_t[...] = grad_rows[...].T
    attend_back(qkv, kmask[...], qmask[...], lse, grad_rows, grad_t, mixed_t, gqkv_out, query_t)
    grad_norm = grad_into_norm(gqkv_out, weights)
    hat, rate = standardize(stacked(x).astype(f32))
    add_row(gain_out, column_sum(grad_norm * hat), first)
    add_row(bias_out, column_sum(grad_norm), first)
    total = upstream.astype(f32) + norm_back(hat, rate, gain[1:2, :], grad_norm)
    unstack(gas_out, total.astype(bf16))


def assemble(count, *refs):
    place, parts, out = refs[0], refs[1:-1], refs[-1]
    for micro in range(out.shape[0]):
        for step in range(count):
            out[micro, piece_at(place, step, count, ROWS // count), :] = parts[micro * count + step][...]


def rows_of(ref):
    value = ref[...]
    return value.reshape(-1, value.shape[-1])


def weight_kernel(pairs, micros, own, by_rows, has_small, *refs):
    out = refs[-1]
    offset = 0
    for pair in range(pairs):
        base = pair * 2 * micros
        total = None
        for index in range(micros):
            piece = dot(rows_of(refs[base + index]), rows_of(refs[base + micros + index]), TN)
            total = piece if total is None else total + piece
        total = total.astype(bf16)
        if by_rows:
            out[0] = total
            continue
        for block in range(total.shape[1] // 1024):
            for shard in range(out.shape[0]):
                out[shard, offset : offset + own, :] = total[
                    shard * own : (shard + 1) * own, block * 1024 : (block + 1) * 1024
                ]
            offset += own
    if has_small:
        out[:, offset:, :] = refs[pairs * 2 * micros][...]


def params():
    return pltpu.CompilerParams(vmem_limit_bytes=VMEM_LIMIT)


def ordered_call(kernel, behind, in_specs, **options):
    count = len(behind)

    def body(*refs):
        kernel(*refs[count:])

    aliases = options.pop("input_output_aliases", {})
    call = pl.pallas_call(
        body,
        in_specs=[pl.BlockSpec(memory_space=pl.ANY)] * count + in_specs,
        input_output_aliases={count + k: v for k, v in aliases.items()},
        compiler_params=params(),
        **options,
    )
    return lambda *operands: call(*behind, *operands)


def whole(shape):
    rank = len(shape)
    return pl.BlockSpec(shape, lambda i: (0,) * rank, pipeline_mode=pl.Buffered(1))


def total_spec(shape):
    rank = len(shape)
    return pl.BlockSpec(shape, lambda i: (0,) * rank)


def step_spec(shape):
    rank = len(shape)
    return pl.BlockSpec((None,) + shape, lambda i: (i,) + (0,) * rank)


def micro_spec(micro, shape):
    rank = len(shape)
    return pl.BlockSpec((None, None) + shape, lambda i: (micro, i) + (0,) * rank)


def shape_of(shape, kind):
    return jax.ShapeDtypeStruct(shape, kind)


def smem():
    return pl.BlockSpec(memory_space=pltpu.SMEM)


def call_space_forward(behind, micro, place, tok, hot, kmask, qmask, gain, bias, table, weights, count):
    _, frames, slots, width = tok.shape
    per = slots // count
    return ordered_call(
        space_forward,
        behind,
        grid=(frames,),
        in_specs=[smem(), micro_spec(micro, (slots, width)), step_spec(hot.shape[1:])]
        + [whole(a.shape) for a in (kmask, qmask, gain, bias, table, weights)],
        out_specs=[
            step_spec((slots, width)), step_spec((slots, 3 * width)), step_spec((slots, width)),
            step_spec((HEADS, slots)),
        ]
        + [step_spec((per, width))] * count,
        out_shape=[
            shape_of((frames, slots, width), bf16), shape_of((frames, slots, 3 * width), bf16),
            shape_of((frames, slots, width), bf16), shape_of((frames, HEADS, slots), f32),
        ]
        + [shape_of((frames, per, width), bf16)] * count,
        scratch_shapes=[pltpu.VMEM((width, ROWS), bf16), pltpu.VMEM((ROWS, width), bf16)],
        name="space_forward",
    )(place, tok, hot, kmask, qmask, gain, bias, table, weights)


def back_scratch(width):
    return [
        pltpu.VMEM((width, ROWS), bf16), pltpu.VMEM((width, ROWS), bf16),
        pltpu.VMEM((width, ROWS), bf16), pltpu.VMEM((ROWS, width), bf16),
    ]


def call_space_backward(
    behind, micro, grads, place, tok, hot, kmask, qmask, gain, table, weights, qkv, mix, lse, buffer
):
    micros, frames, slots, width = tok.shape
    count = len(grads)
    row = shape_of((1, width), f32)
    operands = list(grads) + [place, tok, hot, kmask, qmask, gain, table, weights, qkv, mix, lse]
    specs = (
        [step_spec((slots // count, width))] * count
        + [smem(), micro_spec(micro, (slots, width)), step_spec(hot.shape[1:])]
        + [whole(a.shape) for a in (kmask, qmask, gain, table, weights)]
        + [step_spec((slots, 3 * width)), step_spec((slots, width)), step_spec((HEADS, slots))]
    )
    before = len(operands)
    kernel = functools.partial(space_backward, count)
    aliases = {}
    if buffer is not None:
        aliases = {before: 2}
        operands.append(buffer)
        specs.append(pl.BlockSpec(memory_space=pl.ANY))
        kernel = lambda *refs: space_backward(count, *refs[:before], *refs[before + 1 :])
    return ordered_call(
        kernel,
        behind,
        grid=(frames,),
        in_specs=specs,
        out_specs=[
            step_spec((slots, 3 * width)), step_spec((slots, width)), micro_spec(micro, (slots, width)),
            total_spec((1, width)), total_spec((1, width)), total_spec((hot.shape[2], width)),
        ],
        out_shape=[
            shape_of((frames, slots, 3 * width), bf16), shape_of((frames, slots, width), bf16),
            shape_of((micros, frames, slots, width), f32), row, row, shape_of((hot.shape[2], width), f32),
        ],
        scratch_shapes=back_scratch(width),
        input_output_aliases=aliases,
        name="space_backward",
    )(*operands)


def group_spec(array, count):
    frames, _, width = array.shape
    return pl.BlockSpec((frames, ROWS // (frames * count), width), lambda i: (0, i, 0))


def call_time_forward(behind, x, kmask, qmask, gain, bias, weights):
    count = len(x)
    frames, slots, width = x[0].shape
    groups = slots * frames * count // ROWS
    return ordered_call(
        functools.partial(time_forward, count),
        behind,
        grid=(groups,),
        in_specs=[group_spec(a, count) for a in x] + [whole(a.shape) for a in (kmask, qmask, gain, bias, weights)],
        out_specs=[
            step_spec((ROWS, width)), step_spec((ROWS, 3 * width)), step_spec((ROWS, width)),
            step_spec((HEADS, ROWS)), step_spec((ROWS, width)),
        ],
        out_shape=[
            shape_of((groups, ROWS, width), bf16), shape_of((groups, ROWS, 3 * width), bf16),
            shape_of((groups, ROWS, width), bf16), shape_of((groups, HEADS, ROWS), f32),
            shape_of((groups, ROWS, width), f32),
        ],
        scratch_shapes=[pltpu.VMEM((width, ROWS), bf16)],
        name="time_forward",
    )(*x, kmask, qmask, gain, bias, weights)


def call_feed_forward(behind, grad, x, gain, bias, hidden_bias, out_bias, weights):
    count = len(grad)
    groups, _, width = x.shape
    ff = hidden_bias.shape[1]
    row = shape_of((1, width), f32)
    rows = lambda cols: shape_of((groups, ROWS, cols), bf16)
    return ordered_call(
        functools.partial(feed_forward, count),
        behind,
        grid=(groups,),
        in_specs=[group_spec(a, count) for a in grad]
        + [step_spec((ROWS, width))]
        + [whole(a.shape) for a in (gain, bias, hidden_bias, out_bias, weights)],
        out_specs=[
            step_spec((ROWS, width)), step_spec((ROWS, ff)), step_spec((ROWS, ff)),
            step_spec((ROWS, width)), step_spec((ROWS, width)),
            total_spec((1, width)), total_spec((1, width)), total_spec((1, ff)), total_spec((1, width)),
        ]
        + [group_spec(a, count) for a in grad],
        out_shape=[rows(width), rows(ff), rows(ff), rows(width), rows(width), row, row, shape_of((1, ff), f32), row]
        + [shape_of(a.shape, bf16) for a in grad],
        name="feed_forward",
    )(*grad, x, gain, bias, hidden_bias, out_bias, weights)


def call_time_backward(behind, x, gat, kmask, qmask, gain, weights, qkv, mix, lse):
    count = len(x)
    groups, _, width = gat.shape
    row = shape_of((1, width), f32)
    return ordered_call(
        functools.partial(time_backward, count),
        behind,
        grid=(groups,),
        in_specs=[group_spec(a, count) for a in x]
        + [step_spec((ROWS, width))]
        + [whole(a.shape) for a in (kmask, qmask, gain, weights)]
        + [step_spec((ROWS, 3 * width)), step_spec((ROWS, width)), step_spec((HEADS, ROWS))],
        out_specs=[step_spec((ROWS, 3 * width)), total_spec((1, width)), total_spec((1, width))]
        + [group_spec(a, count) for a in x],
        out_shape=[shape_of((groups, ROWS, 3 * width), bf16), row, row] + [shape_of(a.shape, bf16) for a in x],
        scratch_shapes=back_scratch(width),
        name="time_backward",
    )(*x, gat, kmask, qmask, gain, weights, qkv, mix, lse)


def call_assemble(place, parts):
    micros, count = len(parts), len(parts[0])
    frames, per, width = parts[0][0].shape
    flat = [p for pieces in parts for p in pieces]
    return ordered_call(
        functools.partial(assemble, count),
        [],
        grid=(frames,),
        in_specs=[smem()] + [step_spec((per, width))] * len(flat),
        out_specs=pl.BlockSpec((micros, None, per * count, width), lambda i: (0, i, 0, 0)),
        out_shape=shape_of((micros, frames, per * count, width), bf16),
        name="assemble",
    )(place, *flat)


def weight_grad(behind, pairs, clips, rows, name, small=None, buffer=None, down_at=None):
    own = 1024 // clips
    block = 256
    width = pairs[0][0][0].shape[-1]
    by_rows = down_at is not None

    def left_spec(a):
        rank = a.ndim
        return pl.BlockSpec(a.shape[:-1] + (block,), lambda i: (0,) * (rank - 1) + (i,))

    operands, specs = [], []
    cols = 0
    for lefts, rights in pairs:
        operands += list(lefts) + list(rights)
        specs += [left_spec(a) for a in lefts] + [whole(a.shape) for a in rights]
        cols += rights[0].shape[-1]
    shards = block // own
    if small is not None:
        operands.append(small)
        specs.append(pl.BlockSpec((shards,) + small.shape[1:], lambda i: (i, 0, 0)))
    aliases = {}
    if buffer is not None:
        aliases = {len(operands): 0}
        operands.append(buffer)
        specs.append(pl.BlockSpec(memory_space=pl.ANY))
    if by_rows:
        steps = width // clips // block
        out_spec = pl.BlockSpec((1, block, 1024), lambda i: (i // steps, down_at // block + i % steps, 0))
    else:
        out_rows = cols // 1024 * own + (0 if small is None else small.shape[1])
        out_spec = pl.BlockSpec((shards, out_rows, 1024), lambda i: (i, 0, 0))
    return ordered_call(
        functools.partial(weight_kernel, len(pairs), len(pairs[0][0]), own, by_rows, small is not None),
        behind,
        grid=(width // block,),
        in_specs=specs,
        out_specs=out_spec,
        out_shape=shape_of((clips, rows, 1024), bf16),
        input_output_aliases=aliases,
        name=name,
    )(*operands)


def one_hot(index, count, kind=bf16):
    return (index[..., None] == jnp.arange(count)).astype(kind)


def space_masks(labels):
    keys = one_hot(labels, 128)
    queries = jnp.where(labels[None, :] == jnp.arange(128)[:, None], 0.0, MASKED)
    queries = jnp.where(jnp.arange(128)[:, None] < 8, queries, 0.0).astype(bf16)
    return keys, queries


def time_masks(frames, count, me):
    per = ROWS // frames
    row = jnp.arange(ROWS)
    held = frames // count
    frame = jnp.mod(me - row // (held * per), count) * held + row // per % held
    place = row % per
    lane = jnp.arange(128)
    keys = ((lane[None, :] == place[:, None]) | (lane[None, :] == per + frame[:, None])).astype(bf16)
    other = (lane[:, None] < per) & (lane[:, None] != place[None, :])
    later = (lane[:, None] >= per) & (lane[:, None] < per + frames) & (lane[:, None] - per > frame[None, :])
    queries = jnp.where(other | later, MASKED, 0.0).astype(bf16)
    return keys, queries


def action_rows(labels, owners, actions):
    clip_of = jnp.sum(jnp.where(labels[:, None] == jnp.arange(owners.shape[0]), owners[None, :], 0), axis=1)
    hit = clip_of[:, None] == jnp.arange(actions.shape[0])
    chosen = jnp.sum(jnp.where(hit[:, :, None], actions[None], 0), axis=1)
    return jnp.transpose(chosen)


def exchange(values):
    return lax.all_to_all(values, "tm", 0, 0, tiled=True)


def gather(shards):
    own = shards[0].shape[0]
    parts = []
    for shard in shards:
        rows, cols = shard.shape
        parts += [shard[:, at : at + 1024] for at in range(0, cols, 1024)]
    return lax.all_gather(jnp.concatenate(parts, axis=0), "clip", axis=0, tiled=False)


def reduce_clip(total):
    return lax.psum_scatter(total, "clip", scatter_dimension=0, tiled=False)


def shift(values, step):
    count = lax.axis_size("tm")
    return lax.ppermute(values, "tm", [(k, (k + step) % count) for k in range(count)])


def sum_half(part):
    count = lax.axis_size("tm")
    rows = part.shape[0] // count
    me = lax.axis_index("tm")
    piece = lambda step: lax.dynamic_slice_in_dim(part, lax.rem(me + step, count) * rows, rows, axis=0)
    total = piece(0).astype(f32)
    for received in [shift(piece(step), step) for step in range(1, count)]:
        total = total + received.astype(f32)
    return total.astype(bf16)


def share_half(mine):
    count = lax.axis_size("tm")
    rows = mine.shape[0]
    me = lax.axis_index("tm")
    whole_rows = jnp.zeros((count * rows, mine.shape[1]), mine.dtype)
    for step, held in enumerate([mine] + [shift(mine, step) for step in range(1, count)]):
        at = lax.rem(me + count - step, count) * rows
        whole_rows = lax.dynamic_update_slice_in_dim(whole_rows, held, at, axis=0)
    return whole_rows


def mark(values):
    return values.reshape(-1, values.shape[-1])[:8, :128]


def together(*lists):
    flat = lax.optimization_barrier([a for arrays in lists for a in arrays])
    out = []
    for arrays in lists:
        out.append(list(flat[: len(arrays)]))
        flat = flat[len(arrays) :]
    return out


def columns(rows, own, first, count):
    return jnp.concatenate([rows[(first + c) * own : (first + c + 1) * own] for c in range(count)], axis=1).astype(f32)


def local(
    tokens, segments, assignment, actions, norm_gain, norm_bias,
    space_in, space_out, time_in, time_out, hidden, hidden_bias, down, out_bias,
    action_table, out_grad,
):
    micros, frames_here, slots, width = tokens.shape
    pieces = lax.axis_size("tm")
    clips = lax.axis_size("clip")
    frames = frames_here * pieces
    per = slots // pieces
    own = norm_gain.shape[1]
    nact = action_table.shape[0]
    micro = range(micros)
    hb_rows = hidden_bias.shape[0] // own
    small_rows = 6 + nact + hb_rows + 1

    small = jnp.concatenate(
        [norm_gain, norm_bias, action_table, hidden_bias.reshape(-1, own), out_bias.reshape(-1, own)], axis=0
    )
    small_all = lax.all_gather(small, "clip", axis=0, tiled=False)
    w_space = gather([space_in, space_out])
    w_time = gather([time_in, time_out])
    w_ff = gather([hidden, down])

    rows_by = lambda start, count: jnp.transpose(small_all[:, start : start + count], (1, 0, 2)).reshape(count, width)
    gain = rows_by(0, 3).astype(f32)
    bias = rows_by(3, 3).astype(f32)
    table = jnp.pad(rows_by(6, nact), ((0, 128 - nact), (0, 0)))
    hb_all = small_all[:, 6 + nact : 6 + nact + hb_rows].reshape(1, -1).astype(f32)
    ob_all = small_all[:, 6 + nact + hb_rows :].reshape(1, -1).astype(f32)

    me = lax.axis_index("tm").astype(jnp.int32)
    place = me.reshape(1)
    tmasks = time_masks(frames, pieces, me)
    hots = [one_hot(action_rows(segments[m], assignment[m], actions[m]), 128) for m in micro]
    smasks = [space_masks(segments[m]) for m in micro]

    pick = lambda parts, index: [parts[m][index] for m in micro]
    outward = lambda parts: [parts[0]] + [
        lax.ppermute(parts[d], "tm", [(k, (k + d) % pieces) for k in range(pieces)]) for d in range(1, pieces)
    ]
    inward = lambda parts: [parts[0]] + [
        lax.ppermute(parts[d], "tm", [(k, (k - d) % pieces) for k in range(pieces)]) for d in range(1, pieces)
    ]
    marks = lambda parts: [mark(a) for a in parts[1:]]
    rounded = lambda values, d: lax.dynamic_slice_in_dim(values, (me + d) % pieces * per, per, axis=1).astype(bf16)
    sent = [[rounded(out_grad[m], d) for d in range(pieces)] for m in micro]

    branch = [outward(sent[0])]
    forward, after, middle, ahead, pieces_out, back, gas, last = [], [], [], [], [], [], [], []
    behind = []
    for m in micro:
        forward.append(
            call_space_forward(behind, m, place, tokens, hots[m], *smasks[m], gain, bias, table, w_space, pieces)
        )
        after.append(outward(forward[m][4:]))
        behind = [forward[m][3]] + marks(branch[0])
    for m in micro:
        middle.append(list(call_time_forward(behind, after[m], *tmasks, gain, bias, w_time)))
        behind = [middle[m][3]]
    for m in micro[1:]:
        late, (middle[-1][4],) = together(sent[m], [middle[-1][4]])
        branch.append(outward(late))
    for m in micro:
        ahead.append(call_feed_forward(behind, branch[m], middle[m][4], gain, bias, hb_all, ob_all, w_ff))
        pieces_out.append(inward(ahead[m][9:]))
        behind = [ahead[m][5]]
    behind += marks(pieces_out[0])
    ff_grad = weight_grad(behind, [(pick(ahead, 1), pick(ahead, 4))], clips, 8 * own, "down_grad", down_at=4 * own)
    ff_grad = weight_grad([], [(pick(ahead, 0), pick(ahead, 2))], clips, 8 * own, "hidden_grad", buffer=ff_grad)
    (ff_grad,), pieces_out[-1] = together([ff_grad], pieces_out[-1])
    ff_part = reduce_clip(ff_grad)
    behind = [ff_grad]
    for m in micro:
        back.append(
            call_time_backward(
                behind, after[m], ahead[m][3], *tmasks, gain, w_time, middle[m][1], middle[m][2], middle[m][3]
            )
        )
        gas.append(inward(back[m][3:]))
        behind = [back[m][1]]
    time_grad = weight_grad(
        behind, [(pick(middle, 0), pick(back, 0)), (pick(middle, 2), pick(ahead, 3))], clips, 4 * own, "time_grad"
    )
    (time_grad,), gas[0] = together([time_grad], gas[0])
    time_part = reduce_clip(time_grad)
    behind = [time_grad]
    grad_buffer = None
    for m in micro:
        last.append(
            list(
                call_space_backward(
                    behind, m, gas[m], place, tokens, hots[m], *smasks[m], gain, table, w_space,
                    forward[m][1], forward[m][2], forward[m][3], grad_buffer,
                )
            )
        )
        grad_buffer = last[m][2]
        behind = []
        if m == 0:
            (ff_part,), (last[m][3],) = together([ff_part], [last[m][3]])
            ff_half = sum_half(ff_part)
            behind = [mark(ff_part)]

    total = lambda values: functools.reduce(jnp.add, values)
    gain_grad = jnp.concatenate([total(pick(last, 3)), total(pick(back, 1)), total(pick(ahead, 5))])
    bias_grad = jnp.concatenate([total(pick(last, 4)), total(pick(back, 2)), total(pick(ahead, 6))])
    table_grad = total(pick(last, 5))[:nact]
    hb_grad = total(pick(ahead, 7))
    ob_grad = total(pick(ahead, 8))
    split = lambda a: jnp.transpose(a.reshape(a.shape[0], clips, own), (1, 0, 2))
    small_grads = jnp.concatenate(
        [
            split(gain_grad), split(bias_grad), split(table_grad),
            hb_grad.reshape(clips, hb_rows, own), ob_grad.reshape(clips, 1, own),
        ],
        axis=1,
    ).astype(bf16).reshape(clips, -1)
    extra = 8 * pieces - 4 * own % (8 * pieces)
    small_grads = jnp.pad(small_grads, ((0, 0), (0, extra * 1024 - small_grads.shape[1]))).reshape(clips, extra, 1024)
    space_grad = weight_grad(
        [mark(ff_half)], [(pick(forward, 0), pick(last, 0)), (pick(forward, 2), pick(last, 1))],
        clips, 4 * own + extra, "space_grad", small=small_grads,
    )

    ff_sum = lax.psum(ff_part, "tm")
    (ff_half,), (space_grad,) = together([ff_half], [space_grad])
    space_part = reduce_clip(space_grad)
    ff_sum = share_half(ff_half)
    (time_part,), (ff_half,) = together([time_part], [ff_half])
    time_sum = share_half(sum_half(time_part))
    early = (
        call_assemble(place, pieces_out),
        columns(time_sum, own, 0, 3),
        columns(time_sum, own, 3, 1),
        columns(ff_sum, own, 0, 4),
        ff_sum[4 * own :].astype(f32),
    )
    space_part, *early = lax.optimization_barrier((space_part,) + early)
    space_sum = share_half(sum_half(space_part))
    mine = space_sum[4 * own :].reshape(-1)[: small_rows * own].reshape(small_rows, own).astype(f32)
    return (
        early[0],
        grad_buffer,
        mine[0:3],
        mine[3:6],
        columns(space_sum, own, 0, 3),
        columns(space_sum, own, 3, 1),
        early[1],
        early[2],
        early[3],
        mine[6 + nact : 6 + nact + hb_rows].reshape(-1),
        early[4],
        mine[6 + nact + hb_rows :].reshape(-1),
        mine[6 : 6 + nact],
    )


def solution(mesh):
    rows = P("clip", None)
    cols = P(None, "clip")
    line = P("clip")
    wide = P(None, "tm", "clip", None)
    return jax.shard_map(
        local,
        mesh=mesh,
        in_specs=(
            wide, cols, cols, P(None, None, "tm"), cols, cols,
            rows, rows, rows, rows, rows, line, rows, line, cols, wide,
        ),
        out_specs=(wide, wide, cols, cols, rows, rows, rows, rows, rows, line, rows, line, cols),
        check_vma=False,
    )
```

```python
import functools

import jax
import jax.numpy as jnp
from jax import lax
from jax.experimental import pallas as pl
from jax.experimental.pallas import tpu as pltpu
from jax.sharding import PartitionSpec as P

HEADS = 16
HEAD = 64
EPS = 1e-05
MASKED = -1e30
ROWS = 256
FF_CHUNK = 1024
FF_GROUPS = 1
VMEM_LIMIT = 62 * 1024 * 1024

bf16 = jnp.bfloat16
f32 = jnp.float32

NN = (((1,), (0,)), ((), ()))
NT = (((1,), (1,)), ((), ()))
TN = (((0,), (0,)), ((), ()))


def dot(left, right, form=NN):
    return lax.dot_general(left, right, form, preferred_element_type=f32)


def standardize(values):
    centered = values - jnp.mean(values, axis=-1, keepdims=True)
    rate = lax.rsqrt(jnp.mean(centered * centered, axis=-1, keepdims=True) + EPS)
    return centered * rate, rate


def norm_back(hat, rate, gain, grad):
    scaled = grad * gain
    return rate * (
        scaled
        - jnp.mean(scaled, axis=-1, keepdims=True)
        - hat * jnp.mean(scaled * hat, axis=-1, keepdims=True)
    )


def add_row(ref, row, first):
    @pl.when(first)
    def _():
        ref[...] = row

    @pl.when(jnp.logical_not(first))
    def _():
        ref[...] += row


def column_sum(values):
    return jnp.sum(values, axis=0, keepdims=True)


def pair_slices(pair):
    lane = pair * 128
    return slice(lane, lane + 128), slice(1024 + lane, 1024 + lane + 128), slice(2048 + lane, 2048 + lane + 128)


def attend(qkv_ref, key_mask, query_mask, mixed_t, lse_ref):
    blank = jnp.zeros((HEAD, ROWS), bf16)
    scale = jnp.asarray(HEAD**-0.5, bf16)

    def scores_of(pair):
        q_at, k_at, v_at = pair_slices(pair)
        q_t = (qkv_ref[:, q_at] * scale).T
        keys = jnp.concatenate([qkv_ref[:, k_at], key_mask], axis=1)
        first = jnp.concatenate([q_t[:HEAD], blank, query_mask], axis=0)
        second = jnp.concatenate([blank, q_t[HEAD:], query_mask], axis=0)
        return dot(keys, jnp.concatenate([first, second], axis=1))

    def finish(pair, scores):
        v_t = qkv_ref[:, pair_slices(pair)[2]].T
        top = jnp.max(scores, axis=0, keepdims=True)
        raised = jnp.exp(scores - top)
        total = jnp.sum(raised, axis=0, keepdims=True)
        weights = raised.astype(bf16)
        lse = top + jnp.log(total)
        rate = 1.0 / total
        for part in range(2):
            head = pair * 2 + part
            at = slice(part * ROWS, (part + 1) * ROWS)
            mixed = dot(v_t[part * HEAD : (part + 1) * HEAD], weights[:, at])
            mixed_t[head * HEAD : (head + 1) * HEAD, :] = (mixed * rate[:, at]).astype(bf16)
            lse_ref[head : head + 1, :] = lse[:, at]

    queue = [scores_of(0), scores_of(1)]
    for pair in range(HEADS // 2):
        if pair + 2 < HEADS // 2:
            queue.append(scores_of(pair + 2))
        finish(pair, queue.pop(0))


def attend_back(qkv_ref, key_mask, query_mask, lse_ref, grad_ref, grad_t, mixed_t, out_ref, query_t):
    blank = jnp.zeros((HEAD, ROWS), bf16)
    scale = jnp.asarray(HEAD**-0.5, bf16)
    low_half = lax.broadcasted_iota(jnp.int32, (ROWS, 128), 1) < HEAD
    zero = jnp.zeros((ROWS, 128), bf16)

    def both(top, bottom, extra):
        first = jnp.concatenate([top, blank] + extra, axis=0)
        second = jnp.concatenate([blank, bottom] + extra, axis=0)
        return jnp.concatenate([first, second], axis=1)

    def halves(values):
        return jnp.concatenate([jnp.where(low_half, values, zero), jnp.where(low_half, zero, values)], axis=0)

    def start(pair):
        q_at, k_at, v_at = pair_slices(pair)
        q_t = (qkv_ref[:, q_at] * scale).T
        keys = jnp.concatenate([qkv_ref[:, k_at], key_mask], axis=1)
        scores = dot(keys, both(q_t[:HEAD], q_t[HEAD:], [query_mask]))
        pair_t = grad_t[q_at, :]
        grad_probs = dot(qkv_ref[:, v_at], both(pair_t[:HEAD], pair_t[HEAD:], []))
        return scores, grad_probs

    def finish(pair, scores, grad_probs):
        q_at, k_at, v_at = pair_slices(pair)
        head = pair * 2
        lse = jnp.concatenate([lse_ref[head : head + 1, :], lse_ref[head + 1 : head + 2, :]], axis=1)
        product = grad_t[q_at, :].astype(f32) * mixed_t[q_at, :].astype(f32)
        along = jnp.concatenate([column_sum(product[:HEAD]), column_sum(product[HEAD:])], axis=1)
        probs = jnp.exp(scores - lse)
        grad_scores = (probs * (grad_probs - along)).astype(bf16)
        out_ref[:, v_at] = dot(probs.astype(bf16), halves(grad_ref[:, q_at])).astype(bf16)
        out_ref[:, k_at] = dot(grad_scores, halves(qkv_ref[:, q_at] * scale)).astype(bf16)
        k_t = (qkv_ref[:, k_at] * scale).T
        for part in range(2):
            at = slice((head + part) * HEAD, (head + part + 1) * HEAD)
            columns_at = slice(part * ROWS, (part + 1) * ROWS)
            query_t[at, :] = dot(k_t[part * HEAD : (part + 1) * HEAD], grad_scores[:, columns_at]).astype(bf16)

    ahead = start(0)
    for pair in range(HEADS // 2):
        held = ahead
        if pair + 1 < HEADS // 2:
            ahead = start(pair + 1)
        finish(pair, *held)
    for quarter in range(4):
        at = slice(quarter * 256, (quarter + 1) * 256)
        out_ref[:, at] = query_t[at, :].T


def block_of(weights, index):
    own = 1024 // weights.shape[0]
    return weights[:, index * own : (index + 1) * own, :].reshape(1024, 1024)


def piece_at(place, step, count, rows):
    return pl.ds(pl.multiple_of(lax.rem(place[0] + step, count) * rows, rows), rows)


def stacked(refs, groups=1):
    per = refs[0].shape[1] // groups
    width = refs[0].shape[-1]
    parts = [ref[:, g * per : (g + 1) * per, :].reshape(-1, width) for g in range(groups) for ref in refs]
    return parts[0] if len(parts) == 1 else jnp.concatenate(parts, axis=0)


def unstack(refs, values, groups=1):
    per = refs[0].shape[1] // groups
    rows = values.shape[0] // (len(refs) * groups)
    for g in range(groups):
        for index, ref in enumerate(refs):
            at = (g * len(refs) + index) * rows
            ref[:, g * per : (g + 1) * per, :] = values[at : at + rows].reshape(ref.shape[0], per, ref.shape[2])


def space_forward(
    place, tok, hot, kmask, qmask, gain, bias, table, weights,
    norm_out, qkv_out, mix_out, lse_out, *rest,
):
    after_out, (mixed_t, after) = rest[:-2], rest[-2:]
    embedded = tok[...].astype(f32) + dot(hot[...], table[...])
    hat, _ = standardize(embedded)
    normed = (hat * gain[0:1, :] + bias[0:1, :]).astype(bf16)
    norm_out[...] = normed
    for part in range(3):
        qkv_out[:, part * 1024 : (part + 1) * 1024] = dot(normed, block_of(weights, part)).astype(bf16)
    attend(qkv_out, kmask[...], qmask[...], mixed_t, lse_out)
    mixed = mixed_t[...].T
    mix_out[...] = mixed
    after[...] = (embedded + dot(mixed, block_of(weights, 3))).astype(bf16)
    count = len(after_out)
    for step in range(count):
        after_out[step][...] = after[piece_at(place, step, count, ROWS // count), :]


def grad_into_norm(gqkv, weights):
    total = None
    for part in range(3):
        piece = dot(gqkv[:, part * 1024 : (part + 1) * 1024], block_of(weights, part), NT)
        total = piece if total is None else total + piece
    return total


def space_backward(count, *refs):
    grads, refs = refs[:count], refs[count:]
    (
        place, tok, hot, kmask, qmask, gain, table, weights, qkv, mix, lse,
        gqkv_out, gas_out, tok_out, gain_out, bias_out, table_out, grad_t, mixed_t, query_t, grad_rows,
    ) = refs
    first = pl.program_id(0) == 0
    for step in range(count):
        gas_out[piece_at(place, step, count, ROWS // count), :] = grads[step][...]
    upstream = gas_out[...]
    mixed_t[...] = mix[...].T
    grad_rows[...] = dot(upstream, block_of(weights, 3), NT).astype(bf16)
    grad_t[...] = grad_rows[...].T
    attend_back(qkv, kmask[...], qmask[...], lse, grad_rows, grad_t, mixed_t, gqkv_out, query_t)
    grad_norm = grad_into_norm(gqkv_out, weights)
    embedded = tok[...].astype(f32) + dot(hot[...], table[...])
    hat, rate = standardize(embedded)
    add_row(gain_out, column_sum(grad_norm * hat), first)
    add_row(bias_out, column_sum(grad_norm), first)
    total = upstream.astype(f32) + norm_back(hat, rate, gain[0:1, :], grad_norm)
    tok_out[...] = total
    add_row(table_out, dot(hot[...], total.astype(bf16), TN), first)


def time_forward(count, *refs):
    x, refs = refs[:count], refs[count:]
    kmask, qmask, gain, bias, weights, norm_out, qkv_out, mix_out, lse_out, after_out, mixed_t = refs
    after_space = stacked(x).astype(f32)
    hat, _ = standardize(after_space)
    normed = (hat * gain[1:2, :] + bias[1:2, :]).astype(bf16)
    norm_out[...] = normed
    for part in range(3):
        qkv_out[:, part * 1024 : (part + 1) * 1024] = dot(normed, block_of(weights, part)).astype(bf16)
    attend(qkv_out, kmask[...], qmask[...], mixed_t, lse_out)
    mixed = mixed_t[...].T
    mix_out[...] = mixed
    after_out[...] = after_space + dot(mixed, block_of(weights, 3))


def feed_forward(count, *refs):
    grad, refs = refs[:count], refs[count:]
    x, gain, bias, hidden_bias, out_bias, weights = refs[:6]
    norm_out, act_out, gpre_out, gat_out, branch_out, gain_out, bias_out, hb_out, ob_out = refs[6:15]
    block_out = refs[15:]
    first = pl.program_id(0) == 0
    clips = weights.shape[0]
    own = 1024 // clips
    groups = x.shape[0]
    width = x.shape[2]
    size = FF_CHUNK
    chunks = 4096 // size
    half = 1024 // size
    share = size * clips // 4096
    branch = stacked(grad, groups)
    branch_out[...] = branch.reshape(branch_out.shape)

    def down_of(chunk):
        if share:
            return weights[chunk * share : (chunk + 1) * share, 4 * own :, :].reshape(size, 1024)
        return None

    def hidden_of(chunk):
        block, column = chunk // half, chunk % half
        return weights[:, block * own : (block + 1) * own, column * size : (column + 1) * size].reshape(1024, size)

    part_at = lambda chunk: slice(chunk * size, (chunk + 1) * size)
    back_act = dot(branch, down_of(0), NT)
    after_time = x[...].reshape(groups * ROWS, width)
    hat, rate = standardize(after_time)
    normed = (hat * gain[2:3, :] + bias[2:3, :]).astype(bf16)
    norm_out[...] = normed.reshape(norm_out.shape)
    pre = dot(normed, hidden_of(0)) + hidden_bias[0:1, part_at(0)]
    result = None
    grad_norm = None
    bias_sums = []
    for chunk in range(chunks):
        at = part_at(chunk)
        u, grad_act = pre, back_act
        if chunk + 1 < chunks:
            pre = dot(normed, hidden_of(chunk + 1)) + hidden_bias[0:1, part_at(chunk + 1)]
            back_act = dot(branch, down_of(chunk + 1), NT)
        c0 = 0.7978845608028654
        square = u * u
        t = jnp.tanh(u * (c0 + (c0 * 0.044715) * square))
        half_plus = 0.5 + 0.5 * t
        act = (u * half_plus).astype(bf16)
        act_out[:, :, at] = act.reshape(groups, ROWS, size)
        slope = half_plus + (0.5 * u) * (1.0 - t * t) * (c0 + (3.0 * c0 * 0.044715) * square)
        gpre = (grad_act * slope).astype(bf16)
        gpre_out[:, :, at] = gpre.reshape(groups, ROWS, size)
        bias_sums.append(column_sum(gpre.astype(f32)))
        down = dot(act, down_of(chunk))
        result = down if result is None else result + down
        back = dot(gpre, hidden_of(chunk), NT)
        grad_norm = back if grad_norm is None else grad_norm + back
    block = (after_time + result + out_bias[0:1, :]).astype(bf16)
    unstack(block_out, block, groups)
    upstream = branch.astype(f32)
    gat = (upstream + norm_back(hat, rate, gain[2:3, :], grad_norm)).astype(bf16)
    gat_out[...] = gat.reshape(gat_out.shape)
    add_row(gain_out, column_sum(grad_norm * hat), first)
    add_row(bias_out, column_sum(grad_norm), first)
    add_row(ob_out, column_sum(upstream), first)
    add_row(hb_out, jnp.concatenate(bias_sums, axis=1), first)


def time_backward(count, *refs):
    x, refs = refs[:count], refs[count:]
    gat, kmask, qmask, gain, weights, qkv, mix, lse, gqkv_out, gain_out, bias_out = refs[:11]
    gas_out = refs[11 : 11 + count]
    grad_t, mixed_t, query_t, grad_rows = refs[11 + count :]
    first = pl.program_id(0) == 0
    upstream = gat[...]
    mixed_t[...] = mix[...].T
    grad_rows[...] = dot(upstream, block_of(weights, 3), NT).astype(bf16)
    grad_t[...] = grad_rows[...].T
    attend_back(qkv, kmask[...], qmask[...], lse, grad_rows, grad_t, mixed_t, gqkv_out, query_t)
    grad_norm = grad_into_norm(gqkv_out, weights)
    hat, rate = standardize(stacked(x).astype(f32))
    add_row(gain_out, column_sum(grad_norm * hat), first)
    add_row(bias_out, column_sum(grad_norm), first)
    total = upstream.astype(f32) + norm_back(hat, rate, gain[1:2, :], grad_norm)
    unstack(gas_out, total.astype(bf16))


def assemble(count, *refs):
    place, parts, out = refs[0], refs[1:-1], refs[-1]
    for micro in range(out.shape[0]):
        for step in range(count):
            out[micro, piece_at(place, step, count, ROWS // count), :] = parts[micro * count + step][...]


def rows_of(ref):
    value = ref[...]
    return value.reshape(-1, value.shape[-1])


def weight_kernel(pairs, micros, own, by_rows, has_small, *refs):
    out = refs[-1]
    offset = 0
    for pair in range(pairs):
        base = pair * 2 * micros
        total = None
        for index in range(micros):
            piece = dot(rows_of(refs[base + index]), rows_of(refs[base + micros + index]), TN)
            total = piece if total is None else total + piece
        total = total.astype(bf16)
        if by_rows:
            out[...] = total.reshape(out.shape)
            continue
        for block in range(total.shape[1] // 1024):
            for shard in range(out.shape[0]):
                out[shard, offset : offset + own, :] = total[
                    shard * own : (shard + 1) * own, block * 1024 : (block + 1) * 1024
                ]
            offset += own
    if has_small:
        out[:, offset:, :] = refs[pairs * 2 * micros][...]


def params():
    return pltpu.CompilerParams(vmem_limit_bytes=VMEM_LIMIT)


def ordered_call(kernel, behind, in_specs, **options):
    count = len(behind)

    def body(*refs):
        kernel(*refs[count:])

    aliases = options.pop("input_output_aliases", {})
    call = pl.pallas_call(
        body,
        in_specs=[pl.BlockSpec(memory_space=pl.ANY)] * count + in_specs,
        input_output_aliases={count + k: v for k, v in aliases.items()},
        compiler_params=params(),
        **options,
    )
    return lambda *operands: call(*behind, *operands)


def whole(shape):
    rank = len(shape)
    return pl.BlockSpec(shape, lambda i: (0,) * rank, pipeline_mode=pl.Buffered(1))


def total_spec(shape):
    rank = len(shape)
    return pl.BlockSpec(shape, lambda i: (0,) * rank)


def step_spec(shape):
    rank = len(shape)
    return pl.BlockSpec((None,) + shape, lambda i: (i,) + (0,) * rank)


def micro_spec(micro, shape):
    rank = len(shape)
    return pl.BlockSpec((None, None) + shape, lambda i: (micro, i) + (0,) * rank)


def shape_of(shape, kind):
    return jax.ShapeDtypeStruct(shape, kind)


def smem():
    return pl.BlockSpec(memory_space=pltpu.SMEM)


def call_space_forward(behind, micro, place, tok, hot, kmask, qmask, gain, bias, table, weights, count):
    _, frames, slots, width = tok.shape
    per = slots // count
    return ordered_call(
        space_forward,
        behind,
        grid=(frames,),
        in_specs=[smem(), micro_spec(micro, (slots, width)), step_spec(hot.shape[1:])]
        + [whole(a.shape) for a in (kmask, qmask, gain, bias, table, weights)],
        out_specs=[
            step_spec((slots, width)), step_spec((slots, 3 * width)), step_spec((slots, width)),
            step_spec((HEADS, slots)),
        ]
        + [step_spec((per, width))] * count,
        out_shape=[
            shape_of((frames, slots, width), bf16), shape_of((frames, slots, 3 * width), bf16),
            shape_of((frames, slots, width), bf16), shape_of((frames, HEADS, slots), f32),
        ]
        + [shape_of((frames, per, width), bf16)] * count,
        scratch_shapes=[pltpu.VMEM((width, ROWS), bf16), pltpu.VMEM((ROWS, width), bf16)],
        name="space_forward",
    )(place, tok, hot, kmask, qmask, gain, bias, table, weights)


def back_scratch(width):
    return [
        pltpu.VMEM((width, ROWS), bf16), pltpu.VMEM((width, ROWS), bf16),
        pltpu.VMEM((width, ROWS), bf16), pltpu.VMEM((ROWS, width), bf16),
    ]


def call_space_backward(
    behind, micro, grads, place, tok, hot, kmask, qmask, gain, table, weights, qkv, mix, lse, buffer
):
    micros, frames, slots, width = tok.shape
    count = len(grads)
    row = shape_of((1, width), f32)
    operands = list(grads) + [place, tok, hot, kmask, qmask, gain, table, weights, qkv, mix, lse]
    specs = (
        [step_spec((slots // count, width))] * count
        + [smem(), micro_spec(micro, (slots, width)), step_spec(hot.shape[1:])]
        + [whole(a.shape) for a in (kmask, qmask, gain, table, weights)]
        + [step_spec((slots, 3 * width)), step_spec((slots, width)), step_spec((HEADS, slots))]
    )
    before = len(operands)
    kernel = functools.partial(space_backward, count)
    aliases = {}
    if buffer is not None:
        aliases = {before: 2}
        operands.append(buffer)
        specs.append(pl.BlockSpec(memory_space=pl.ANY))
        kernel = lambda *refs: space_backward(count, *refs[:before], *refs[before + 1 :])
    return ordered_call(
        kernel,
        behind,
        grid=(frames,),
        in_specs=specs,
        out_specs=[
            step_spec((slots, 3 * width)), step_spec((slots, width)), micro_spec(micro, (slots, width)),
            total_spec((1, width)), total_spec((1, width)), total_spec((hot.shape[2], width)),
        ],
        out_shape=[
            shape_of((frames, slots, 3 * width), bf16), shape_of((frames, slots, width), bf16),
            shape_of((micros, frames, slots, width), f32), row, row, shape_of((hot.shape[2], width), f32),
        ],
        scratch_shapes=back_scratch(width),
        input_output_aliases=aliases,
        name="space_backward",
    )(*operands)


def group_spec(array, count):
    frames, _, width = array.shape
    return pl.BlockSpec((frames, ROWS // (frames * count), width), lambda i: (0, i, 0))


def call_time_forward(behind, x, kmask, qmask, gain, bias, weights):
    count = len(x)
    frames, slots, width = x[0].shape
    groups = slots * frames * count // ROWS
    return ordered_call(
        functools.partial(time_forward, count),
        behind,
        grid=(groups,),
        in_specs=[group_spec(a, count) for a in x] + [whole(a.shape) for a in (kmask, qmask, gain, bias, weights)],
        out_specs=[
            step_spec((ROWS, width)), step_spec((ROWS, 3 * width)), step_spec((ROWS, width)),
            step_spec((HEADS, ROWS)), step_spec((ROWS, width)),
        ],
        out_shape=[
            shape_of((groups, ROWS, width), bf16), shape_of((groups, ROWS, 3 * width), bf16),
            shape_of((groups, ROWS, width), bf16), shape_of((groups, HEADS, ROWS), f32),
            shape_of((groups, ROWS, width), f32),
        ],
        scratch_shapes=[pltpu.VMEM((width, ROWS), bf16)],
        name="time_forward",
    )(*x, kmask, qmask, gain, bias, weights)


def call_feed_forward(behind, grad, x, gain, bias, hidden_bias, out_bias, weights):
    count = len(grad)
    groups, _, width = x.shape
    ff = hidden_bias.shape[1]
    each = FF_GROUPS if groups % FF_GROUPS == 0 else 1
    row = shape_of((1, width), f32)
    rows = lambda cols: shape_of((groups, ROWS, cols), bf16)
    spec = lambda cols: pl.BlockSpec((each, ROWS, cols), lambda i: (i, 0, 0))
    grad_spec = lambda a: pl.BlockSpec(
        (a.shape[0], each * ROWS // (a.shape[0] * count), width), lambda i: (0, i, 0)
    )
    return ordered_call(
        functools.partial(feed_forward, count),
        behind,
        grid=(groups // each,),
        in_specs=[grad_spec(a) for a in grad]
        + [spec(width)]
        + [whole(a.shape) for a in (gain, bias, hidden_bias, out_bias, weights)],
        out_specs=[
            spec(width), spec(ff), spec(ff), spec(width), spec(width),
            total_spec((1, width)), total_spec((1, width)), total_spec((1, ff)), total_spec((1, width)),
        ]
        + [grad_spec(a) for a in grad],
        out_shape=[rows(width), rows(ff), rows(ff), rows(width), rows(width), row, row, shape_of((1, ff), f32), row]
        + [shape_of(a.shape, bf16) for a in grad],
        name="feed_forward",
    )(*grad, x, gain, bias, hidden_bias, out_bias, weights)


def call_time_backward(behind, x, gat, kmask, qmask, gain, weights, qkv, mix, lse):
    count = len(x)
    groups, _, width = gat.shape
    row = shape_of((1, width), f32)
    return ordered_call(
        functools.partial(time_backward, count),
        behind,
        grid=(groups,),
        in_specs=[group_spec(a, count) for a in x]
        + [step_spec((ROWS, width))]
        + [whole(a.shape) for a in (kmask, qmask, gain, weights)]
        + [step_spec((ROWS, 3 * width)), step_spec((ROWS, width)), step_spec((HEADS, ROWS))],
        out_specs=[step_spec((ROWS, 3 * width)), total_spec((1, width)), total_spec((1, width))]
        + [group_spec(a, count) for a in x],
        out_shape=[shape_of((groups, ROWS, 3 * width), bf16), row, row] + [shape_of(a.shape, bf16) for a in x],
        scratch_shapes=back_scratch(width),
        name="time_backward",
    )(*x, gat, kmask, qmask, gain, weights, qkv, mix, lse)


def call_assemble(place, parts):
    micros, count = len(parts), len(parts[0])
    frames, per, width = parts[0][0].shape
    flat = [p for pieces in parts for p in pieces]
    return ordered_call(
        functools.partial(assemble, count),
        [],
        grid=(frames,),
        in_specs=[smem()] + [step_spec((per, width))] * len(flat),
        out_specs=pl.BlockSpec((micros, None, per * count, width), lambda i: (0, i, 0, 0)),
        out_shape=shape_of((micros, frames, per * count, width), bf16),
        name="assemble",
    )(place, *flat)


def weight_grad(behind, pairs, clips, rows, name, small=None, down_at=None):
    own = 1024 // clips
    block = 256 if down_at is None else 512
    width = pairs[0][0][0].shape[-1]
    by_rows = down_at is not None

    def left_spec(a):
        rank = a.ndim
        return pl.BlockSpec(a.shape[:-1] + (block,), lambda i: (0,) * (rank - 1) + (i,))

    operands, specs = [], []
    cols = 0
    for lefts, rights in pairs:
        operands += list(lefts) + list(rights)
        specs += [left_spec(a) for a in lefts] + [whole(a.shape) for a in rights]
        cols += rights[0].shape[-1]
    shards = block // own
    if small is not None:
        operands.append(small)
        specs.append(pl.BlockSpec((shards,) + small.shape[1:], lambda i: (i, 0, 0)))
    if by_rows:
        per = width // clips
        out_spec = pl.BlockSpec((block // per, per, 1024), lambda i: (i, down_at // per, 0))
    else:
        out_rows = cols // 1024 * own + (0 if small is None else small.shape[1])
        out_spec = pl.BlockSpec((shards, out_rows, 1024), lambda i: (i, 0, 0))
    return ordered_call(
        functools.partial(weight_kernel, len(pairs), len(pairs[0][0]), own, by_rows, small is not None),
        behind,
        grid=(width // block,),
        in_specs=specs,
        out_specs=out_spec,
        out_shape=shape_of((clips, rows, 1024), bf16),
        name=name,
    )(*operands)


def column_kernel(starts, micros, *refs):
    out = refs[-1]
    step = pl.program_id(0)
    for pair, (start, end) in enumerate(starts):
        lefts = refs[pair * 2 * micros : pair * 2 * micros + micros]
        rights = refs[pair * 2 * micros + micros : (pair + 1) * 2 * micros]

        def fill():
            total = None
            for left, right in zip(lefts, rights):
                piece = dot(rows_of(left), rows_of(right), TN)
                total = piece if total is None else total + piece
            out[...] = total.astype(bf16).reshape(out.shape)

        if len(starts) == 1:
            fill()
        else:
            pl.when(jnp.logical_and(step >= start, step < end))(fill)


def weight_columns(behind, pairs, clips, rows, name, buffer=None):
    own = 1024 // clips
    block = 512
    operands, specs, starts = [], [], []
    step = 0
    for lefts, rights in pairs:
        count = rights[0].shape[-1] // block

        def right_spec(a, start=step, last=count - 1):
            rank = a.ndim
            return pl.BlockSpec(
                a.shape[:-1] + (block,), lambda i: (0,) * (rank - 1) + (jnp.clip(i - start, 0, last),)
            )

        operands += list(lefts) + list(rights)
        specs += [whole(a.shape) for a in lefts] + [right_spec(a) for a in rights]
        starts.append((step, step + count))
        step += count
    kernel = functools.partial(column_kernel, starts, len(pairs[0][0]))
    aliases = {}
    if buffer is not None:
        before = len(operands)
        aliases = {before: 0}
        operands.append(buffer)
        specs.append(pl.BlockSpec(memory_space=pl.ANY))
        inner = kernel
        kernel = lambda *refs: inner(*refs[:before], *refs[before + 1 :])
    return ordered_call(
        kernel,
        behind,
        grid=(step,),
        in_specs=specs,
        out_specs=pl.BlockSpec((clips, own, block), lambda i: (0, i // 2, i % 2)),
        out_shape=shape_of((clips, rows, 1024), bf16),
        input_output_aliases=aliases,
        name=name,
    )(*operands)


def one_hot(index, count, kind=bf16):
    return (index[..., None] == jnp.arange(count)).astype(kind)


def space_masks(labels):
    keys = one_hot(labels, 128)
    queries = jnp.where(labels[None, :] == jnp.arange(128)[:, None], 0.0, MASKED)
    queries = jnp.where(jnp.arange(128)[:, None] < 8, queries, 0.0).astype(bf16)
    return keys, queries


def time_masks(frames, count, me):
    per = ROWS // frames
    row = jnp.arange(ROWS)
    held = frames // count
    frame = jnp.mod(me - row // (held * per), count) * held + row // per % held
    place = row % per
    lane = jnp.arange(128)
    keys = ((lane[None, :] == place[:, None]) | (lane[None, :] == per + frame[:, None])).astype(bf16)
    other = (lane[:, None] < per) & (lane[:, None] != place[None, :])
    later = (lane[:, None] >= per) & (lane[:, None] < per + frames) & (lane[:, None] - per > frame[None, :])
    queries = jnp.where(other | later, MASKED, 0.0).astype(bf16)
    return keys, queries


def action_rows(labels, owners, actions):
    clip_of = jnp.sum(jnp.where(labels[:, None] == jnp.arange(owners.shape[0]), owners[None, :], 0), axis=1)
    hit = clip_of[:, None] == jnp.arange(actions.shape[0])
    chosen = jnp.sum(jnp.where(hit[:, :, None], actions[None], 0), axis=1)
    return jnp.transpose(chosen)


def exchange(values):
    return lax.all_to_all(values, "tm", 0, 0, tiled=True)


def gather(shards):
    own = shards[0].shape[0]
    parts = []
    for shard in shards:
        rows, cols = shard.shape
        parts += [shard[:, at : at + 1024] for at in range(0, cols, 1024)]
    return lax.all_gather(jnp.concatenate(parts, axis=0), "clip", axis=0, tiled=False)


def reduce_clip(total):
    return lax.psum_scatter(total, "clip", scatter_dimension=0, tiled=False)


def shift(values, step):
    count = lax.axis_size("tm")
    return lax.ppermute(values, "tm", [(k, (k + step) % count) for k in range(count)])


def sum_half(part):
    count = lax.axis_size("tm")
    rows = part.shape[0] // count
    me = lax.axis_index("tm")
    piece = lambda step: lax.dynamic_slice_in_dim(part, lax.rem(me + step, count) * rows, rows, axis=0)
    total = piece(0).astype(f32)
    for received in [shift(piece(step), step) for step in range(1, count)]:
        total = total + received.astype(f32)
    return total.astype(bf16)


def share_half(mine):
    count = lax.axis_size("tm")
    rows = mine.shape[0]
    me = lax.axis_index("tm")
    whole_rows = jnp.zeros((count * rows, mine.shape[1]), mine.dtype)
    for step, held in enumerate([mine] + [shift(mine, step) for step in range(1, count)]):
        at = lax.rem(me + count - step, count) * rows
        whole_rows = lax.dynamic_update_slice_in_dim(whole_rows, held, at, axis=0)
    return whole_rows


def mark(values):
    return values.reshape(-1, values.shape[-1])[:8, :128]


def together(*lists):
    flat = lax.optimization_barrier([a for arrays in lists for a in arrays])
    out = []
    for arrays in lists:
        out.append(list(flat[: len(arrays)]))
        flat = flat[len(arrays) :]
    return out


def columns(rows, own, first, count):
    return jnp.concatenate([rows[(first + c) * own : (first + c + 1) * own] for c in range(count)], axis=1).astype(f32)


def local(
    tokens, segments, assignment, actions, norm_gain, norm_bias,
    space_in, space_out, time_in, time_out, hidden, hidden_bias, down, out_bias,
    action_table, out_grad,
):
    micros, frames_here, slots, width = tokens.shape
    pieces = lax.axis_size("tm")
    clips = lax.axis_size("clip")
    frames = frames_here * pieces
    per = slots // pieces
    own = norm_gain.shape[1]
    nact = action_table.shape[0]
    micro = range(micros)
    hb_rows = hidden_bias.shape[0] // own
    small_rows = 6 + nact + hb_rows + 1

    small = jnp.concatenate(
        [norm_gain, norm_bias, action_table, hidden_bias.reshape(-1, own), out_bias.reshape(-1, own)], axis=0
    )
    small_all = lax.all_gather(small, "clip", axis=0, tiled=False)
    w_space = gather([space_in, space_out])
    w_time = gather([time_in, time_out])
    w_ff = gather([hidden, down])

    rows_by = lambda start, count: jnp.transpose(small_all[:, start : start + count], (1, 0, 2)).reshape(count, width)
    gain = rows_by(0, 3).astype(f32)
    bias = rows_by(3, 3).astype(f32)
    table = jnp.pad(rows_by(6, nact), ((0, 128 - nact), (0, 0)))
    hb_all = small_all[:, 6 + nact : 6 + nact + hb_rows].reshape(1, -1).astype(f32)
    ob_all = small_all[:, 6 + nact + hb_rows :].reshape(1, -1).astype(f32)

    me = lax.axis_index("tm").astype(jnp.int32)
    place = me.reshape(1)
    tmasks = time_masks(frames, pieces, me)
    hots = [one_hot(action_rows(segments[m], assignment[m], actions[m]), 128) for m in micro]
    smasks = [space_masks(segments[m]) for m in micro]

    pick = lambda parts, index: [parts[m][index] for m in micro]
    outward = lambda parts: [parts[0]] + [
        lax.ppermute(parts[d], "tm", [(k, (k + d) % pieces) for k in range(pieces)]) for d in range(1, pieces)
    ]
    inward = lambda parts: [parts[0]] + [
        lax.ppermute(parts[d], "tm", [(k, (k - d) % pieces) for k in range(pieces)]) for d in range(1, pieces)
    ]
    marks = lambda parts: [mark(a) for a in parts[1:]]
    rounded = lambda values, d: lax.dynamic_slice_in_dim(values, (me + d) % pieces * per, per, axis=1).astype(bf16)
    sent = [[rounded(out_grad[m], d) for d in range(pieces)] for m in micro]

    branch = [outward(sent[0])]
    forward, after, middle, ahead, pieces_out, back, gas, last = [], [], [], [], [], [], [], []
    behind = []
    for m in micro:
        forward.append(
            call_space_forward(behind, m, place, tokens, hots[m], *smasks[m], gain, bias, table, w_space, pieces)
        )
        after.append(outward(forward[m][4:]))
        behind = [forward[m][3]] + marks(branch[0])
    for m in micro:
        middle.append(list(call_time_forward(behind, after[m], *tmasks, gain, bias, w_time)))
        behind = [middle[m][3]]
    for m in micro[1:]:
        late, (middle[-1][4],) = together(sent[m], [middle[-1][4]])
        branch.append(outward(late))
    for m in micro:
        ahead.append(call_feed_forward(behind, branch[m], middle[m][4], gain, bias, hb_all, ob_all, w_ff))
        pieces_out.append(inward(ahead[m][9:]))
        behind = [ahead[m][5]]
    behind += marks(pieces_out[0])
    ff_grad = weight_grad(behind, [(pick(ahead, 1), pick(ahead, 4))], clips, 8 * own, "down_grad", down_at=4 * own)
    ff_grad = weight_columns([], [(pick(ahead, 0), pick(ahead, 2))], clips, 8 * own, "hidden_grad", buffer=ff_grad)
    (ff_grad,), pieces_out[-1] = together([ff_grad], pieces_out[-1])
    ff_part = reduce_clip(ff_grad)
    behind = [ff_grad]
    for m in micro:
        back.append(
            call_time_backward(
                behind, after[m], ahead[m][3], *tmasks, gain, w_time, middle[m][1], middle[m][2], middle[m][3]
            )
        )
        gas.append(inward(back[m][3:]))
        behind = [back[m][1]]
    time_grad = weight_columns(
        behind, [(pick(middle, 0), pick(back, 0)), (pick(middle, 2), pick(ahead, 3))], clips, 4 * own, "time_grad"
    )
    (time_grad,), gas[0] = together([time_grad], gas[0])
    time_part = reduce_clip(time_grad)
    behind = [time_grad]
    grad_buffer = None
    for m in micro:
        last.append(
            list(
                call_space_backward(
                    behind, m, gas[m], place, tokens, hots[m], *smasks[m], gain, table, w_space,
                    forward[m][1], forward[m][2], forward[m][3], grad_buffer,
                )
            )
        )
        grad_buffer = last[m][2]
        behind = []
        if m == 0:
            (ff_part,), (last[m][3],) = together([ff_part], [last[m][3]])
            ff_half = sum_half(ff_part)
            behind = [mark(ff_part)]

    total = lambda values: functools.reduce(jnp.add, values)
    gain_grad = jnp.concatenate([total(pick(last, 3)), total(pick(back, 1)), total(pick(ahead, 5))])
    bias_grad = jnp.concatenate([total(pick(last, 4)), total(pick(back, 2)), total(pick(ahead, 6))])
    table_grad = total(pick(last, 5))[:nact]
    hb_grad = total(pick(ahead, 7))
    ob_grad = total(pick(ahead, 8))
    split = lambda a: jnp.transpose(a.reshape(a.shape[0], clips, own), (1, 0, 2))
    small_grads = jnp.concatenate(
        [
            split(gain_grad), split(bias_grad), split(table_grad),
            hb_grad.reshape(clips, hb_rows, own), ob_grad.reshape(clips, 1, own),
        ],
        axis=1,
    ).astype(bf16).reshape(clips, -1)
    extra = 8 * pieces - 4 * own % (8 * pieces)
    small_grads = jnp.pad(small_grads, ((0, 0), (0, extra * 1024 - small_grads.shape[1]))).reshape(clips, extra, 1024)
    space_grad = weight_grad(
        [mark(ff_half)], [(pick(forward, 0), pick(last, 0)), (pick(forward, 2), pick(last, 1))],
        clips, 4 * own + extra, "space_grad", small=small_grads,
    )

    ff_sum = lax.psum(ff_part, "tm")
    (ff_half,), (space_grad,) = together([ff_half], [space_grad])
    space_part = reduce_clip(space_grad)
    ff_sum = share_half(ff_half)
    (time_part,), (ff_half,) = together([time_part], [ff_half])
    time_sum = share_half(sum_half(time_part))
    early = (
        call_assemble(place, pieces_out),
        columns(time_sum, own, 0, 3),
        columns(time_sum, own, 3, 1),
        columns(ff_sum, own, 0, 4),
        ff_sum[4 * own :].astype(f32),
    )
    space_part, *early = lax.optimization_barrier((space_part,) + early)
    space_sum = share_half(sum_half(space_part))
    mine = space_sum[4 * own :].reshape(-1)[: small_rows * own].reshape(small_rows, own).astype(f32)
    return (
        early[0],
        grad_buffer,
        mine[0:3],
        mine[3:6],
        columns(space_sum, own, 0, 3),
        columns(space_sum, own, 3, 1),
        early[1],
        early[2],
        early[3],
        mine[6 + nact : 6 + nact + hb_rows].reshape(-1),
        early[4],
        mine[6 + nact + hb_rows :].reshape(-1),
        mine[6 : 6 + nact],
    )


def solution(mesh):
    rows = P("clip", None)
    cols = P(None, "clip")
    line = P("clip")
    wide = P(None, "tm", "clip", None)
    return jax.shard_map(
        local,
        mesh=mesh,
        in_specs=(
            wide, cols, cols, P(None, None, "tm"), cols, cols,
            rows, rows, rows, rows, rows, line, rows, line, cols, wide,
        ),
        out_specs=(wide, wide, cols, cols, rows, rows, rows, rows, rows, line, rows, line, cols),
        check_vma=False,
    )
```

```python
import functools

import jax
import jax.numpy as jnp
from jax import lax
from jax.experimental import pallas as pl
from jax.experimental.pallas import tpu as pltpu
from jax.sharding import PartitionSpec as P

HEADS = 16
HEAD = 64
EPS = 1e-05
MASKED = -1e30
ROWS = 256
FF_CHUNK = 1024
FF_GROUPS = 1
VMEM_LIMIT = 62 * 1024 * 1024

bf16 = jnp.bfloat16
f32 = jnp.float32

NN = (((1,), (0,)), ((), ()))
NT = (((1,), (1,)), ((), ()))
TN = (((0,), (0,)), ((), ()))


def dot(left, right, form=NN):
    return lax.dot_general(left, right, form, preferred_element_type=f32)


def standardize(values):
    centered = values - jnp.mean(values, axis=-1, keepdims=True)
    rate = lax.rsqrt(jnp.mean(centered * centered, axis=-1, keepdims=True) + EPS)
    return centered * rate, rate


def norm_back(hat, rate, gain, grad):
    scaled = grad * gain
    return rate * (
        scaled
        - jnp.mean(scaled, axis=-1, keepdims=True)
        - hat * jnp.mean(scaled * hat, axis=-1, keepdims=True)
    )


def add_row(ref, row, first):
    @pl.when(first)
    def _():
        ref[...] = row

    @pl.when(jnp.logical_not(first))
    def _():
        ref[...] += row


def column_sum(values):
    return jnp.sum(values, axis=0, keepdims=True)


def pair_slices(pair):
    lane = pair * 128
    return slice(lane, lane + 128), slice(1024 + lane, 1024 + lane + 128), slice(2048 + lane, 2048 + lane + 128)


def attend(qkv_ref, key_mask, query_mask, mixed_t, lse_ref):
    blank = jnp.zeros((HEAD, ROWS), bf16)
    scale = jnp.asarray(HEAD**-0.5, bf16)

    def scores_of(pair):
        q_at, k_at, v_at = pair_slices(pair)
        q_t = (qkv_ref[:, q_at] * scale).T
        keys = jnp.concatenate([qkv_ref[:, k_at], key_mask], axis=1)
        first = jnp.concatenate([q_t[:HEAD], blank, query_mask], axis=0)
        second = jnp.concatenate([blank, q_t[HEAD:], query_mask], axis=0)
        return dot(keys, jnp.concatenate([first, second], axis=1))

    def finish(pair, scores):
        v_t = qkv_ref[:, pair_slices(pair)[2]].T
        top = jnp.max(scores, axis=0, keepdims=True)
        raised = jnp.exp(scores - top)
        total = jnp.sum(raised, axis=0, keepdims=True)
        weights = raised.astype(bf16)
        lse = top + jnp.log(total)
        rate = 1.0 / total
        for part in range(2):
            head = pair * 2 + part
            at = slice(part * ROWS, (part + 1) * ROWS)
            mixed = dot(v_t[part * HEAD : (part + 1) * HEAD], weights[:, at])
            mixed_t[head * HEAD : (head + 1) * HEAD, :] = (mixed * rate[:, at]).astype(bf16)
            lse_ref[head : head + 1, :] = lse[:, at]

    queue = [scores_of(0), scores_of(1)]
    for pair in range(HEADS // 2):
        if pair + 2 < HEADS // 2:
            queue.append(scores_of(pair + 2))
        finish(pair, queue.pop(0))


def attend_back(qkv_ref, key_mask, query_mask, lse_ref, grad_ref, grad_t, mixed_t, out_ref, query_t):
    blank = jnp.zeros((HEAD, ROWS), bf16)
    scale = jnp.asarray(HEAD**-0.5, bf16)
    low_half = lax.broadcasted_iota(jnp.int32, (ROWS, 128), 1) < HEAD
    zero = jnp.zeros((ROWS, 128), bf16)

    def both(top, bottom, extra):
        first = jnp.concatenate([top, blank] + extra, axis=0)
        second = jnp.concatenate([blank, bottom] + extra, axis=0)
        return jnp.concatenate([first, second], axis=1)

    def halves(values):
        return jnp.concatenate([jnp.where(low_half, values, zero), jnp.where(low_half, zero, values)], axis=0)

    def start(pair):
        q_at, k_at, v_at = pair_slices(pair)
        q_t = (qkv_ref[:, q_at] * scale).T
        keys = jnp.concatenate([qkv_ref[:, k_at], key_mask], axis=1)
        scores = dot(keys, both(q_t[:HEAD], q_t[HEAD:], [query_mask]))
        pair_t = grad_t[q_at, :]
        grad_probs = dot(qkv_ref[:, v_at], both(pair_t[:HEAD], pair_t[HEAD:], []))
        return scores, grad_probs

    def finish(pair, scores, grad_probs):
        q_at, k_at, v_at = pair_slices(pair)
        head = pair * 2
        lse = jnp.concatenate([lse_ref[head : head + 1, :], lse_ref[head + 1 : head + 2, :]], axis=1)
        product = grad_t[q_at, :].astype(f32) * mixed_t[q_at, :].astype(f32)
        along = jnp.concatenate([column_sum(product[:HEAD]), column_sum(product[HEAD:])], axis=1)
        probs = jnp.exp(scores - lse)
        grad_scores = (probs * (grad_probs - along)).astype(bf16)
        out_ref[:, v_at] = dot(probs.astype(bf16), halves(grad_ref[:, q_at])).astype(bf16)
        out_ref[:, k_at] = dot(grad_scores, halves(qkv_ref[:, q_at] * scale)).astype(bf16)
        k_t = (qkv_ref[:, k_at] * scale).T
        for part in range(2):
            at = slice((head + part) * HEAD, (head + part + 1) * HEAD)
            columns_at = slice(part * ROWS, (part + 1) * ROWS)
            query_t[at, :] = dot(k_t[part * HEAD : (part + 1) * HEAD], grad_scores[:, columns_at]).astype(bf16)

    ahead = start(0)
    for pair in range(HEADS // 2):
        held = ahead
        if pair + 1 < HEADS // 2:
            ahead = start(pair + 1)
        finish(pair, *held)
    for quarter in range(4):
        at = slice(quarter * 256, (quarter + 1) * 256)
        out_ref[:, at] = query_t[at, :].T


def block_of(weights, index):
    own = 1024 // weights.shape[0]
    return weights[:, index * own : (index + 1) * own, :].reshape(1024, 1024)


def piece_at(place, step, count, rows):
    return pl.ds(pl.multiple_of(lax.rem(place[0] + step, count) * rows, rows), rows)


def stacked(refs, groups=1):
    per = refs[0].shape[1] // groups
    width = refs[0].shape[-1]
    parts = [ref[:, g * per : (g + 1) * per, :].reshape(-1, width) for g in range(groups) for ref in refs]
    return parts[0] if len(parts) == 1 else jnp.concatenate(parts, axis=0)


def unstack(refs, values, groups=1):
    per = refs[0].shape[1] // groups
    rows = values.shape[0] // (len(refs) * groups)
    for g in range(groups):
        for index, ref in enumerate(refs):
            at = (g * len(refs) + index) * rows
            ref[:, g * per : (g + 1) * per, :] = values[at : at + rows].reshape(ref.shape[0], per, ref.shape[2])


def space_forward(
    place, tok, hot, kmask, qmask, gain, bias, table, weights,
    norm_out, qkv_out, mix_out, lse_out, *rest,
):
    after_out, (mixed_t, after) = rest[:-2], rest[-2:]
    embedded = tok[...].astype(f32) + dot(hot[...], table[...])
    hat, _ = standardize(embedded)
    normed = (hat * gain[0:1, :] + bias[0:1, :]).astype(bf16)
    norm_out[...] = normed
    for part in range(3):
        qkv_out[:, part * 1024 : (part + 1) * 1024] = dot(normed, block_of(weights, part)).astype(bf16)
    attend(qkv_out, kmask[...], qmask[...], mixed_t, lse_out)
    mixed = mixed_t[...].T
    mix_out[...] = mixed
    after[...] = (embedded + dot(mixed, block_of(weights, 3))).astype(bf16)
    count = len(after_out)
    for step in range(count):
        after_out[step][...] = after[piece_at(place, step, count, ROWS // count), :]


def grad_into_norm(gqkv, weights):
    total = None
    for part in range(3):
        piece = dot(gqkv[:, part * 1024 : (part + 1) * 1024], block_of(weights, part), NT)
        total = piece if total is None else total + piece
    return total


def space_backward(count, *refs):
    grads, refs = refs[:count], refs[count:]
    (
        place, tok, hot, kmask, qmask, gain, table, weights, qkv, mix, lse,
        gqkv_out, gas_out, tok_out, gain_out, bias_out, table_out, grad_t, mixed_t, query_t, grad_rows,
    ) = refs
    first = pl.program_id(0) == 0
    for step in range(count):
        gas_out[piece_at(place, step, count, ROWS // count), :] = grads[step][...]
    upstream = gas_out[...]
    mixed_t[...] = mix[...].T
    grad_rows[...] = dot(upstream, block_of(weights, 3), NT).astype(bf16)
    grad_t[...] = grad_rows[...].T
    attend_back(qkv, kmask[...], qmask[...], lse, grad_rows, grad_t, mixed_t, gqkv_out, query_t)
    grad_norm = grad_into_norm(gqkv_out, weights)
    embedded = tok[...].astype(f32) + dot(hot[...], table[...])
    hat, rate = standardize(embedded)
    add_row(gain_out, column_sum(grad_norm * hat), first)
    add_row(bias_out, column_sum(grad_norm), first)
    total = upstream.astype(f32) + norm_back(hat, rate, gain[0:1, :], grad_norm)
    tok_out[...] = total
    add_row(table_out, dot(hot[...], total.astype(bf16), TN), first)


def time_forward(count, *refs):
    x, refs = refs[:count], refs[count:]
    kmask, qmask, gain, bias, weights, norm_out, qkv_out, mix_out, lse_out, after_out, mixed_t = refs
    after_space = stacked(x).astype(f32)
    hat, _ = standardize(after_space)
    normed = (hat * gain[1:2, :] + bias[1:2, :]).astype(bf16)
    norm_out[...] = normed
    for part in range(3):
        qkv_out[:, part * 1024 : (part + 1) * 1024] = dot(normed, block_of(weights, part)).astype(bf16)
    attend(qkv_out, kmask[...], qmask[...], mixed_t, lse_out)
    mixed = mixed_t[...].T
    mix_out[...] = mixed
    after_out[...] = after_space + dot(mixed, block_of(weights, 3))


def feed_forward(count, *refs):
    grad, refs = refs[:count], refs[count:]
    x, gain, bias, hidden_bias, out_bias, weights = refs[:6]
    norm_out, act_out, gpre_out, gat_out, branch_out, gain_out, bias_out, hb_out, ob_out = refs[6:15]
    block_out = refs[15:]
    first = pl.program_id(0) == 0
    clips = weights.shape[0]
    own = 1024 // clips
    groups = x.shape[0]
    width = x.shape[2]
    size = FF_CHUNK
    chunks = 4096 // size
    half = 1024 // size
    share = size * clips // 4096
    branch = stacked(grad, groups)
    branch_out[...] = branch.reshape(branch_out.shape)

    def down_of(chunk):
        if share:
            return weights[chunk * share : (chunk + 1) * share, 4 * own :, :].reshape(size, 1024)
        return None

    def hidden_of(chunk):
        block, column = chunk // half, chunk % half
        return weights[:, block * own : (block + 1) * own, column * size : (column + 1) * size].reshape(1024, size)

    part_at = lambda chunk: slice(chunk * size, (chunk + 1) * size)
    back_act = dot(branch, down_of(0), NT)
    after_time = x[...].reshape(groups * ROWS, width)
    hat, rate = standardize(after_time)
    normed = (hat * gain[2:3, :] + bias[2:3, :]).astype(bf16)
    norm_out[...] = normed.reshape(norm_out.shape)
    pre = dot(normed, hidden_of(0)) + hidden_bias[0:1, part_at(0)]
    result = None
    grad_norm = None
    bias_sums = []
    for chunk in range(chunks):
        at = part_at(chunk)
        u, grad_act = pre, back_act
        if chunk + 1 < chunks:
            pre = dot(normed, hidden_of(chunk + 1)) + hidden_bias[0:1, part_at(chunk + 1)]
            back_act = dot(branch, down_of(chunk + 1), NT)
        c0 = 0.7978845608028654
        square = u * u
        t = jnp.tanh(u * (c0 + (c0 * 0.044715) * square))
        half_plus = 0.5 + 0.5 * t
        act = (u * half_plus).astype(bf16)
        act_out[:, :, at] = act.reshape(groups, ROWS, size)
        slope = half_plus + (0.5 * u) * (1.0 - t * t) * (c0 + (3.0 * c0 * 0.044715) * square)
        gpre = (grad_act * slope).astype(bf16)
        gpre_out[:, :, at] = gpre.reshape(groups, ROWS, size)
        bias_sums.append(column_sum(gpre.astype(f32)))
        down = dot(act, down_of(chunk))
        result = down if result is None else result + down
        back = dot(gpre, hidden_of(chunk), NT)
        grad_norm = back if grad_norm is None else grad_norm + back
    block = (after_time + result + out_bias[0:1, :]).astype(bf16)
    unstack(block_out, block, groups)
    upstream = branch.astype(f32)
    gat = (upstream + norm_back(hat, rate, gain[2:3, :], grad_norm)).astype(bf16)
    gat_out[...] = gat.reshape(gat_out.shape)
    add_row(gain_out, column_sum(grad_norm * hat), first)
    add_row(bias_out, column_sum(grad_norm), first)
    add_row(ob_out, column_sum(upstream), first)
    add_row(hb_out, jnp.concatenate(bias_sums, axis=1), first)


def time_backward(count, *refs):
    x, refs = refs[:count], refs[count:]
    gat, kmask, qmask, gain, weights, qkv, mix, lse, gqkv_out, gain_out, bias_out = refs[:11]
    gas_out = refs[11 : 11 + count]
    grad_t, mixed_t, query_t, grad_rows = refs[11 + count :]
    first = pl.program_id(0) == 0
    upstream = gat[...]
    mixed_t[...] = mix[...].T
    grad_rows[...] = dot(upstream, block_of(weights, 3), NT).astype(bf16)
    grad_t[...] = grad_rows[...].T
    attend_back(qkv, kmask[...], qmask[...], lse, grad_rows, grad_t, mixed_t, gqkv_out, query_t)
    grad_norm = grad_into_norm(gqkv_out, weights)
    hat, rate = standardize(stacked(x).astype(f32))
    add_row(gain_out, column_sum(grad_norm * hat), first)
    add_row(bias_out, column_sum(grad_norm), first)
    total = upstream.astype(f32) + norm_back(hat, rate, gain[1:2, :], grad_norm)
    unstack(gas_out, total.astype(bf16))


def assemble(count, *refs):
    place, parts, out = refs[0], refs[1:-1], refs[-1]
    for micro in range(out.shape[0]):
        for step in range(count):
            out[micro, piece_at(place, step, count, ROWS // count), :] = parts[micro * count + step][...]


def rows_of(ref):
    value = ref[...]
    return value.reshape(-1, value.shape[-1])


def weight_kernel(pairs, micros, own, by_rows, has_small, *refs):
    out = refs[-1]
    offset = 0
    for pair in range(pairs):
        base = pair * 2 * micros
        total = None
        for index in range(micros):
            piece = dot(rows_of(refs[base + index]), rows_of(refs[base + micros + index]), TN)
            total = piece if total is None else total + piece
        total = total.astype(bf16)
        if by_rows:
            out[...] = total.reshape(out.shape)
            continue
        for block in range(total.shape[1] // 1024):
            for shard in range(out.shape[0]):
                out[shard, offset : offset + own, :] = total[
                    shard * own : (shard + 1) * own, block * 1024 : (block + 1) * 1024
                ]
            offset += own
    if has_small:
        out[:, offset:, :] = refs[pairs * 2 * micros][...]


def params():
    return pltpu.CompilerParams(vmem_limit_bytes=VMEM_LIMIT)


def ordered_call(kernel, behind, in_specs, **options):
    count = len(behind)

    def body(*refs):
        kernel(*refs[count:])

    aliases = options.pop("input_output_aliases", {})
    call = pl.pallas_call(
        body,
        in_specs=[pl.BlockSpec(memory_space=pl.ANY)] * count + in_specs,
        input_output_aliases={count + k: v for k, v in aliases.items()},
        compiler_params=params(),
        **options,
    )
    return lambda *operands: call(*behind, *operands)


def whole(shape):
    rank = len(shape)
    return pl.BlockSpec(shape, lambda i: (0,) * rank, pipeline_mode=pl.Buffered(1))


def total_spec(shape):
    rank = len(shape)
    return pl.BlockSpec(shape, lambda i: (0,) * rank)


def step_spec(shape):
    rank = len(shape)
    return pl.BlockSpec((None,) + shape, lambda i: (i,) + (0,) * rank)


def micro_spec(micro, shape):
    rank = len(shape)
    return pl.BlockSpec((None, None) + shape, lambda i: (micro, i) + (0,) * rank)


def shape_of(shape, kind):
    return jax.ShapeDtypeStruct(shape, kind)


def smem():
    return pl.BlockSpec(memory_space=pltpu.SMEM)


def call_space_forward(behind, micro, place, tok, hot, kmask, qmask, gain, bias, table, weights, count):
    _, frames, slots, width = tok.shape
    per = slots // count
    return ordered_call(
        space_forward,
        behind,
        grid=(frames,),
        in_specs=[smem(), micro_spec(micro, (slots, width)), step_spec(hot.shape[1:])]
        + [whole(a.shape) for a in (kmask, qmask, gain, bias, table, weights)],
        out_specs=[
            step_spec((slots, width)), step_spec((slots, 3 * width)), step_spec((slots, width)),
            step_spec((HEADS, slots)),
        ]
        + [step_spec((per, width))] * count,
        out_shape=[
            shape_of((frames, slots, width), bf16), shape_of((frames, slots, 3 * width), bf16),
            shape_of((frames, slots, width), bf16), shape_of((frames, HEADS, slots), f32),
        ]
        + [shape_of((frames, per, width), bf16)] * count,
        scratch_shapes=[pltpu.VMEM((width, ROWS), bf16), pltpu.VMEM((ROWS, width), bf16)],
        name="space_forward",
    )(place, tok, hot, kmask, qmask, gain, bias, table, weights)


def back_scratch(width):
    return [
        pltpu.VMEM((width, ROWS), bf16), pltpu.VMEM((width, ROWS), bf16),
        pltpu.VMEM((width, ROWS), bf16), pltpu.VMEM((ROWS, width), bf16),
    ]


def call_space_backward(
    behind, micro, grads, place, tok, hot, kmask, qmask, gain, table, weights, qkv, mix, lse, buffer
):
    micros, frames, slots, width = tok.shape
    count = len(grads)
    row = shape_of((1, width), f32)
    operands = list(grads) + [place, tok, hot, kmask, qmask, gain, table, weights, qkv, mix, lse]
    specs = (
        [step_spec((slots // count, width))] * count
        + [smem(), micro_spec(micro, (slots, width)), step_spec(hot.shape[1:])]
        + [whole(a.shape) for a in (kmask, qmask, gain, table, weights)]
        + [step_spec((slots, 3 * width)), step_spec((slots, width)), step_spec((HEADS, slots))]
    )
    before = len(operands)
    kernel = functools.partial(space_backward, count)
    aliases = {}
    if buffer is not None:
        aliases = {before: 2}
        operands.append(buffer)
        specs.append(pl.BlockSpec(memory_space=pl.ANY))
        kernel = lambda *refs: space_backward(count, *refs[:before], *refs[before + 1 :])
    return ordered_call(
        kernel,
        behind,
        grid=(frames,),
        in_specs=specs,
        out_specs=[
            step_spec((slots, 3 * width)), step_spec((slots, width)), micro_spec(micro, (slots, width)),
            total_spec((1, width)), total_spec((1, width)), total_spec((hot.shape[2], width)),
        ],
        out_shape=[
            shape_of((frames, slots, 3 * width), bf16), shape_of((frames, slots, width), bf16),
            shape_of((micros, frames, slots, width), f32), row, row, shape_of((hot.shape[2], width), f32),
        ],
        scratch_shapes=back_scratch(width),
        input_output_aliases=aliases,
        name="space_backward",
    )(*operands)


def group_spec(array, count):
    frames, _, width = array.shape
    return pl.BlockSpec((frames, ROWS // (frames * count), width), lambda i: (0, i, 0))


def call_time_forward(behind, x, kmask, qmask, gain, bias, weights):
    count = len(x)
    frames, slots, width = x[0].shape
    groups = slots * frames * count // ROWS
    return ordered_call(
        functools.partial(time_forward, count),
        behind,
        grid=(groups,),
        in_specs=[group_spec(a, count) for a in x] + [whole(a.shape) for a in (kmask, qmask, gain, bias, weights)],
        out_specs=[
            step_spec((ROWS, width)), step_spec((ROWS, 3 * width)), step_spec((ROWS, width)),
            step_spec((HEADS, ROWS)), step_spec((ROWS, width)),
        ],
        out_shape=[
            shape_of((groups, ROWS, width), bf16), shape_of((groups, ROWS, 3 * width), bf16),
            shape_of((groups, ROWS, width), bf16), shape_of((groups, HEADS, ROWS), f32),
            shape_of((groups, ROWS, width), f32),
        ],
        scratch_shapes=[pltpu.VMEM((width, ROWS), bf16)],
        name="time_forward",
    )(*x, kmask, qmask, gain, bias, weights)


def call_feed_forward(behind, grad, x, gain, bias, hidden_bias, out_bias, weights):
    count = len(grad)
    groups, _, width = x.shape
    ff = hidden_bias.shape[1]
    each = FF_GROUPS if groups % FF_GROUPS == 0 else 1
    row = shape_of((1, width), f32)
    rows = lambda cols: shape_of((groups, ROWS, cols), bf16)
    spec = lambda cols: pl.BlockSpec((each, ROWS, cols), lambda i: (i, 0, 0))
    grad_spec = lambda a: pl.BlockSpec(
        (a.shape[0], each * ROWS // (a.shape[0] * count), width), lambda i: (0, i, 0)
    )
    return ordered_call(
        functools.partial(feed_forward, count),
        behind,
        grid=(groups // each,),
        in_specs=[grad_spec(a) for a in grad]
        + [spec(width)]
        + [whole(a.shape) for a in (gain, bias, hidden_bias, out_bias, weights)],
        out_specs=[
            spec(width), spec(ff), spec(ff), spec(width), spec(width),
            total_spec((1, width)), total_spec((1, width)), total_spec((1, ff)), total_spec((1, width)),
        ]
        + [grad_spec(a) for a in grad],
        out_shape=[rows(width), rows(ff), rows(ff), rows(width), rows(width), row, row, shape_of((1, ff), f32), row]
        + [shape_of(a.shape, bf16) for a in grad],
        name="feed_forward",
    )(*grad, x, gain, bias, hidden_bias, out_bias, weights)


def call_time_backward(behind, x, gat, kmask, qmask, gain, weights, qkv, mix, lse):
    count = len(x)
    groups, _, width = gat.shape
    row = shape_of((1, width), f32)
    return ordered_call(
        functools.partial(time_backward, count),
        behind,
        grid=(groups,),
        in_specs=[group_spec(a, count) for a in x]
        + [step_spec((ROWS, width))]
        + [whole(a.shape) for a in (kmask, qmask, gain, weights)]
        + [step_spec((ROWS, 3 * width)), step_spec((ROWS, width)), step_spec((HEADS, ROWS))],
        out_specs=[step_spec((ROWS, 3 * width)), total_spec((1, width)), total_spec((1, width))]
        + [group_spec(a, count) for a in x],
        out_shape=[shape_of((groups, ROWS, 3 * width), bf16), row, row] + [shape_of(a.shape, bf16) for a in x],
        scratch_shapes=back_scratch(width),
        name="time_backward",
    )(*x, gat, kmask, qmask, gain, weights, qkv, mix, lse)


def call_assemble(place, parts):
    micros, count = len(parts), len(parts[0])
    frames, per, width = parts[0][0].shape
    flat = [p for pieces in parts for p in pieces]
    return ordered_call(
        functools.partial(assemble, count),
        [],
        grid=(frames,),
        in_specs=[smem()] + [step_spec((per, width))] * len(flat),
        out_specs=pl.BlockSpec((micros, None, per * count, width), lambda i: (0, i, 0, 0)),
        out_shape=shape_of((micros, frames, per * count, width), bf16),
        name="assemble",
    )(place, *flat)


def weight_grad(behind, pairs, clips, rows, name, small=None, down_at=None):
    own = 1024 // clips
    block = 256 if down_at is None else 512
    width = pairs[0][0][0].shape[-1]
    by_rows = down_at is not None

    def left_spec(a):
        rank = a.ndim
        return pl.BlockSpec(a.shape[:-1] + (block,), lambda i: (0,) * (rank - 1) + (i,))

    operands, specs = [], []
    cols = 0
    for lefts, rights in pairs:
        operands += list(lefts) + list(rights)
        specs += [left_spec(a) for a in lefts] + [whole(a.shape) for a in rights]
        cols += rights[0].shape[-1]
    shards = block // own
    if small is not None:
        operands.append(small)
        specs.append(pl.BlockSpec((shards,) + small.shape[1:], lambda i: (i, 0, 0)))
    if by_rows:
        per = width // clips
        out_spec = pl.BlockSpec((block // per, per, 1024), lambda i: (i, down_at // per, 0))
    else:
        out_rows = cols // 1024 * own + (0 if small is None else small.shape[1])
        out_spec = pl.BlockSpec((shards, out_rows, 1024), lambda i: (i, 0, 0))
    return ordered_call(
        functools.partial(weight_kernel, len(pairs), len(pairs[0][0]), own, by_rows, small is not None),
        behind,
        grid=(width // block,),
        in_specs=specs,
        out_specs=out_spec,
        out_shape=shape_of((clips, rows, 1024), bf16),
        name=name,
    )(*operands)


def column_kernel(starts, micros, *refs):
    out = refs[-1]
    step = pl.program_id(0)
    for pair, (start, end) in enumerate(starts):
        lefts = refs[pair * 2 * micros : pair * 2 * micros + micros]
        rights = refs[pair * 2 * micros + micros : (pair + 1) * 2 * micros]

        def fill():
            total = None
            for left, right in zip(lefts, rights):
                piece = dot(rows_of(left), rows_of(right), TN)
                total = piece if total is None else total + piece
            out[...] = total.astype(bf16).reshape(out.shape)

        if len(starts) == 1:
            fill()
        else:
            pl.when(jnp.logical_and(step >= start, step < end))(fill)


def weight_columns(behind, pairs, clips, rows, name, buffer=None):
    own = 1024 // clips
    block = 512
    operands, specs, starts = [], [], []
    step = 0
    for lefts, rights in pairs:
        count = rights[0].shape[-1] // block

        def right_spec(a, start=step, last=count - 1):
            rank = a.ndim
            return pl.BlockSpec(
                a.shape[:-1] + (block,), lambda i: (0,) * (rank - 1) + (jnp.clip(i - start, 0, last),)
            )

        operands += list(lefts) + list(rights)
        specs += [whole(a.shape) for a in lefts] + [right_spec(a) for a in rights]
        starts.append((step, step + count))
        step += count
    kernel = functools.partial(column_kernel, starts, len(pairs[0][0]))
    aliases = {}
    if buffer is not None:
        before = len(operands)
        aliases = {before: 0}
        operands.append(buffer)
        specs.append(pl.BlockSpec(memory_space=pl.ANY))
        inner = kernel
        kernel = lambda *refs: inner(*refs[:before], *refs[before + 1 :])
    return ordered_call(
        kernel,
        behind,
        grid=(step,),
        in_specs=specs,
        out_specs=pl.BlockSpec((clips, own, block), lambda i: (0, i // 2, i % 2)),
        out_shape=shape_of((clips, rows, 1024), bf16),
        input_output_aliases=aliases,
        name=name,
    )(*operands)


def one_hot(index, count, kind=bf16):
    return (index[..., None] == jnp.arange(count)).astype(kind)


def space_masks(labels):
    keys = one_hot(labels, 128)
    queries = jnp.where(labels[None, :] == jnp.arange(128)[:, None], 0.0, MASKED)
    queries = jnp.where(jnp.arange(128)[:, None] < 8, queries, 0.0).astype(bf16)
    return keys, queries


def time_masks(frames, count, me):
    per = ROWS // frames
    row = jnp.arange(ROWS)
    held = frames // count
    frame = jnp.mod(me - row // (held * per), count) * held + row // per % held
    place = row % per
    lane = jnp.arange(128)
    keys = ((lane[None, :] == place[:, None]) | (lane[None, :] == per + frame[:, None])).astype(bf16)
    other = (lane[:, None] < per) & (lane[:, None] != place[None, :])
    later = (lane[:, None] >= per) & (lane[:, None] < per + frames) & (lane[:, None] - per > frame[None, :])
    queries = jnp.where(other | later, MASKED, 0.0).astype(bf16)
    return keys, queries


def action_rows(labels, owners, actions):
    clip_of = jnp.sum(jnp.where(labels[:, None] == jnp.arange(owners.shape[0]), owners[None, :], 0), axis=1)
    hit = clip_of[:, None] == jnp.arange(actions.shape[0])
    chosen = jnp.sum(jnp.where(hit[:, :, None], actions[None], 0), axis=1)
    return jnp.transpose(chosen)


def exchange(values):
    return lax.all_to_all(values, "tm", 0, 0, tiled=True)


def gather(shards):
    own = shards[0].shape[0]
    parts = []
    for shard in shards:
        rows, cols = shard.shape
        parts += [shard[:, at : at + 1024] for at in range(0, cols, 1024)]
    return lax.all_gather(jnp.concatenate(parts, axis=0), "clip", axis=0, tiled=False)


def reduce_clip(total):
    return lax.psum_scatter(total, "clip", scatter_dimension=0, tiled=False)


def shift(values, step):
    count = lax.axis_size("tm")
    return lax.ppermute(values, "tm", [(k, (k + step) % count) for k in range(count)])


def sum_half(part):
    count = lax.axis_size("tm")
    rows = part.shape[0] // count
    me = lax.axis_index("tm")
    piece = lambda step: lax.dynamic_slice_in_dim(part, lax.rem(me + step, count) * rows, rows, axis=0)
    total = piece(0).astype(f32)
    for received in [shift(piece(step), step) for step in range(1, count)]:
        total = total + received.astype(f32)
    return total.astype(bf16)


def share_half(mine):
    count = lax.axis_size("tm")
    rows = mine.shape[0]
    me = lax.axis_index("tm")
    whole_rows = jnp.zeros((count * rows, mine.shape[1]), mine.dtype)
    for step, held in enumerate([mine] + [shift(mine, step) for step in range(1, count)]):
        at = lax.rem(me + count - step, count) * rows
        whole_rows = lax.dynamic_update_slice_in_dim(whole_rows, held, at, axis=0)
    return whole_rows


def mark(values):
    return values.reshape(-1, values.shape[-1])[:8, :128]


def together(*lists):
    flat = lax.optimization_barrier([a for arrays in lists for a in arrays])
    out = []
    for arrays in lists:
        out.append(list(flat[: len(arrays)]))
        flat = flat[len(arrays) :]
    return out


def columns(rows, own, first, count):
    return jnp.concatenate([rows[(first + c) * own : (first + c + 1) * own] for c in range(count)], axis=1).astype(f32)


def local(
    tokens, segments, assignment, actions, norm_gain, norm_bias,
    space_in, space_out, time_in, time_out, hidden, hidden_bias, down, out_bias,
    action_table, out_grad,
):
    micros, frames_here, slots, width = tokens.shape
    pieces = lax.axis_size("tm")
    clips = lax.axis_size("clip")
    frames = frames_here * pieces
    per = slots // pieces
    own = norm_gain.shape[1]
    nact = action_table.shape[0]
    micro = range(micros)
    hb_rows = hidden_bias.shape[0] // own
    small_rows = 6 + nact + hb_rows + 1

    small = jnp.concatenate(
        [norm_gain, norm_bias, action_table, hidden_bias.reshape(-1, own), out_bias.reshape(-1, own)], axis=0
    )
    small_all = lax.all_gather(small, "clip", axis=0, tiled=False)
    w_space = gather([space_in, space_out])
    w_time = gather([time_in, time_out])
    w_ff = gather([hidden, down])

    rows_by = lambda start, count: jnp.transpose(small_all[:, start : start + count], (1, 0, 2)).reshape(count, width)
    gain = rows_by(0, 3).astype(f32)
    bias = rows_by(3, 3).astype(f32)
    table = jnp.pad(rows_by(6, nact), ((0, 128 - nact), (0, 0)))
    hb_all = small_all[:, 6 + nact : 6 + nact + hb_rows].reshape(1, -1).astype(f32)
    ob_all = small_all[:, 6 + nact + hb_rows :].reshape(1, -1).astype(f32)

    me = lax.axis_index("tm").astype(jnp.int32)
    place = me.reshape(1)
    tmasks = time_masks(frames, pieces, me)
    hots = [one_hot(action_rows(segments[m], assignment[m], actions[m]), 128) for m in micro]
    smasks = [space_masks(segments[m]) for m in micro]

    pick = lambda parts, index: [parts[m][index] for m in micro]
    outward = lambda parts: [parts[0]] + [
        lax.ppermute(parts[d], "tm", [(k, (k + d) % pieces) for k in range(pieces)]) for d in range(1, pieces)
    ]
    inward = lambda parts: [parts[0]] + [
        lax.ppermute(parts[d], "tm", [(k, (k - d) % pieces) for k in range(pieces)]) for d in range(1, pieces)
    ]
    marks = lambda parts: [mark(a) for a in parts[1:]]
    rounded = lambda values, d: lax.dynamic_slice_in_dim(values, (me + d) % pieces * per, per, axis=1).astype(bf16)
    sent = [[rounded(out_grad[m], d) for d in range(pieces)] for m in micro]

    branch = [outward(sent[0])]
    forward, after, middle, ahead, pieces_out, back, gas, last = [], [], [], [], [], [], [], []
    behind = []
    for m in micro:
        forward.append(
            call_space_forward(behind, m, place, tokens, hots[m], *smasks[m], gain, bias, table, w_space, pieces)
        )
        after.append(outward(forward[m][4:]))
        behind = [forward[m][3]] + marks(branch[0])
    for m in micro:
        middle.append(list(call_time_forward(behind, after[m], *tmasks, gain, bias, w_time)))
        behind = [middle[m][3]]
    for m in micro[1:]:
        late, (middle[-1][4],) = together(sent[m], [middle[-1][4]])
        branch.append(outward(late))
    for m in micro:
        ahead.append(call_feed_forward(behind, branch[m], middle[m][4], gain, bias, hb_all, ob_all, w_ff))
        pieces_out.append(inward(ahead[m][9:]))
        behind = [ahead[m][5]]
    behind += marks(pieces_out[0])
    ff_grad = weight_grad(behind, [(pick(ahead, 1), pick(ahead, 4))], clips, 8 * own, "down_grad", down_at=4 * own)
    ff_grad = weight_columns([], [(pick(ahead, 0), pick(ahead, 2))], clips, 8 * own, "hidden_grad", buffer=ff_grad)
    (ff_grad,), pieces_out[-1] = together([ff_grad], pieces_out[-1])
    ff_part = reduce_clip(ff_grad)
    behind = [ff_grad]
    for m in micro:
        back.append(
            call_time_backward(
                behind, after[m], ahead[m][3], *tmasks, gain, w_time, middle[m][1], middle[m][2], middle[m][3]
            )
        )
        gas.append(inward(back[m][3:]))
        behind = [back[m][1]]
    grad_buffer = None
    for m in micro:
        last.append(
            list(
                call_space_backward(
                    behind, m, gas[m], place, tokens, hots[m], *smasks[m], gain, table, w_space,
                    forward[m][1], forward[m][2], forward[m][3], grad_buffer,
                )
            )
        )
        grad_buffer = last[m][2]
        if m == 0:
            time_grad = weight_columns(
                [last[m][3]], [(pick(middle, 0), pick(back, 0)), (pick(middle, 2), pick(ahead, 3))],
                clips, 4 * own, "time_grad",
            )
            (time_grad,), gas[-1] = together([time_grad], gas[-1])
            time_part = reduce_clip(time_grad)
            (ff_part,), (last[m][4],) = together([ff_part], [last[m][4]])
            ff_half = sum_half(ff_part)
            behind = [mark(time_grad[0]), mark(ff_part)]

    total = lambda values: functools.reduce(jnp.add, values)
    gain_grad = jnp.concatenate([total(pick(last, 3)), total(pick(back, 1)), total(pick(ahead, 5))])
    bias_grad = jnp.concatenate([total(pick(last, 4)), total(pick(back, 2)), total(pick(ahead, 6))])
    table_grad = total(pick(last, 5))[:nact]
    hb_grad = total(pick(ahead, 7))
    ob_grad = total(pick(ahead, 8))
    split = lambda a: jnp.transpose(a.reshape(a.shape[0], clips, own), (1, 0, 2))
    small_grads = jnp.concatenate(
        [
            split(gain_grad), split(bias_grad), split(table_grad),
            hb_grad.reshape(clips, hb_rows, own), ob_grad.reshape(clips, 1, own),
        ],
        axis=1,
    ).astype(bf16).reshape(clips, -1)
    extra = 8 * pieces - 4 * own % (8 * pieces)
    small_grads = jnp.pad(small_grads, ((0, 0), (0, extra * 1024 - small_grads.shape[1]))).reshape(clips, extra, 1024)
    space_grad = weight_grad(
        [mark(ff_half)], [(pick(forward, 0), pick(last, 0)), (pick(forward, 2), pick(last, 1))],
        clips, 4 * own + extra, "space_grad", small=small_grads,
    )

    ff_sum = lax.psum(ff_part, "tm")
    (ff_half,), (space_grad,) = together([ff_half], [space_grad])
    space_part = reduce_clip(space_grad)
    ff_sum = share_half(ff_half)
    (time_part,), (ff_half,) = together([time_part], [ff_half])
    time_sum = share_half(sum_half(time_part))
    early = (
        call_assemble(place, pieces_out),
        columns(time_sum, own, 0, 3),
        columns(time_sum, own, 3, 1),
        columns(ff_sum, own, 0, 4),
        ff_sum[4 * own :].astype(f32),
    )
    space_part, *early = lax.optimization_barrier((space_part,) + early)
    space_sum = share_half(sum_half(space_part))
    mine = space_sum[4 * own :].reshape(-1)[: small_rows * own].reshape(small_rows, own).astype(f32)
    return (
        early[0],
        grad_buffer,
        mine[0:3],
        mine[3:6],
        columns(space_sum, own, 0, 3),
        columns(space_sum, own, 3, 1),
        early[1],
        early[2],
        early[3],
        mine[6 + nact : 6 + nact + hb_rows].reshape(-1),
        early[4],
        mine[6 + nact + hb_rows :].reshape(-1),
        mine[6 : 6 + nact],
    )


def solution(mesh):
    rows = P("clip", None)
    cols = P(None, "clip")
    line = P("clip")
    wide = P(None, "tm", "clip", None)
    return jax.shard_map(
        local,
        mesh=mesh,
        in_specs=(
            wide, cols, cols, P(None, None, "tm"), cols, cols,
            rows, rows, rows, rows, rows, line, rows, line, cols, wide,
        ),
        out_specs=(wide, wide, cols, cols, rows, rows, rows, rows, rows, line, rows, line, cols),
        check_vma=False,
    )
```

```python
import functools

import jax
import jax.numpy as jnp
from jax import lax
from jax.experimental import pallas as pl
from jax.experimental.pallas import tpu as pltpu
from jax.sharding import PartitionSpec as P

HEADS = 16
HEAD = 64
EPS = 1e-05
MASKED = -1e30
ROWS = 256
FF_CHUNK = 1024
FF_GROUPS = 1
VMEM_LIMIT = 62 * 1024 * 1024

bf16 = jnp.bfloat16
f32 = jnp.float32

NN = (((1,), (0,)), ((), ()))
NT = (((1,), (1,)), ((), ()))
TN = (((0,), (0,)), ((), ()))


def dot(left, right, form=NN):
    return lax.dot_general(left, right, form, preferred_element_type=f32)


def standardize(values):
    centered = values - jnp.mean(values, axis=-1, keepdims=True)
    rate = lax.rsqrt(jnp.mean(centered * centered, axis=-1, keepdims=True) + EPS)
    return centered * rate, rate


def norm_back(hat, rate, gain, grad):
    scaled = grad * gain
    return rate * (
        scaled
        - jnp.mean(scaled, axis=-1, keepdims=True)
        - hat * jnp.mean(scaled * hat, axis=-1, keepdims=True)
    )


def add_row(ref, row, first):
    @pl.when(first)
    def _():
        ref[...] = row

    @pl.when(jnp.logical_not(first))
    def _():
        ref[...] += row


def column_sum(values):
    return jnp.sum(values, axis=0, keepdims=True)


def pair_slices(pair):
    lane = pair * 128
    return slice(lane, lane + 128), slice(1024 + lane, 1024 + lane + 128), slice(2048 + lane, 2048 + lane + 128)


def attend(qkv_ref, key_mask, query_mask, mixed_t, lse_ref):
    blank = jnp.zeros((HEAD, ROWS), bf16)
    scale = jnp.asarray(HEAD**-0.5, bf16)

    def scores_of(pair):
        q_at, k_at, v_at = pair_slices(pair)
        q_t = (qkv_ref[:, q_at] * scale).T
        keys = jnp.concatenate([qkv_ref[:, k_at], key_mask], axis=1)
        first = jnp.concatenate([q_t[:HEAD], blank, query_mask], axis=0)
        second = jnp.concatenate([blank, q_t[HEAD:], query_mask], axis=0)
        return dot(keys, jnp.concatenate([first, second], axis=1))

    def finish(pair, scores):
        v_t = qkv_ref[:, pair_slices(pair)[2]].T
        top = jnp.max(scores, axis=0, keepdims=True)
        raised = jnp.exp(scores - top)
        total = jnp.sum(raised, axis=0, keepdims=True)
        weights = raised.astype(bf16)
        lse = top + jnp.log(total)
        rate = 1.0 / total
        for part in range(2):
            head = pair * 2 + part
            at = slice(part * ROWS, (part + 1) * ROWS)
            mixed = dot(v_t[part * HEAD : (part + 1) * HEAD], weights[:, at])
            mixed_t[head * HEAD : (head + 1) * HEAD, :] = (mixed * rate[:, at]).astype(bf16)
            lse_ref[head : head + 1, :] = lse[:, at]

    queue = [scores_of(0), scores_of(1)]
    for pair in range(HEADS // 2):
        if pair + 2 < HEADS // 2:
            queue.append(scores_of(pair + 2))
        finish(pair, queue.pop(0))


def attend_back(qkv_ref, key_mask, query_mask, lse_ref, grad_ref, grad_t, mixed_t, out_ref, query_t):
    blank = jnp.zeros((HEAD, ROWS), bf16)
    scale = jnp.asarray(HEAD**-0.5, bf16)
    low_half = lax.broadcasted_iota(jnp.int32, (ROWS, 128), 1) < HEAD
    zero = jnp.zeros((ROWS, 128), bf16)

    def both(top, bottom, extra):
        first = jnp.concatenate([top, blank] + extra, axis=0)
        second = jnp.concatenate([blank, bottom] + extra, axis=0)
        return jnp.concatenate([first, second], axis=1)

    def halves(values):
        return jnp.concatenate([jnp.where(low_half, values, zero), jnp.where(low_half, zero, values)], axis=0)

    def start(pair):
        q_at, k_at, v_at = pair_slices(pair)
        q_t = (qkv_ref[:, q_at] * scale).T
        keys = jnp.concatenate([qkv_ref[:, k_at], key_mask], axis=1)
        scores = dot(keys, both(q_t[:HEAD], q_t[HEAD:], [query_mask]))
        pair_t = grad_t[q_at, :]
        grad_probs = dot(qkv_ref[:, v_at], both(pair_t[:HEAD], pair_t[HEAD:], []))
        return scores, grad_probs

    def finish(pair, scores, grad_probs):
        q_at, k_at, v_at = pair_slices(pair)
        head = pair * 2
        lse = jnp.concatenate([lse_ref[head : head + 1, :], lse_ref[head + 1 : head + 2, :]], axis=1)
        product = grad_t[q_at, :].astype(f32) * mixed_t[q_at, :].astype(f32)
        along = jnp.concatenate([column_sum(product[:HEAD]), column_sum(product[HEAD:])], axis=1)
        probs = jnp.exp(scores - lse)
        grad_scores = (probs * (grad_probs - along)).astype(bf16)
        out_ref[:, v_at] = dot(probs.astype(bf16), halves(grad_ref[:, q_at])).astype(bf16)
        out_ref[:, k_at] = dot(grad_scores, halves(qkv_ref[:, q_at] * scale)).astype(bf16)
        k_t = (qkv_ref[:, k_at] * scale).T
        for part in range(2):
            at = slice((head + part) * HEAD, (head + part + 1) * HEAD)
            columns_at = slice(part * ROWS, (part + 1) * ROWS)
            query_t[at, :] = dot(k_t[part * HEAD : (part + 1) * HEAD], grad_scores[:, columns_at]).astype(bf16)

    ahead = start(0)
    for pair in range(HEADS // 2):
        held = ahead
        if pair + 1 < HEADS // 2:
            ahead = start(pair + 1)
        finish(pair, *held)
    for quarter in range(4):
        at = slice(quarter * 256, (quarter + 1) * 256)
        out_ref[:, at] = query_t[at, :].T


def block_of(weights, index):
    own = 1024 // weights.shape[0]
    return weights[:, index * own : (index + 1) * own, :].reshape(1024, 1024)


def piece_at(place, step, count, rows):
    return pl.ds(pl.multiple_of(lax.rem(place[0] + step, count) * rows, rows), rows)


def stacked(refs, groups=1):
    per = refs[0].shape[1] // groups
    width = refs[0].shape[-1]
    parts = [ref[:, g * per : (g + 1) * per, :].reshape(-1, width) for g in range(groups) for ref in refs]
    return parts[0] if len(parts) == 1 else jnp.concatenate(parts, axis=0)


def unstack(refs, values, groups=1):
    per = refs[0].shape[1] // groups
    rows = values.shape[0] // (len(refs) * groups)
    for g in range(groups):
        for index, ref in enumerate(refs):
            at = (g * len(refs) + index) * rows
            ref[:, g * per : (g + 1) * per, :] = values[at : at + rows].reshape(ref.shape[0], per, ref.shape[2])


def space_forward(
    place, tok, hot, kmask, qmask, gain, bias, table, weights,
    norm_out, qkv_out, mix_out, lse_out, *rest,
):
    after_out, (mixed_t, after) = rest[:-2], rest[-2:]
    embedded = tok[...].astype(f32) + dot(hot[...], table[...])
    hat, _ = standardize(embedded)
    normed = (hat * gain[0:1, :] + bias[0:1, :]).astype(bf16)
    norm_out[...] = normed
    for part in range(3):
        qkv_out[:, part * 1024 : (part + 1) * 1024] = dot(normed, block_of(weights, part)).astype(bf16)
    attend(qkv_out, kmask[...], qmask[...], mixed_t, lse_out)
    mixed = mixed_t[...].T
    mix_out[...] = mixed
    after[...] = (embedded + dot(mixed, block_of(weights, 3))).astype(bf16)
    count = len(after_out)
    for step in range(count):
        after_out[step][...] = after[piece_at(place, step, count, ROWS // count), :]


def grad_into_norm(gqkv, weights):
    total = None
    for part in range(3):
        piece = dot(gqkv[:, part * 1024 : (part + 1) * 1024], block_of(weights, part), NT)
        total = piece if total is None else total + piece
    return total


def space_backward(count, *refs):
    grads, refs = refs[:count], refs[count:]
    (
        place, tok, hot, kmask, qmask, gain, table, weights, qkv, mix, lse,
        gqkv_out, gas_out, tok_out, gain_out, bias_out, table_out, grad_t, mixed_t, query_t, grad_rows,
    ) = refs
    first = pl.program_id(0) == 0
    for step in range(count):
        gas_out[piece_at(place, step, count, ROWS // count), :] = grads[step][...]
    upstream = gas_out[...]
    mixed_t[...] = mix[...].T
    grad_rows[...] = dot(upstream, block_of(weights, 3), NT).astype(bf16)
    grad_t[...] = grad_rows[...].T
    attend_back(qkv, kmask[...], qmask[...], lse, grad_rows, grad_t, mixed_t, gqkv_out, query_t)
    grad_norm = grad_into_norm(gqkv_out, weights)
    embedded = tok[...].astype(f32) + dot(hot[...], table[...])
    hat, rate = standardize(embedded)
    add_row(gain_out, column_sum(grad_norm * hat), first)
    add_row(bias_out, column_sum(grad_norm), first)
    total = upstream.astype(f32) + norm_back(hat, rate, gain[0:1, :], grad_norm)
    tok_out[...] = total
    add_row(table_out, dot(hot[...], total.astype(bf16), TN), first)


def time_forward(count, *refs):
    x, refs = refs[:count], refs[count:]
    kmask, qmask, gain, bias, weights, norm_out, qkv_out, mix_out, lse_out, after_out, mixed_t = refs
    after_space = stacked(x).astype(f32)
    hat, _ = standardize(after_space)
    normed = (hat * gain[1:2, :] + bias[1:2, :]).astype(bf16)
    norm_out[...] = normed
    for part in range(3):
        qkv_out[:, part * 1024 : (part + 1) * 1024] = dot(normed, block_of(weights, part)).astype(bf16)
    attend(qkv_out, kmask[...], qmask[...], mixed_t, lse_out)
    mixed = mixed_t[...].T
    mix_out[...] = mixed
    after_out[...] = after_space + dot(mixed, block_of(weights, 3))


def feed_forward(count, *refs):
    grad, refs = refs[:count], refs[count:]
    x, gain, bias, hidden_bias, out_bias, weights = refs[:6]
    norm_out, act_out, gpre_out, gat_out, branch_out, gain_out, bias_out, hb_out, ob_out = refs[6:15]
    block_out = refs[15:]
    first = pl.program_id(0) == 0
    clips = weights.shape[0]
    own = 1024 // clips
    groups = x.shape[0]
    width = x.shape[2]
    size = FF_CHUNK
    chunks = 4096 // size
    half = 1024 // size
    share = size * clips // 4096
    branch = stacked(grad, groups)
    branch_out[...] = branch.reshape(branch_out.shape)

    def down_of(chunk):
        if share:
            return weights[chunk * share : (chunk + 1) * share, 4 * own :, :].reshape(size, 1024)
        return None

    def hidden_of(chunk):
        block, column = chunk // half, chunk % half
        return weights[:, block * own : (block + 1) * own, column * size : (column + 1) * size].reshape(1024, size)

    part_at = lambda chunk: slice(chunk * size, (chunk + 1) * size)
    back_act = dot(branch, down_of(0), NT)
    after_time = x[...].reshape(groups * ROWS, width)
    hat, rate = standardize(after_time)
    normed = (hat * gain[2:3, :] + bias[2:3, :]).astype(bf16)
    norm_out[...] = normed.reshape(norm_out.shape)
    pre = dot(normed, hidden_of(0)) + hidden_bias[0:1, part_at(0)]
    result = None
    grad_norm = None
    bias_sums = []
    for chunk in range(chunks):
        at = part_at(chunk)
        u, grad_act = pre, back_act
        if chunk + 1 < chunks:
            pre = dot(normed, hidden_of(chunk + 1)) + hidden_bias[0:1, part_at(chunk + 1)]
            back_act = dot(branch, down_of(chunk + 1), NT)
        c0 = 0.7978845608028654
        square = u * u
        t = jnp.tanh(u * (c0 + (c0 * 0.044715) * square))
        half_plus = 0.5 + 0.5 * t
        act = (u * half_plus).astype(bf16)
        act_out[:, :, at] = act.reshape(groups, ROWS, size)
        slope = half_plus + (0.5 * u) * (1.0 - t * t) * (c0 + (3.0 * c0 * 0.044715) * square)
        gpre = (grad_act * slope).astype(bf16)
        gpre_out[:, :, at] = gpre.reshape(groups, ROWS, size)
        bias_sums.append(column_sum(gpre.astype(f32)))
        down = dot(act, down_of(chunk))
        result = down if result is None else result + down
        back = dot(gpre, hidden_of(chunk), NT)
        grad_norm = back if grad_norm is None else grad_norm + back
    block = (after_time + result + out_bias[0:1, :]).astype(bf16)
    unstack(block_out, block, groups)
    upstream = branch.astype(f32)
    gat = (upstream + norm_back(hat, rate, gain[2:3, :], grad_norm)).astype(bf16)
    gat_out[...] = gat.reshape(gat_out.shape)
    add_row(gain_out, column_sum(grad_norm * hat), first)
    add_row(bias_out, column_sum(grad_norm), first)
    add_row(ob_out, column_sum(upstream), first)
    add_row(hb_out, jnp.concatenate(bias_sums, axis=1), first)


def time_backward(count, *refs):
    x, refs = refs[:count], refs[count:]
    gat, kmask, qmask, gain, weights, qkv, mix, lse, gqkv_out, gain_out, bias_out = refs[:11]
    gas_out = refs[11 : 11 + count]
    grad_t, mixed_t, query_t, grad_rows = refs[11 + count :]
    first = pl.program_id(0) == 0
    upstream = gat[...]
    mixed_t[...] = mix[...].T
    grad_rows[...] = dot(upstream, block_of(weights, 3), NT).astype(bf16)
    grad_t[...] = grad_rows[...].T
    attend_back(qkv, kmask[...], qmask[...], lse, grad_rows, grad_t, mixed_t, gqkv_out, query_t)
    grad_norm = grad_into_norm(gqkv_out, weights)
    hat, rate = standardize(stacked(x).astype(f32))
    add_row(gain_out, column_sum(grad_norm * hat), first)
    add_row(bias_out, column_sum(grad_norm), first)
    total = upstream.astype(f32) + norm_back(hat, rate, gain[1:2, :], grad_norm)
    unstack(gas_out, total.astype(bf16))


def assemble(count, *refs):
    place, parts, out = refs[0], refs[1:-1], refs[-1]
    for micro in range(out.shape[0]):
        for step in range(count):
            out[micro, piece_at(place, step, count, ROWS // count), :] = parts[micro * count + step][...]


def rows_of(ref):
    value = ref[...]
    return value.reshape(-1, value.shape[-1])


def weight_kernel(pairs, micros, own, by_rows, has_small, *refs):
    out = refs[-1]
    offset = 0
    for pair in range(pairs):
        base = pair * 2 * micros
        total = None
        for index in range(micros):
            piece = dot(rows_of(refs[base + index]), rows_of(refs[base + micros + index]), TN)
            total = piece if total is None else total + piece
        total = total.astype(bf16)
        if by_rows:
            out[...] = total.reshape(out.shape)
            continue
        for block in range(total.shape[1] // 1024):
            for shard in range(out.shape[0]):
                out[shard, offset : offset + own, :] = total[
                    shard * own : (shard + 1) * own, block * 1024 : (block + 1) * 1024
                ]
            offset += own
    if has_small:
        out[:, offset:, :] = refs[pairs * 2 * micros][...]


def params():
    return pltpu.CompilerParams(vmem_limit_bytes=VMEM_LIMIT)


def ordered_call(kernel, behind, in_specs, **options):
    count = len(behind)

    def body(*refs):
        kernel(*refs[count:])

    aliases = options.pop("input_output_aliases", {})
    call = pl.pallas_call(
        body,
        in_specs=[pl.BlockSpec(memory_space=pl.ANY)] * count + in_specs,
        input_output_aliases={count + k: v for k, v in aliases.items()},
        compiler_params=params(),
        **options,
    )
    return lambda *operands: call(*behind, *operands)


def whole(shape):
    rank = len(shape)
    return pl.BlockSpec(shape, lambda i: (0,) * rank, pipeline_mode=pl.Buffered(1))


def total_spec(shape):
    rank = len(shape)
    return pl.BlockSpec(shape, lambda i: (0,) * rank)


def step_spec(shape):
    rank = len(shape)
    return pl.BlockSpec((None,) + shape, lambda i: (i,) + (0,) * rank)


def micro_spec(micro, shape):
    rank = len(shape)
    return pl.BlockSpec((None, None) + shape, lambda i: (micro, i) + (0,) * rank)


def shape_of(shape, kind):
    return jax.ShapeDtypeStruct(shape, kind)


def smem():
    return pl.BlockSpec(memory_space=pltpu.SMEM)


def call_space_forward(behind, micro, place, tok, hot, kmask, qmask, gain, bias, table, weights, count):
    _, frames, slots, width = tok.shape
    per = slots // count
    return ordered_call(
        space_forward,
        behind,
        grid=(frames,),
        in_specs=[smem(), micro_spec(micro, (slots, width)), step_spec(hot.shape[1:])]
        + [whole(a.shape) for a in (kmask, qmask, gain, bias, table, weights)],
        out_specs=[
            step_spec((slots, width)), step_spec((slots, 3 * width)), step_spec((slots, width)),
            step_spec((HEADS, slots)),
        ]
        + [step_spec((per, width))] * count,
        out_shape=[
            shape_of((frames, slots, width), bf16), shape_of((frames, slots, 3 * width), bf16),
            shape_of((frames, slots, width), bf16), shape_of((frames, HEADS, slots), f32),
        ]
        + [shape_of((frames, per, width), bf16)] * count,
        scratch_shapes=[pltpu.VMEM((width, ROWS), bf16), pltpu.VMEM((ROWS, width), bf16)],
        name="space_forward",
    )(place, tok, hot, kmask, qmask, gain, bias, table, weights)


def back_scratch(width):
    return [
        pltpu.VMEM((width, ROWS), bf16), pltpu.VMEM((width, ROWS), bf16),
        pltpu.VMEM((width, ROWS), bf16), pltpu.VMEM((ROWS, width), bf16),
    ]


def call_space_backward(
    behind, micro, grads, place, tok, hot, kmask, qmask, gain, table, weights, qkv, mix, lse, buffer
):
    micros, frames, slots, width = tok.shape
    count = len(grads)
    row = shape_of((1, width), f32)
    operands = list(grads) + [place, tok, hot, kmask, qmask, gain, table, weights, qkv, mix, lse]
    specs = (
        [step_spec((slots // count, width))] * count
        + [smem(), micro_spec(micro, (slots, width)), step_spec(hot.shape[1:])]
        + [whole(a.shape) for a in (kmask, qmask, gain, table, weights)]
        + [step_spec((slots, 3 * width)), step_spec((slots, width)), step_spec((HEADS, slots))]
    )
    before = len(operands)
    kernel = functools.partial(space_backward, count)
    aliases = {}
    if buffer is not None:
        aliases = {before: 2}
        operands.append(buffer)
        specs.append(pl.BlockSpec(memory_space=pl.ANY))
        kernel = lambda *refs: space_backward(count, *refs[:before], *refs[before + 1 :])
    return ordered_call(
        kernel,
        behind,
        grid=(frames,),
        in_specs=specs,
        out_specs=[
            step_spec((slots, 3 * width)), step_spec((slots, width)), micro_spec(micro, (slots, width)),
            total_spec((1, width)), total_spec((1, width)), total_spec((hot.shape[2], width)),
        ],
        out_shape=[
            shape_of((frames, slots, 3 * width), bf16), shape_of((frames, slots, width), bf16),
            shape_of((micros, frames, slots, width), f32), row, row, shape_of((hot.shape[2], width), f32),
        ],
        scratch_shapes=back_scratch(width),
        input_output_aliases=aliases,
        name="space_backward",
    )(*operands)


def group_spec(array, count):
    frames, _, width = array.shape
    return pl.BlockSpec((frames, ROWS // (frames * count), width), lambda i: (0, i, 0))


def call_time_forward(behind, x, kmask, qmask, gain, bias, weights):
    count = len(x)
    frames, slots, width = x[0].shape
    groups = slots * frames * count // ROWS
    return ordered_call(
        functools.partial(time_forward, count),
        behind,
        grid=(groups,),
        in_specs=[group_spec(a, count) for a in x] + [whole(a.shape) for a in (kmask, qmask, gain, bias, weights)],
        out_specs=[
            step_spec((ROWS, width)), step_spec((ROWS, 3 * width)), step_spec((ROWS, width)),
            step_spec((HEADS, ROWS)), step_spec((ROWS, width)),
        ],
        out_shape=[
            shape_of((groups, ROWS, width), bf16), shape_of((groups, ROWS, 3 * width), bf16),
            shape_of((groups, ROWS, width), bf16), shape_of((groups, HEADS, ROWS), f32),
            shape_of((groups, ROWS, width), f32),
        ],
        scratch_shapes=[pltpu.VMEM((width, ROWS), bf16)],
        name="time_forward",
    )(*x, kmask, qmask, gain, bias, weights)


def call_feed_forward(behind, grad, x, gain, bias, hidden_bias, out_bias, weights):
    count = len(grad)
    groups, _, width = x.shape
    ff = hidden_bias.shape[1]
    each = FF_GROUPS if groups % FF_GROUPS == 0 else 1
    row = shape_of((1, width), f32)
    rows = lambda cols: shape_of((groups, ROWS, cols), bf16)
    spec = lambda cols: pl.BlockSpec((each, ROWS, cols), lambda i: (i, 0, 0))
    grad_spec = lambda a: pl.BlockSpec(
        (a.shape[0], each * ROWS // (a.shape[0] * count), width), lambda i: (0, i, 0)
    )
    return ordered_call(
        functools.partial(feed_forward, count),
        behind,
        grid=(groups // each,),
        in_specs=[grad_spec(a) for a in grad]
        + [spec(width)]
        + [whole(a.shape) for a in (gain, bias, hidden_bias, out_bias, weights)],
        out_specs=[
            spec(width), spec(ff), spec(ff), spec(width), spec(width),
            total_spec((1, width)), total_spec((1, width)), total_spec((1, ff)), total_spec((1, width)),
        ]
        + [grad_spec(a) for a in grad],
        out_shape=[rows(width), rows(ff), rows(ff), rows(width), rows(width), row, row, shape_of((1, ff), f32), row]
        + [shape_of(a.shape, bf16) for a in grad],
        name="feed_forward",
    )(*grad, x, gain, bias, hidden_bias, out_bias, weights)


def call_time_backward(behind, x, gat, kmask, qmask, gain, weights, qkv, mix, lse):
    count = len(x)
    groups, _, width = gat.shape
    row = shape_of((1, width), f32)
    return ordered_call(
        functools.partial(time_backward, count),
        behind,
        grid=(groups,),
        in_specs=[group_spec(a, count) for a in x]
        + [step_spec((ROWS, width))]
        + [whole(a.shape) for a in (kmask, qmask, gain, weights)]
        + [step_spec((ROWS, 3 * width)), step_spec((ROWS, width)), step_spec((HEADS, ROWS))],
        out_specs=[step_spec((ROWS, 3 * width)), total_spec((1, width)), total_spec((1, width))]
        + [group_spec(a, count) for a in x],
        out_shape=[shape_of((groups, ROWS, 3 * width), bf16), row, row] + [shape_of(a.shape, bf16) for a in x],
        scratch_shapes=back_scratch(width),
        name="time_backward",
    )(*x, gat, kmask, qmask, gain, weights, qkv, mix, lse)


def call_assemble(place, parts):
    micros, count = len(parts), len(parts[0])
    frames, per, width = parts[0][0].shape
    flat = [p for pieces in parts for p in pieces]
    return ordered_call(
        functools.partial(assemble, count),
        [],
        grid=(frames,),
        in_specs=[smem()] + [step_spec((per, width))] * len(flat),
        out_specs=pl.BlockSpec((micros, None, per * count, width), lambda i: (0, i, 0, 0)),
        out_shape=shape_of((micros, frames, per * count, width), bf16),
        name="assemble",
    )(place, *flat)


def weight_grad(behind, pairs, clips, rows, name, small=None, down_at=None):
    own = 1024 // clips
    block = 256 if down_at is None else 512
    width = pairs[0][0][0].shape[-1]
    by_rows = down_at is not None

    def left_spec(a):
        rank = a.ndim
        return pl.BlockSpec(a.shape[:-1] + (block,), lambda i: (0,) * (rank - 1) + (i,))

    operands, specs = [], []
    cols = 0
    for lefts, rights in pairs:
        operands += list(lefts) + list(rights)
        specs += [left_spec(a) for a in lefts] + [whole(a.shape) for a in rights]
        cols += rights[0].shape[-1]
    shards = block // own
    if small is not None:
        operands.append(small)
        specs.append(pl.BlockSpec((shards,) + small.shape[1:], lambda i: (i, 0, 0)))
    if by_rows:
        per = width // clips
        out_spec = pl.BlockSpec((block // per, per, 1024), lambda i: (i, down_at // per, 0))
    else:
        out_rows = cols // 1024 * own + (0 if small is None else small.shape[1])
        out_spec = pl.BlockSpec((shards, out_rows, 1024), lambda i: (i, 0, 0))
    return ordered_call(
        functools.partial(weight_kernel, len(pairs), len(pairs[0][0]), own, by_rows, small is not None),
        behind,
        grid=(width // block,),
        in_specs=specs,
        out_specs=out_spec,
        out_shape=shape_of((clips, rows, 1024), bf16),
        name=name,
    )(*operands)


def column_kernel(starts, micros, *refs):
    out = refs[-1]
    step = pl.program_id(0)
    for pair, (start, end) in enumerate(starts):
        lefts = refs[pair * 2 * micros : pair * 2 * micros + micros]
        rights = refs[pair * 2 * micros + micros : (pair + 1) * 2 * micros]

        def fill():
            total = None
            for left, right in zip(lefts, rights):
                piece = dot(rows_of(left), rows_of(right), TN)
                total = piece if total is None else total + piece
            out[...] = total.astype(bf16).reshape(out.shape)

        if len(starts) == 1:
            fill()
        else:
            pl.when(jnp.logical_and(step >= start, step < end))(fill)


def weight_columns(behind, pairs, clips, rows, name, buffer=None):
    own = 1024 // clips
    block = 512
    operands, specs, starts = [], [], []
    step = 0
    for lefts, rights in pairs:
        count = rights[0].shape[-1] // block

        def right_spec(a, start=step, last=count - 1):
            rank = a.ndim
            return pl.BlockSpec(
                a.shape[:-1] + (block,), lambda i: (0,) * (rank - 1) + (jnp.clip(i - start, 0, last),)
            )

        operands += list(lefts) + list(rights)
        specs += [whole(a.shape) for a in lefts] + [right_spec(a) for a in rights]
        starts.append((step, step + count))
        step += count
    kernel = functools.partial(column_kernel, starts, len(pairs[0][0]))
    aliases = {}
    if buffer is not None:
        before = len(operands)
        aliases = {before: 0}
        operands.append(buffer)
        specs.append(pl.BlockSpec(memory_space=pl.ANY))
        inner = kernel
        kernel = lambda *refs: inner(*refs[:before], *refs[before + 1 :])
    return ordered_call(
        kernel,
        behind,
        grid=(step,),
        in_specs=specs,
        out_specs=pl.BlockSpec((clips, own, block), lambda i: (0, i // 2, i % 2)),
        out_shape=shape_of((clips, rows, 1024), bf16),
        input_output_aliases=aliases,
        name=name,
    )(*operands)


def one_hot(index, count, kind=bf16):
    return (index[..., None] == jnp.arange(count)).astype(kind)


def space_masks(labels):
    keys = one_hot(labels, 128)
    queries = jnp.where(labels[None, :] == jnp.arange(128)[:, None], 0.0, MASKED)
    queries = jnp.where(jnp.arange(128)[:, None] < 8, queries, 0.0).astype(bf16)
    return keys, queries


def time_masks(frames, count, me):
    per = ROWS // frames
    row = jnp.arange(ROWS)
    held = frames // count
    frame = jnp.mod(me - row // (held * per), count) * held + row // per % held
    place = row % per
    lane = jnp.arange(128)
    keys = ((lane[None, :] == place[:, None]) | (lane[None, :] == per + frame[:, None])).astype(bf16)
    other = (lane[:, None] < per) & (lane[:, None] != place[None, :])
    later = (lane[:, None] >= per) & (lane[:, None] < per + frames) & (lane[:, None] - per > frame[None, :])
    queries = jnp.where(other | later, MASKED, 0.0).astype(bf16)
    return keys, queries


def action_rows(labels, owners, actions):
    clip_of = jnp.sum(jnp.where(labels[:, None] == jnp.arange(owners.shape[0]), owners[None, :], 0), axis=1)
    hit = clip_of[:, None] == jnp.arange(actions.shape[0])
    chosen = jnp.sum(jnp.where(hit[:, :, None], actions[None], 0), axis=1)
    return jnp.transpose(chosen)


def exchange(values):
    return lax.all_to_all(values, "tm", 0, 0, tiled=True)


def gather(shards):
    own = shards[0].shape[0]
    parts = []
    for shard in shards:
        rows, cols = shard.shape
        parts += [shard[:, at : at + 1024] for at in range(0, cols, 1024)]
    return lax.all_gather(jnp.concatenate(parts, axis=0), "clip", axis=0, tiled=False)


def reduce_clip(total):
    return lax.psum_scatter(total, "clip", scatter_dimension=0, tiled=False)


def shift(values, step):
    count = lax.axis_size("tm")
    return lax.ppermute(values, "tm", [(k, (k + step) % count) for k in range(count)])


def sum_half(part):
    count = lax.axis_size("tm")
    rows = part.shape[0] // count
    me = lax.axis_index("tm")
    piece = lambda step: lax.dynamic_slice_in_dim(part, lax.rem(me + step, count) * rows, rows, axis=0)
    total = piece(0).astype(f32)
    for received in [shift(piece(step), step) for step in range(1, count)]:
        total = total + received.astype(f32)
    return total.astype(bf16)


def share_half(mine):
    count = lax.axis_size("tm")
    rows = mine.shape[0]
    me = lax.axis_index("tm")
    whole_rows = jnp.zeros((count * rows, mine.shape[1]), mine.dtype)
    for step, held in enumerate([mine] + [shift(mine, step) for step in range(1, count)]):
        at = lax.rem(me + count - step, count) * rows
        whole_rows = lax.dynamic_update_slice_in_dim(whole_rows, held, at, axis=0)
    return whole_rows


def mark(values):
    return values.reshape(-1, values.shape[-1])[:8, :128]


def together(*lists):
    flat = lax.optimization_barrier([a for arrays in lists for a in arrays])
    out = []
    for arrays in lists:
        out.append(list(flat[: len(arrays)]))
        flat = flat[len(arrays) :]
    return out


def columns(rows, own, first, count):
    return jnp.concatenate([rows[(first + c) * own : (first + c + 1) * own] for c in range(count)], axis=1).astype(f32)


def local(
    tokens, segments, assignment, actions, norm_gain, norm_bias,
    space_in, space_out, time_in, time_out, hidden, hidden_bias, down, out_bias,
    action_table, out_grad,
):
    micros, frames_here, slots, width = tokens.shape
    pieces = lax.axis_size("tm")
    clips = lax.axis_size("clip")
    frames = frames_here * pieces
    per = slots // pieces
    own = norm_gain.shape[1]
    nact = action_table.shape[0]
    micro = range(micros)
    hb_rows = hidden_bias.shape[0] // own
    small_rows = 6 + nact + hb_rows + 1

    small = jnp.concatenate(
        [norm_gain, norm_bias, action_table, hidden_bias.reshape(-1, own), out_bias.reshape(-1, own)], axis=0
    )
    small_all = lax.all_gather(small, "clip", axis=0, tiled=False)
    w_space = gather([space_in, space_out])
    w_time = gather([time_in, time_out])
    w_ff = gather([hidden, down])

    rows_by = lambda start, count: jnp.transpose(small_all[:, start : start + count], (1, 0, 2)).reshape(count, width)
    gain = rows_by(0, 3).astype(f32)
    bias = rows_by(3, 3).astype(f32)
    table = jnp.pad(rows_by(6, nact), ((0, 128 - nact), (0, 0)))
    hb_all = small_all[:, 6 + nact : 6 + nact + hb_rows].reshape(1, -1).astype(f32)
    ob_all = small_all[:, 6 + nact + hb_rows :].reshape(1, -1).astype(f32)

    me = lax.axis_index("tm").astype(jnp.int32)
    place = me.reshape(1)
    tmasks = time_masks(frames, pieces, me)
    hots = [one_hot(action_rows(segments[m], assignment[m], actions[m]), 128) for m in micro]
    smasks = [space_masks(segments[m]) for m in micro]

    pick = lambda parts, index: [parts[m][index] for m in micro]
    outward = lambda parts: [parts[0]] + [
        lax.ppermute(parts[d], "tm", [(k, (k + d) % pieces) for k in range(pieces)]) for d in range(1, pieces)
    ]
    inward = lambda parts: [parts[0]] + [
        lax.ppermute(parts[d], "tm", [(k, (k - d) % pieces) for k in range(pieces)]) for d in range(1, pieces)
    ]
    marks = lambda parts: [mark(a) for a in parts[1:]]
    rounded = lambda values, d: lax.dynamic_slice_in_dim(values, (me + d) % pieces * per, per, axis=1).astype(bf16)
    sent = [[rounded(out_grad[m], d) for d in range(pieces)] for m in micro]

    branch = [outward(sent[0])]
    forward, after, middle, ahead, pieces_out, back, gas, last = [], [], [], [], [], [], [], []
    behind = []
    for m in micro:
        forward.append(
            call_space_forward(behind, m, place, tokens, hots[m], *smasks[m], gain, bias, table, w_space, pieces)
        )
        after.append(outward(forward[m][4:]))
        behind = [forward[m][3]] + marks(branch[0])
    for m in micro:
        middle.append(list(call_time_forward(behind, after[m], *tmasks, gain, bias, w_time)))
        behind = [middle[m][3]]
    for m in micro[1:]:
        late, (middle[-1][4],) = together(sent[m], [middle[-1][4]])
        branch.append(outward(late))
    for m in micro:
        ahead.append(call_feed_forward(behind, branch[m], middle[m][4], gain, bias, hb_all, ob_all, w_ff))
        pieces_out.append(inward(ahead[m][9:]))
        behind = [ahead[m][5]]
    behind += marks(pieces_out[0])
    ff_grad = weight_grad(behind, [(pick(ahead, 1), pick(ahead, 4))], clips, 8 * own, "down_grad", down_at=4 * own)
    ff_grad = weight_columns([], [(pick(ahead, 0), pick(ahead, 2))], clips, 8 * own, "hidden_grad", buffer=ff_grad)
    (ff_grad,), pieces_out[-1] = together([ff_grad], pieces_out[-1])
    ff_part = reduce_clip(ff_grad)
    behind = [ff_grad]
    for m in micro:
        back.append(
            call_time_backward(
                behind, after[m], ahead[m][3], *tmasks, gain, w_time, middle[m][1], middle[m][2], middle[m][3]
            )
        )
        gas.append(inward(back[m][3:]))
        behind = [back[m][1]]
    time_grad = weight_columns(
        behind, [(pick(middle, 0), pick(back, 0)), (pick(middle, 2), pick(ahead, 3))], clips, 4 * own, "time_grad"
    )
    (time_grad,), gas[0] = together([time_grad], gas[0])
    time_part = reduce_clip(time_grad)
    behind = [time_grad]
    grad_buffer = None
    for m in micro:
        last.append(
            list(
                call_space_backward(
                    behind, m, gas[m], place, tokens, hots[m], *smasks[m], gain, table, w_space,
                    forward[m][1], forward[m][2], forward[m][3], grad_buffer,
                )
            )
        )
        grad_buffer = last[m][2]
        behind = []
        if m == 0:
            (ff_part,), (last[m][3],), gas[-1] = together([ff_part], [last[m][3]], gas[-1])
            ff_half = sum_half(ff_part)
            behind = [mark(ff_part)]

    total = lambda values: functools.reduce(jnp.add, values)
    gain_grad = jnp.concatenate([total(pick(last, 3)), total(pick(back, 1)), total(pick(ahead, 5))])
    bias_grad = jnp.concatenate([total(pick(last, 4)), total(pick(back, 2)), total(pick(ahead, 6))])
    table_grad = total(pick(last, 5))[:nact]
    hb_grad = total(pick(ahead, 7))
    ob_grad = total(pick(ahead, 8))
    split = lambda a: jnp.transpose(a.reshape(a.shape[0], clips, own), (1, 0, 2))
    small_grads = jnp.concatenate(
        [
            split(gain_grad), split(bias_grad), split(table_grad),
            hb_grad.reshape(clips, hb_rows, own), ob_grad.reshape(clips, 1, own),
        ],
        axis=1,
    ).astype(bf16).reshape(clips, -1)
    extra = 8 * pieces - 4 * own % (8 * pieces)
    small_grads = jnp.pad(small_grads, ((0, 0), (0, extra * 1024 - small_grads.shape[1]))).reshape(clips, extra, 1024)
    space_grad = weight_grad(
        [mark(ff_half)], [(pick(forward, 0), pick(last, 0)), (pick(forward, 2), pick(last, 1))],
        clips, 4 * own + extra, "space_grad", small=small_grads,
    )

    ff_sum = lax.psum(ff_part, "tm")
    (ff_half,), (space_grad,) = together([ff_half], [space_grad])
    space_part = reduce_clip(space_grad)
    ff_sum = share_half(ff_half)
    (time_part,), (ff_half,) = together([time_part], [ff_half])
    time_sum = share_half(sum_half(time_part))
    early = (
        call_assemble(place, pieces_out),
        columns(time_sum, own, 0, 3),
        columns(time_sum, own, 3, 1),
        columns(ff_sum, own, 0, 4),
        ff_sum[4 * own :].astype(f32),
    )
    space_part, *early = lax.optimization_barrier((space_part,) + early)
    space_sum = lax.psum(space_part, "tm")
    mine = space_sum[4 * own :].reshape(-1)[: small_rows * own].reshape(small_rows, own).astype(f32)
    return (
        early[0],
        grad_buffer,
        mine[0:3],
        mine[3:6],
        columns(space_sum, own, 0, 3),
        columns(space_sum, own, 3, 1),
        early[1],
        early[2],
        early[3],
        mine[6 + nact : 6 + nact + hb_rows].reshape(-1),
        early[4],
        mine[6 + nact + hb_rows :].reshape(-1),
        mine[6 : 6 + nact],
    )


def solution(mesh):
    rows = P("clip", None)
    cols = P(None, "clip")
    line = P("clip")
    wide = P(None, "tm", "clip", None)
    return jax.shard_map(
        local,
        mesh=mesh,
        in_specs=(
            wide, cols, cols, P(None, None, "tm"), cols, cols,
            rows, rows, rows, rows, rows, line, rows, line, cols, wide,
        ),
        out_specs=(wide, wide, cols, cols, rows, rows, rows, rows, rows, line, rows, line, cols),
        check_vma=False,
    )
```

```python
import functools

import jax
import jax.numpy as jnp
from jax import lax
from jax.experimental import pallas as pl
from jax.experimental.pallas import tpu as pltpu
from jax.sharding import PartitionSpec as P

HEADS = 16
HEAD = 64
EPS = 1e-05
MASKED = -1e30
ROWS = 256
FF_CHUNK = 1024
FF_GROUPS = 1
VMEM_LIMIT = 62 * 1024 * 1024

bf16 = jnp.bfloat16
f32 = jnp.float32

NN = (((1,), (0,)), ((), ()))
NT = (((1,), (1,)), ((), ()))
TN = (((0,), (0,)), ((), ()))


def dot(left, right, form=NN):
    return lax.dot_general(left, right, form, preferred_element_type=f32)


def standardize(values):
    centered = values - jnp.mean(values, axis=-1, keepdims=True)
    rate = lax.rsqrt(jnp.mean(centered * centered, axis=-1, keepdims=True) + EPS)
    return centered * rate, rate


def norm_back(hat, rate, gain, grad):
    scaled = grad * gain
    return rate * (
        scaled
        - jnp.mean(scaled, axis=-1, keepdims=True)
        - hat * jnp.mean(scaled * hat, axis=-1, keepdims=True)
    )


def add_row(ref, row, first):
    @pl.when(first)
    def _():
        ref[...] = row

    @pl.when(jnp.logical_not(first))
    def _():
        ref[...] += row


def column_sum(values):
    return jnp.sum(values, axis=0, keepdims=True)


def pair_slices(pair):
    lane = pair * 128
    return slice(lane, lane + 128), slice(1024 + lane, 1024 + lane + 128), slice(2048 + lane, 2048 + lane + 128)


def attend(qkv_ref, key_mask, query_mask, mixed_t, lse_ref):
    blank = jnp.zeros((HEAD, ROWS), bf16)
    scale = jnp.asarray(HEAD**-0.5, bf16)

    def scores_of(pair):
        q_at, k_at, v_at = pair_slices(pair)
        q_t = (qkv_ref[:, q_at] * scale).T
        keys = jnp.concatenate([qkv_ref[:, k_at], key_mask], axis=1)
        first = jnp.concatenate([q_t[:HEAD], blank, query_mask], axis=0)
        second = jnp.concatenate([blank, q_t[HEAD:], query_mask], axis=0)
        return dot(keys, jnp.concatenate([first, second], axis=1))

    def finish(pair, scores):
        v_t = qkv_ref[:, pair_slices(pair)[2]].T
        top = jnp.max(scores, axis=0, keepdims=True)
        raised = jnp.exp(scores - top)
        total = jnp.sum(raised, axis=0, keepdims=True)
        weights = raised.astype(bf16)
        lse = top + jnp.log(total)
        rate = 1.0 / total
        for part in range(2):
            head = pair * 2 + part
            at = slice(part * ROWS, (part + 1) * ROWS)
            mixed = dot(v_t[part * HEAD : (part + 1) * HEAD], weights[:, at])
            mixed_t[head * HEAD : (head + 1) * HEAD, :] = (mixed * rate[:, at]).astype(bf16)
            lse_ref[head : head + 1, :] = lse[:, at]

    queue = [scores_of(0), scores_of(1)]
    for pair in range(HEADS // 2):
        if pair + 2 < HEADS // 2:
            queue.append(scores_of(pair + 2))
        finish(pair, queue.pop(0))


def attend_back(qkv_ref, key_mask, query_mask, lse_ref, grad_ref, grad_t, mixed_t, out_ref, query_t):
    blank = jnp.zeros((HEAD, ROWS), bf16)
    scale = jnp.asarray(HEAD**-0.5, bf16)
    low_half = lax.broadcasted_iota(jnp.int32, (ROWS, 128), 1) < HEAD
    zero = jnp.zeros((ROWS, 128), bf16)

    def both(top, bottom, extra):
        first = jnp.concatenate([top, blank] + extra, axis=0)
        second = jnp.concatenate([blank, bottom] + extra, axis=0)
        return jnp.concatenate([first, second], axis=1)

    def halves(values):
        return jnp.concatenate([jnp.where(low_half, values, zero), jnp.where(low_half, zero, values)], axis=0)

    def start(pair):
        q_at, k_at, v_at = pair_slices(pair)
        q_t = (qkv_ref[:, q_at] * scale).T
        keys = jnp.concatenate([qkv_ref[:, k_at], key_mask], axis=1)
        scores = dot(keys, both(q_t[:HEAD], q_t[HEAD:], [query_mask]))
        pair_t = grad_t[q_at, :]
        grad_probs = dot(qkv_ref[:, v_at], both(pair_t[:HEAD], pair_t[HEAD:], []))
        return scores, grad_probs

    def finish(pair, scores, grad_probs):
        q_at, k_at, v_at = pair_slices(pair)
        head = pair * 2
        lse = jnp.concatenate([lse_ref[head : head + 1, :], lse_ref[head + 1 : head + 2, :]], axis=1)
        product = grad_t[q_at, :].astype(f32) * mixed_t[q_at, :].astype(f32)
        along = jnp.concatenate([column_sum(product[:HEAD]), column_sum(product[HEAD:])], axis=1)
        probs = jnp.exp(scores - lse)
        grad_scores = (probs * (grad_probs - along)).astype(bf16)
        out_ref[:, v_at] = dot(probs.astype(bf16), halves(grad_ref[:, q_at])).astype(bf16)
        out_ref[:, k_at] = dot(grad_scores, halves(qkv_ref[:, q_at] * scale)).astype(bf16)
        k_t = (qkv_ref[:, k_at] * scale).T
        for part in range(2):
            at = slice((head + part) * HEAD, (head + part + 1) * HEAD)
            columns_at = slice(part * ROWS, (part + 1) * ROWS)
            query_t[at, :] = dot(k_t[part * HEAD : (part + 1) * HEAD], grad_scores[:, columns_at]).astype(bf16)

    ahead = start(0)
    for pair in range(HEADS // 2):
        held = ahead
        if pair + 1 < HEADS // 2:
            ahead = start(pair + 1)
        finish(pair, *held)
    for quarter in range(4):
        at = slice(quarter * 256, (quarter + 1) * 256)
        out_ref[:, at] = query_t[at, :].T


def block_of(weights, index):
    own = 1024 // weights.shape[0]
    return weights[:, index * own : (index + 1) * own, :].reshape(1024, 1024)


def piece_at(place, step, count, rows):
    return pl.ds(pl.multiple_of(lax.rem(place[0] + step, count) * rows, rows), rows)


def stacked(refs, groups=1):
    per = refs[0].shape[1] // groups
    width = refs[0].shape[-1]
    parts = [ref[:, g * per : (g + 1) * per, :].reshape(-1, width) for g in range(groups) for ref in refs]
    return parts[0] if len(parts) == 1 else jnp.concatenate(parts, axis=0)


def unstack(refs, values, groups=1):
    per = refs[0].shape[1] // groups
    rows = values.shape[0] // (len(refs) * groups)
    for g in range(groups):
        for index, ref in enumerate(refs):
            at = (g * len(refs) + index) * rows
            ref[:, g * per : (g + 1) * per, :] = values[at : at + rows].reshape(ref.shape[0], per, ref.shape[2])


def space_forward(
    place, tok, hot, kmask, qmask, gain, bias, table, weights,
    norm_out, qkv_out, mix_out, lse_out, *rest,
):
    after_out, (mixed_t, after) = rest[:-2], rest[-2:]
    embedded = tok[...].astype(f32) + dot(hot[...], table[...])
    hat, _ = standardize(embedded)
    normed = (hat * gain[0:1, :] + bias[0:1, :]).astype(bf16)
    norm_out[...] = normed
    for part in range(3):
        qkv_out[:, part * 1024 : (part + 1) * 1024] = dot(normed, block_of(weights, part)).astype(bf16)
    attend(qkv_out, kmask[...], qmask[...], mixed_t, lse_out)
    mixed = mixed_t[...].T
    mix_out[...] = mixed
    after[...] = (embedded + dot(mixed, block_of(weights, 3))).astype(bf16)
    count = len(after_out)
    for step in range(count):
        after_out[step][...] = after[piece_at(place, step, count, ROWS // count), :]


def grad_into_norm(gqkv, weights):
    total = None
    for part in range(3):
        piece = dot(gqkv[:, part * 1024 : (part + 1) * 1024], block_of(weights, part), NT)
        total = piece if total is None else total + piece
    return total


def space_backward(count, *refs):
    grads, refs = refs[:count], refs[count:]
    (
        place, tok, hot, kmask, qmask, gain, table, weights, qkv, mix, lse,
        gqkv_out, gas_out, tok_out, gain_out, bias_out, table_out, grad_t, mixed_t, query_t, grad_rows,
    ) = refs
    first = pl.program_id(0) == 0
    for step in range(count):
        gas_out[piece_at(place, step, count, ROWS // count), :] = grads[step][...]
    upstream = gas_out[...]
    mixed_t[...] = mix[...].T
    grad_rows[...] = dot(upstream, block_of(weights, 3), NT).astype(bf16)
    grad_t[...] = grad_rows[...].T
    attend_back(qkv, kmask[...], qmask[...], lse, grad_rows, grad_t, mixed_t, gqkv_out, query_t)
    grad_norm = grad_into_norm(gqkv_out, weights)
    embedded = tok[...].astype(f32) + dot(hot[...], table[...])
    hat, rate = standardize(embedded)
    add_row(gain_out, column_sum(grad_norm * hat), first)
    add_row(bias_out, column_sum(grad_norm), first)
    total = upstream.astype(f32) + norm_back(hat, rate, gain[0:1, :], grad_norm)
    tok_out[...] = total
    add_row(table_out, dot(hot[...], total.astype(bf16), TN), first)


def time_forward(count, *refs):
    x, refs = refs[:count], refs[count:]
    kmask, qmask, gain, bias, weights, norm_out, qkv_out, mix_out, lse_out, after_out, mixed_t = refs
    after_space = stacked(x).astype(f32)
    hat, _ = standardize(after_space)
    normed = (hat * gain[1:2, :] + bias[1:2, :]).astype(bf16)
    norm_out[...] = normed
    for part in range(3):
        qkv_out[:, part * 1024 : (part + 1) * 1024] = dot(normed, block_of(weights, part)).astype(bf16)
    attend(qkv_out, kmask[...], qmask[...], mixed_t, lse_out)
    mixed = mixed_t[...].T
    mix_out[...] = mixed
    after_out[...] = after_space + dot(mixed, block_of(weights, 3))


def feed_forward(count, *refs):
    grad, refs = refs[:count], refs[count:]
    x, gain, bias, hidden_bias, out_bias, weights = refs[:6]
    norm_out, act_out, gpre_out, gat_out, branch_out, gain_out, bias_out, hb_out, ob_out = refs[6:15]
    block_out = refs[15:]
    first = pl.program_id(0) == 0
    clips = weights.shape[0]
    own = 1024 // clips
    groups = x.shape[0]
    width = x.shape[2]
    size = FF_CHUNK
    chunks = 4096 // size
    half = 1024 // size
    share = size * clips // 4096
    branch = stacked(grad, groups)
    branch_out[...] = branch.reshape(branch_out.shape)

    def down_of(chunk):
        if share:
            return weights[chunk * share : (chunk + 1) * share, 4 * own :, :].reshape(size, 1024)
        return None

    def hidden_of(chunk):
        block, column = chunk // half, chunk % half
        return weights[:, block * own : (block + 1) * own, column * size : (column + 1) * size].reshape(1024, size)

    part_at = lambda chunk: slice(chunk * size, (chunk + 1) * size)
    back_act = dot(branch, down_of(0), NT)
    after_time = x[...].reshape(groups * ROWS, width)
    hat, rate = standardize(after_time)
    normed = (hat * gain[2:3, :] + bias[2:3, :]).astype(bf16)
    norm_out[...] = normed.reshape(norm_out.shape)
    pre = dot(normed, hidden_of(0)) + hidden_bias[0:1, part_at(0)]
    result = None
    grad_norm = None
    bias_sums = []
    for chunk in range(chunks):
        at = part_at(chunk)
        u, grad_act = pre, back_act
        if chunk + 1 < chunks:
            pre = dot(normed, hidden_of(chunk + 1)) + hidden_bias[0:1, part_at(chunk + 1)]
            back_act = dot(branch, down_of(chunk + 1), NT)
        c0 = 0.7978845608028654
        square = u * u
        t = jnp.tanh(u * (c0 + (c0 * 0.044715) * square))
        half_plus = 0.5 + 0.5 * t
        act = (u * half_plus).astype(bf16)
        act_out[:, :, at] = act.reshape(groups, ROWS, size)
        slope = half_plus + (0.5 * u) * (1.0 - t * t) * (c0 + (3.0 * c0 * 0.044715) * square)
        gpre = (grad_act * slope).astype(bf16)
        gpre_out[:, :, at] = gpre.reshape(groups, ROWS, size)
        bias_sums.append(column_sum(gpre.astype(f32)))
        down = dot(act, down_of(chunk))
        result = down if result is None else result + down
        back = dot(gpre, hidden_of(chunk), NT)
        grad_norm = back if grad_norm is None else grad_norm + back
    block = (after_time + result + out_bias[0:1, :]).astype(bf16)
    unstack(block_out, block, groups)
    upstream = branch.astype(f32)
    gat = (upstream + norm_back(hat, rate, gain[2:3, :], grad_norm)).astype(bf16)
    gat_out[...] = gat.reshape(gat_out.shape)
    add_row(gain_out, column_sum(grad_norm * hat), first)
    add_row(bias_out, column_sum(grad_norm), first)
    add_row(ob_out, column_sum(upstream), first)
    add_row(hb_out, jnp.concatenate(bias_sums, axis=1), first)


def time_backward(count, *refs):
    x, refs = refs[:count], refs[count:]
    gat, kmask, qmask, gain, weights, qkv, mix, lse, gqkv_out, gain_out, bias_out = refs[:11]
    gas_out = refs[11 : 11 + count]
    grad_t, mixed_t, query_t, grad_rows = refs[11 + count :]
    first = pl.program_id(0) == 0
    upstream = gat[...]
    mixed_t[...] = mix[...].T
    grad_rows[...] = dot(upstream, block_of(weights, 3), NT).astype(bf16)
    grad_t[...] = grad_rows[...].T
    attend_back(qkv, kmask[...], qmask[...], lse, grad_rows, grad_t, mixed_t, gqkv_out, query_t)
    grad_norm = grad_into_norm(gqkv_out, weights)
    hat, rate = standardize(stacked(x).astype(f32))
    add_row(gain_out, column_sum(grad_norm * hat), first)
    add_row(bias_out, column_sum(grad_norm), first)
    total = upstream.astype(f32) + norm_back(hat, rate, gain[1:2, :], grad_norm)
    unstack(gas_out, total.astype(bf16))


def assemble(count, *refs):
    place, parts, out = refs[0], refs[1:-1], refs[-1]
    for micro in range(out.shape[0]):
        for step in range(count):
            out[micro, piece_at(place, step, count, ROWS // count), :] = parts[micro * count + step][...]


def rows_of(ref):
    value = ref[...]
    return value.reshape(-1, value.shape[-1])


def weight_kernel(pairs, micros, own, by_rows, has_small, *refs):
    out = refs[-1]
    offset = 0
    for pair in range(pairs):
        base = pair * 2 * micros
        total = None
        for index in range(micros):
            piece = dot(rows_of(refs[base + index]), rows_of(refs[base + micros + index]), TN)
            total = piece if total is None else total + piece
        total = total.astype(bf16)
        if by_rows:
            out[...] = total.reshape(out.shape)
            continue
        for block in range(total.shape[1] // 1024):
            for shard in range(out.shape[0]):
                out[shard, offset : offset + own, :] = total[
                    shard * own : (shard + 1) * own, block * 1024 : (block + 1) * 1024
                ]
            offset += own
    if has_small:
        out[:, offset:, :] = refs[pairs * 2 * micros][...]


def params():
    return pltpu.CompilerParams(vmem_limit_bytes=VMEM_LIMIT)


def ordered_call(kernel, behind, in_specs, **options):
    count = len(behind)

    def body(*refs):
        kernel(*refs[count:])

    aliases = options.pop("input_output_aliases", {})
    call = pl.pallas_call(
        body,
        in_specs=[pl.BlockSpec(memory_space=pl.ANY)] * count + in_specs,
        input_output_aliases={count + k: v for k, v in aliases.items()},
        compiler_params=params(),
        **options,
    )
    return lambda *operands: call(*behind, *operands)


def whole(shape):
    rank = len(shape)
    return pl.BlockSpec(shape, lambda i: (0,) * rank, pipeline_mode=pl.Buffered(1))


def total_spec(shape):
    rank = len(shape)
    return pl.BlockSpec(shape, lambda i: (0,) * rank)


def step_spec(shape):
    rank = len(shape)
    return pl.BlockSpec((None,) + shape, lambda i: (i,) + (0,) * rank)


def micro_spec(micro, shape):
    rank = len(shape)
    return pl.BlockSpec((None, None) + shape, lambda i: (micro, i) + (0,) * rank)


def shape_of(shape, kind):
    return jax.ShapeDtypeStruct(shape, kind)


def smem():
    return pl.BlockSpec(memory_space=pltpu.SMEM)


def call_space_forward(behind, micro, place, tok, hot, kmask, qmask, gain, bias, table, weights, count):
    _, frames, slots, width = tok.shape
    per = slots // count
    return ordered_call(
        space_forward,
        behind,
        grid=(frames,),
        in_specs=[smem(), micro_spec(micro, (slots, width)), step_spec(hot.shape[1:])]
        + [whole(a.shape) for a in (kmask, qmask, gain, bias, table, weights)],
        out_specs=[
            step_spec((slots, width)), step_spec((slots, 3 * width)), step_spec((slots, width)),
            step_spec((HEADS, slots)),
        ]
        + [step_spec((per, width))] * count,
        out_shape=[
            shape_of((frames, slots, width), bf16), shape_of((frames, slots, 3 * width), bf16),
            shape_of((frames, slots, width), bf16), shape_of((frames, HEADS, slots), f32),
        ]
        + [shape_of((frames, per, width), bf16)] * count,
        scratch_shapes=[pltpu.VMEM((width, ROWS), bf16), pltpu.VMEM((ROWS, width), bf16)],
        name="space_forward",
    )(place, tok, hot, kmask, qmask, gain, bias, table, weights)


def back_scratch(width):
    return [
        pltpu.VMEM((width, ROWS), bf16), pltpu.VMEM((width, ROWS), bf16),
        pltpu.VMEM((width, ROWS), bf16), pltpu.VMEM((ROWS, width), bf16),
    ]


def call_space_backward(
    behind, micro, grads, place, tok, hot, kmask, qmask, gain, table, weights, qkv, mix, lse, buffer
):
    micros, frames, slots, width = tok.shape
    count = len(grads)
    row = shape_of((1, width), f32)
    operands = list(grads) + [place, tok, hot, kmask, qmask, gain, table, weights, qkv, mix, lse]
    specs = (
        [step_spec((slots // count, width))] * count
        + [smem(), micro_spec(micro, (slots, width)), step_spec(hot.shape[1:])]
        + [whole(a.shape) for a in (kmask, qmask, gain, table, weights)]
        + [step_spec((slots, 3 * width)), step_spec((slots, width)), step_spec((HEADS, slots))]
    )
    before = len(operands)
    kernel = functools.partial(space_backward, count)
    aliases = {}
    if buffer is not None:
        aliases = {before: 2}
        operands.append(buffer)
        specs.append(pl.BlockSpec(memory_space=pl.ANY))
        kernel = lambda *refs: space_backward(count, *refs[:before], *refs[before + 1 :])
    return ordered_call(
        kernel,
        behind,
        grid=(frames,),
        in_specs=specs,
        out_specs=[
            step_spec((slots, 3 * width)), step_spec((slots, width)), micro_spec(micro, (slots, width)),
            total_spec((1, width)), total_spec((1, width)), total_spec((hot.shape[2], width)),
        ],
        out_shape=[
            shape_of((frames, slots, 3 * width), bf16), shape_of((frames, slots, width), bf16),
            shape_of((micros, frames, slots, width), f32), row, row, shape_of((hot.shape[2], width), f32),
        ],
        scratch_shapes=back_scratch(width),
        input_output_aliases=aliases,
        name="space_backward",
    )(*operands)


def group_spec(array, count):
    frames, _, width = array.shape
    return pl.BlockSpec((frames, ROWS // (frames * count), width), lambda i: (0, i, 0))


def call_time_forward(behind, x, kmask, qmask, gain, bias, weights):
    count = len(x)
    frames, slots, width = x[0].shape
    groups = slots * frames * count // ROWS
    return ordered_call(
        functools.partial(time_forward, count),
        behind,
        grid=(groups,),
        in_specs=[group_spec(a, count) for a in x] + [whole(a.shape) for a in (kmask, qmask, gain, bias, weights)],
        out_specs=[
            step_spec((ROWS, width)), step_spec((ROWS, 3 * width)), step_spec((ROWS, width)),
            step_spec((HEADS, ROWS)), step_spec((ROWS, width)),
        ],
        out_shape=[
            shape_of((groups, ROWS, width), bf16), shape_of((groups, ROWS, 3 * width), bf16),
            shape_of((groups, ROWS, width), bf16), shape_of((groups, HEADS, ROWS), f32),
            shape_of((groups, ROWS, width), f32),
        ],
        scratch_shapes=[pltpu.VMEM((width, ROWS), bf16)],
        name="time_forward",
    )(*x, kmask, qmask, gain, bias, weights)


def call_feed_forward(behind, grad, x, gain, bias, hidden_bias, out_bias, weights):
    count = len(grad)
    groups, _, width = x.shape
    ff = hidden_bias.shape[1]
    each = FF_GROUPS if groups % FF_GROUPS == 0 else 1
    row = shape_of((1, width), f32)
    rows = lambda cols: shape_of((groups, ROWS, cols), bf16)
    spec = lambda cols: pl.BlockSpec((each, ROWS, cols), lambda i: (i, 0, 0))
    grad_spec = lambda a: pl.BlockSpec(
        (a.shape[0], each * ROWS // (a.shape[0] * count), width), lambda i: (0, i, 0)
    )
    return ordered_call(
        functools.partial(feed_forward, count),
        behind,
        grid=(groups // each,),
        in_specs=[grad_spec(a) for a in grad]
        + [spec(width)]
        + [whole(a.shape) for a in (gain, bias, hidden_bias, out_bias, weights)],
        out_specs=[
            spec(width), spec(ff), spec(ff), spec(width), spec(width),
            total_spec((1, width)), total_spec((1, width)), total_spec((1, ff)), total_spec((1, width)),
        ]
        + [grad_spec(a) for a in grad],
        out_shape=[rows(width), rows(ff), rows(ff), rows(width), rows(width), row, row, shape_of((1, ff), f32), row]
        + [shape_of(a.shape, bf16) for a in grad],
        name="feed_forward",
    )(*grad, x, gain, bias, hidden_bias, out_bias, weights)


def call_time_backward(behind, x, gat, kmask, qmask, gain, weights, qkv, mix, lse):
    count = len(x)
    groups, _, width = gat.shape
    row = shape_of((1, width), f32)
    return ordered_call(
        functools.partial(time_backward, count),
        behind,
        grid=(groups,),
        in_specs=[group_spec(a, count) for a in x]
        + [step_spec((ROWS, width))]
        + [whole(a.shape) for a in (kmask, qmask, gain, weights)]
        + [step_spec((ROWS, 3 * width)), step_spec((ROWS, width)), step_spec((HEADS, ROWS))],
        out_specs=[step_spec((ROWS, 3 * width)), total_spec((1, width)), total_spec((1, width))]
        + [group_spec(a, count) for a in x],
        out_shape=[shape_of((groups, ROWS, 3 * width), bf16), row, row] + [shape_of(a.shape, bf16) for a in x],
        scratch_shapes=back_scratch(width),
        name="time_backward",
    )(*x, gat, kmask, qmask, gain, weights, qkv, mix, lse)


def call_assemble(place, parts):
    micros, count = len(parts), len(parts[0])
    frames, per, width = parts[0][0].shape
    flat = [p for pieces in parts for p in pieces]
    return ordered_call(
        functools.partial(assemble, count),
        [],
        grid=(frames,),
        in_specs=[smem()] + [step_spec((per, width))] * len(flat),
        out_specs=pl.BlockSpec((micros, None, per * count, width), lambda i: (0, i, 0, 0)),
        out_shape=shape_of((micros, frames, per * count, width), bf16),
        name="assemble",
    )(place, *flat)


def weight_grad(behind, pairs, clips, rows, name, small=None, down_at=None):
    own = 1024 // clips
    block = 256 if down_at is None else 512
    width = pairs[0][0][0].shape[-1]
    by_rows = down_at is not None

    def left_spec(a):
        rank = a.ndim
        return pl.BlockSpec(a.shape[:-1] + (block,), lambda i: (0,) * (rank - 1) + (i,))

    operands, specs = [], []
    cols = 0
    for lefts, rights in pairs:
        operands += list(lefts) + list(rights)
        specs += [left_spec(a) for a in lefts] + [whole(a.shape) for a in rights]
        cols += rights[0].shape[-1]
    shards = block // own
    if small is not None:
        operands.append(small)
        specs.append(pl.BlockSpec((shards,) + small.shape[1:], lambda i: (i, 0, 0)))
    if by_rows:
        per = width // clips
        out_spec = pl.BlockSpec((block // per, per, 1024), lambda i: (i, down_at // per, 0))
    else:
        out_rows = cols // 1024 * own + (0 if small is None else small.shape[1])
        out_spec = pl.BlockSpec((shards, out_rows, 1024), lambda i: (i, 0, 0))
    return ordered_call(
        functools.partial(weight_kernel, len(pairs), len(pairs[0][0]), own, by_rows, small is not None),
        behind,
        grid=(width // block,),
        in_specs=specs,
        out_specs=out_spec,
        out_shape=shape_of((clips, rows, 1024), bf16),
        name=name,
    )(*operands)


def column_kernel(starts, micros, *refs):
    out = refs[-1]
    step = pl.program_id(0)
    for pair, (start, end) in enumerate(starts):
        lefts = refs[pair * 2 * micros : pair * 2 * micros + micros]
        rights = refs[pair * 2 * micros + micros : (pair + 1) * 2 * micros]

        def fill():
            total = None
            for left, right in zip(lefts, rights):
                piece = dot(rows_of(left), rows_of(right), TN)
                total = piece if total is None else total + piece
            out[...] = total.astype(bf16).reshape(out.shape)

        if len(starts) == 1:
            fill()
        else:
            pl.when(jnp.logical_and(step >= start, step < end))(fill)


def weight_columns(behind, pairs, clips, rows, name, buffer=None):
    own = 1024 // clips
    block = 512
    operands, specs, starts = [], [], []
    step = 0
    for lefts, rights in pairs:
        count = rights[0].shape[-1] // block

        def right_spec(a, start=step, last=count - 1):
            rank = a.ndim
            return pl.BlockSpec(
                a.shape[:-1] + (block,), lambda i: (0,) * (rank - 1) + (jnp.clip(i - start, 0, last),)
            )

        operands += list(lefts) + list(rights)
        specs += [whole(a.shape) for a in lefts] + [right_spec(a) for a in rights]
        starts.append((step, step + count))
        step += count
    kernel = functools.partial(column_kernel, starts, len(pairs[0][0]))
    aliases = {}
    if buffer is not None:
        before = len(operands)
        aliases = {before: 0}
        operands.append(buffer)
        specs.append(pl.BlockSpec(memory_space=pl.ANY))
        inner = kernel
        kernel = lambda *refs: inner(*refs[:before], *refs[before + 1 :])
    return ordered_call(
        kernel,
        behind,
        grid=(step,),
        in_specs=specs,
        out_specs=pl.BlockSpec((clips, own, block), lambda i: (0, i // 2, i % 2)),
        out_shape=shape_of((clips, rows, 1024), bf16),
        input_output_aliases=aliases,
        name=name,
    )(*operands)


def one_hot(index, count, kind=bf16):
    return (index[..., None] == jnp.arange(count)).astype(kind)


def space_masks(labels):
    keys = one_hot(labels, 128)
    queries = jnp.where(labels[None, :] == jnp.arange(128)[:, None], 0.0, MASKED)
    queries = jnp.where(jnp.arange(128)[:, None] < 8, queries, 0.0).astype(bf16)
    return keys, queries


def time_masks(frames, count, me):
    per = ROWS // frames
    row = jnp.arange(ROWS)
    held = frames // count
    frame = jnp.mod(me - row // (held * per), count) * held + row // per % held
    place = row % per
    lane = jnp.arange(128)
    keys = ((lane[None, :] == place[:, None]) | (lane[None, :] == per + frame[:, None])).astype(bf16)
    other = (lane[:, None] < per) & (lane[:, None] != place[None, :])
    later = (lane[:, None] >= per) & (lane[:, None] < per + frames) & (lane[:, None] - per > frame[None, :])
    queries = jnp.where(other | later, MASKED, 0.0).astype(bf16)
    return keys, queries


def action_rows(labels, owners, actions):
    clip_of = jnp.sum(jnp.where(labels[:, None] == jnp.arange(owners.shape[0]), owners[None, :], 0), axis=1)
    hit = clip_of[:, None] == jnp.arange(actions.shape[0])
    chosen = jnp.sum(jnp.where(hit[:, :, None], actions[None], 0), axis=1)
    return jnp.transpose(chosen)


def exchange(values):
    return lax.all_to_all(values, "tm", 0, 0, tiled=True)


def gather(shards):
    own = shards[0].shape[0]
    parts = []
    for shard in shards:
        rows, cols = shard.shape
        parts += [shard[:, at : at + 1024] for at in range(0, cols, 1024)]
    return lax.all_gather(jnp.concatenate(parts, axis=0), "clip", axis=0, tiled=False)


def reduce_clip(total):
    return lax.psum_scatter(total, "clip", scatter_dimension=0, tiled=False)


def shift(values, step):
    count = lax.axis_size("tm")
    return lax.ppermute(values, "tm", [(k, (k + step) % count) for k in range(count)])


def sum_half(part):
    count = lax.axis_size("tm")
    rows = part.shape[0] // count
    me = lax.axis_index("tm")
    piece = lambda step: lax.dynamic_slice_in_dim(part, lax.rem(me + step, count) * rows, rows, axis=0)
    total = piece(0).astype(f32)
    for received in [shift(piece(step), step) for step in range(1, count)]:
        total = total + received.astype(f32)
    return total.astype(bf16)


def share(mine):
    return [mine] + [shift(mine, step) for step in range(1, lax.axis_size("tm"))]


def joined(held):
    count = len(held)
    rows, width = held[0].shape
    me = lax.axis_index("tm")
    values = jnp.zeros((count * rows, width), held[0].dtype)
    for step, piece in enumerate(held):
        values = lax.dynamic_update_slice_in_dim(values, piece, lax.rem(me + count - step, count) * rows, axis=0)
    return values


def mark(values):
    return values.reshape(-1, values.shape[-1])[:8, :128]


def together(*lists):
    flat = lax.optimization_barrier([a for arrays in lists for a in arrays])
    out = []
    for arrays in lists:
        out.append(list(flat[: len(arrays)]))
        flat = flat[len(arrays) :]
    return out


def columns(rows, own, first, count):
    return jnp.concatenate([rows[(first + c) * own : (first + c + 1) * own] for c in range(count)], axis=1).astype(f32)


def local(
    tokens, segments, assignment, actions, norm_gain, norm_bias,
    space_in, space_out, time_in, time_out, hidden, hidden_bias, down, out_bias,
    action_table, out_grad,
):
    micros, frames_here, slots, width = tokens.shape
    pieces = lax.axis_size("tm")
    clips = lax.axis_size("clip")
    frames = frames_here * pieces
    per = slots // pieces
    own = norm_gain.shape[1]
    nact = action_table.shape[0]
    micro = range(micros)
    hb_rows = hidden_bias.shape[0] // own
    small_rows = 6 + nact + hb_rows + 1

    small = jnp.concatenate(
        [norm_gain, norm_bias, action_table, hidden_bias.reshape(-1, own), out_bias.reshape(-1, own)], axis=0
    )
    small_all = lax.all_gather(small, "clip", axis=0, tiled=False)
    w_space = gather([space_in, space_out])
    w_time = gather([time_in, time_out])
    w_ff = gather([hidden, down])

    rows_by = lambda start, count: jnp.transpose(small_all[:, start : start + count], (1, 0, 2)).reshape(count, width)
    gain = rows_by(0, 3).astype(f32)
    bias = rows_by(3, 3).astype(f32)
    table = jnp.pad(rows_by(6, nact), ((0, 128 - nact), (0, 0)))
    hb_all = small_all[:, 6 + nact : 6 + nact + hb_rows].reshape(1, -1).astype(f32)
    ob_all = small_all[:, 6 + nact + hb_rows :].reshape(1, -1).astype(f32)

    me = lax.axis_index("tm").astype(jnp.int32)
    place = me.reshape(1)
    tmasks = time_masks(frames, pieces, me)
    hots = [one_hot(action_rows(segments[m], assignment[m], actions[m]), 128) for m in micro]
    smasks = [space_masks(segments[m]) for m in micro]

    pick = lambda parts, index: [parts[m][index] for m in micro]
    outward = lambda parts: [parts[0]] + [
        lax.ppermute(parts[d], "tm", [(k, (k + d) % pieces) for k in range(pieces)]) for d in range(1, pieces)
    ]
    inward = lambda parts: [parts[0]] + [
        lax.ppermute(parts[d], "tm", [(k, (k - d) % pieces) for k in range(pieces)]) for d in range(1, pieces)
    ]
    marks = lambda parts: [mark(a) for a in parts[1:]]
    rounded = lambda values, d: lax.dynamic_slice_in_dim(values, (me + d) % pieces * per, per, axis=1).astype(bf16)
    sent = [[rounded(out_grad[m], d) for d in range(pieces)] for m in micro]

    branch = [outward(sent[0])]
    forward, after, middle, ahead, pieces_out, back, gas, last = [], [], [], [], [], [], [], []
    behind = []
    for m in micro:
        forward.append(
            call_space_forward(behind, m, place, tokens, hots[m], *smasks[m], gain, bias, table, w_space, pieces)
        )
        after.append(outward(forward[m][4:]))
        behind = [forward[m][3]] + marks(branch[0])
    for m in micro:
        middle.append(list(call_time_forward(behind, after[m], *tmasks, gain, bias, w_time)))
        behind = [middle[m][3]]
    for m in micro[1:]:
        late, (middle[-1][4],) = together(sent[m], [middle[-1][4]])
        branch.append(outward(late))
    for m in micro:
        ahead.append(call_feed_forward(behind, branch[m], middle[m][4], gain, bias, hb_all, ob_all, w_ff))
        pieces_out.append(inward(ahead[m][9:]))
        behind = [ahead[m][5]]
    behind += marks(pieces_out[0])
    ff_grad = weight_grad(behind, [(pick(ahead, 1), pick(ahead, 4))], clips, 8 * own, "down_grad", down_at=4 * own)
    ff_grad = weight_columns([], [(pick(ahead, 0), pick(ahead, 2))], clips, 8 * own, "hidden_grad", buffer=ff_grad)
    (ff_grad,), pieces_out[-1] = together([ff_grad], pieces_out[-1])
    ff_part = reduce_clip(ff_grad)
    behind = [ff_grad]
    for m in micro:
        back.append(
            call_time_backward(
                behind, after[m], ahead[m][3], *tmasks, gain, w_time, middle[m][1], middle[m][2], middle[m][3]
            )
        )
        gas.append(inward(back[m][3:]))
        behind = [back[m][1]]
    time_grad = weight_columns(
        behind, [(pick(middle, 0), pick(back, 0)), (pick(middle, 2), pick(ahead, 3))], clips, 4 * own, "time_grad"
    )
    (time_grad,), gas[0] = together([time_grad], gas[0])
    time_part = reduce_clip(time_grad)
    behind = [time_grad]
    grad_buffer = None
    for m in micro:
        last.append(
            list(
                call_space_backward(
                    behind, m, gas[m], place, tokens, hots[m], *smasks[m], gain, table, w_space,
                    forward[m][1], forward[m][2], forward[m][3], grad_buffer,
                )
            )
        )
        grad_buffer = last[m][2]
        behind = []
        if m == 0:
            (ff_part,), (last[m][3],), gas[-1] = together([ff_part], [last[m][3]], gas[-1])
            ff_half = sum_half(ff_part)
            behind = [mark(ff_part)]

    total = lambda values: functools.reduce(jnp.add, values)
    gain_grad = jnp.concatenate([total(pick(last, 3)), total(pick(back, 1)), total(pick(ahead, 5))])
    bias_grad = jnp.concatenate([total(pick(last, 4)), total(pick(back, 2)), total(pick(ahead, 6))])
    table_grad = total(pick(last, 5))[:nact]
    hb_grad = total(pick(ahead, 7))
    ob_grad = total(pick(ahead, 8))
    split = lambda a: jnp.transpose(a.reshape(a.shape[0], clips, own), (1, 0, 2))
    small_grads = jnp.concatenate(
        [
            split(gain_grad), split(bias_grad), split(table_grad),
            hb_grad.reshape(clips, hb_rows, own), ob_grad.reshape(clips, 1, own),
        ],
        axis=1,
    ).astype(bf16).reshape(clips, -1)
    extra = 8 * pieces - 4 * own % (8 * pieces)
    small_grads = jnp.pad(small_grads, ((0, 0), (0, extra * 1024 - small_grads.shape[1]))).reshape(clips, extra, 1024)
    space_grad = weight_grad(
        [mark(ff_half)], [(pick(forward, 0), pick(last, 0)), (pick(forward, 2), pick(last, 1))],
        clips, 4 * own + extra, "space_grad", small=small_grads,
    )

    ff_shared = share(ff_half)
    (space_grad,), (time_part,), ff_shared[1::2] = together([space_grad], [time_part], ff_shared[1::2])
    space_part = reduce_clip(space_grad)
    ff_sum = joined(ff_shared)
    time_sum = joined(share(sum_half(time_part)))
    early = (
        call_assemble(place, pieces_out),
        columns(time_sum, own, 0, 3),
        columns(time_sum, own, 3, 1),
        columns(ff_sum, own, 0, 4),
        ff_sum[4 * own :].astype(f32),
    )
    space_part, *early = lax.optimization_barrier((space_part,) + early)
    space_sum = joined(share(sum_half(space_part)))
    mine = space_sum[4 * own :].reshape(-1)[: small_rows * own].reshape(small_rows, own).astype(f32)
    return (
        early[0],
        grad_buffer,
        mine[0:3],
        mine[3:6],
        columns(space_sum, own, 0, 3),
        columns(space_sum, own, 3, 1),
        early[1],
        early[2],
        early[3],
        mine[6 + nact : 6 + nact + hb_rows].reshape(-1),
        early[4],
        mine[6 + nact + hb_rows :].reshape(-1),
        mine[6 : 6 + nact],
    )


def solution(mesh):
    rows = P("clip", None)
    cols = P(None, "clip")
    line = P("clip")
    wide = P(None, "tm", "clip", None)
    return jax.shard_map(
        local,
        mesh=mesh,
        in_specs=(
            wide, cols, cols, P(None, None, "tm"), cols, cols,
            rows, rows, rows, rows, rows, line, rows, line, cols, wide,
        ),
        out_specs=(wide, wide, cols, cols, rows, rows, rows, rows, rows, line, rows, line, cols),
        check_vma=False,
    )
```

```python
import functools

import jax
import jax.numpy as jnp
from jax import lax
from jax.experimental import pallas as pl
from jax.experimental.pallas import tpu as pltpu
from jax.sharding import PartitionSpec as P

HEADS = 16
HEAD = 64
EPS = 1e-05
MASKED = -1e30
ROWS = 256
RAISED = (HEADS // 2, ROWS, 2 * ROWS)
FF_CHUNK = 1024
FF_GROUPS = 1
VMEM_LIMIT = 62 * 1024 * 1024

bf16 = jnp.bfloat16
f32 = jnp.float32

NN = (((1,), (0,)), ((), ()))
NT = (((1,), (1,)), ((), ()))
TN = (((0,), (0,)), ((), ()))


def dot(left, right, form=NN):
    return lax.dot_general(left, right, form, preferred_element_type=f32)


def standardize(values):
    centered = values - jnp.mean(values, axis=-1, keepdims=True)
    rate = lax.rsqrt(jnp.mean(centered * centered, axis=-1, keepdims=True) + EPS)
    return centered * rate, rate


def norm_back(hat, rate, gain, grad):
    scaled = grad * gain
    return rate * (
        scaled
        - jnp.mean(scaled, axis=-1, keepdims=True)
        - hat * jnp.mean(scaled * hat, axis=-1, keepdims=True)
    )


def add_row(ref, row, first):
    @pl.when(first)
    def _():
        ref[...] = row

    @pl.when(jnp.logical_not(first))
    def _():
        ref[...] += row


def column_sum(values):
    return jnp.sum(values, axis=0, keepdims=True)


def pair_slices(pair):
    lane = pair * 128
    return slice(lane, lane + 128), slice(1024 + lane, 1024 + lane + 128), slice(2048 + lane, 2048 + lane + 128)


def attend(qkv_ref, key_mask, query_mask, mixed_t, raised_ref, rate_ref):
    blank = jnp.zeros((HEAD, ROWS), bf16)
    scale = jnp.asarray(HEAD**-0.5, bf16)

    def scores_of(pair):
        q_at, k_at, v_at = pair_slices(pair)
        q_t = (qkv_ref[:, q_at] * scale).T
        keys = jnp.concatenate([qkv_ref[:, k_at], key_mask], axis=1)
        first = jnp.concatenate([q_t[:HEAD], blank, query_mask], axis=0)
        second = jnp.concatenate([blank, q_t[HEAD:], query_mask], axis=0)
        return dot(keys, jnp.concatenate([first, second], axis=1))

    def finish(pair, scores):
        v_t = qkv_ref[:, pair_slices(pair)[2]].T
        top = jnp.max(scores, axis=0, keepdims=True)
        raised = jnp.exp(scores - top)
        total = jnp.sum(raised, axis=0, keepdims=True)
        weights = raised.astype(bf16)
        rate = 1.0 / total
        raised_ref[pair] = weights
        for part in range(2):
            head = pair * 2 + part
            at = slice(part * ROWS, (part + 1) * ROWS)
            mixed = dot(v_t[part * HEAD : (part + 1) * HEAD], weights[:, at])
            mixed_t[head * HEAD : (head + 1) * HEAD, :] = (mixed * rate[:, at]).astype(bf16)
            rate_ref[head : head + 1, :] = rate[:, at]

    queue = [scores_of(0), scores_of(1)]
    for pair in range(HEADS // 2):
        if pair + 2 < HEADS // 2:
            queue.append(scores_of(pair + 2))
        finish(pair, queue.pop(0))


def attend_back(qkv_ref, raised_ref, rate_ref, grad_ref, grad_t, mixed_t, out_ref, query_t):
    blank = jnp.zeros((HEAD, ROWS), bf16)
    scale = jnp.asarray(HEAD**-0.5, bf16)
    low_half = lax.broadcasted_iota(jnp.int32, (ROWS, 128), 1) < HEAD
    zero = jnp.zeros((ROWS, 128), bf16)

    def both(top, bottom):
        first = jnp.concatenate([top, blank], axis=0)
        second = jnp.concatenate([blank, bottom], axis=0)
        return jnp.concatenate([first, second], axis=1)

    def halves(values):
        return jnp.concatenate([jnp.where(low_half, values, zero), jnp.where(low_half, zero, values)], axis=0)

    def start(pair):
        q_at, _, v_at = pair_slices(pair)
        pair_t = grad_t[q_at, :]
        return dot(qkv_ref[:, v_at], both(pair_t[:HEAD], pair_t[HEAD:]))

    def finish(pair, grad_probs):
        q_at, k_at, v_at = pair_slices(pair)
        head = pair * 2
        rate = jnp.concatenate([rate_ref[head : head + 1, :], rate_ref[head + 1 : head + 2, :]], axis=1)
        product = grad_t[q_at, :].astype(f32) * mixed_t[q_at, :].astype(f32)
        along = jnp.concatenate([column_sum(product[:HEAD]), column_sum(product[HEAD:])], axis=1)
        probs = raised_ref[pair].astype(f32) * rate
        grad_scores = (probs * (grad_probs - along)).astype(bf16)
        out_ref[:, v_at] = dot(probs.astype(bf16), halves(grad_ref[:, q_at])).astype(bf16)
        out_ref[:, k_at] = dot(grad_scores, halves(qkv_ref[:, q_at] * scale)).astype(bf16)
        k_t = (qkv_ref[:, k_at] * scale).T
        for part in range(2):
            at = slice((head + part) * HEAD, (head + part + 1) * HEAD)
            columns_at = slice(part * ROWS, (part + 1) * ROWS)
            query_t[at, :] = dot(k_t[part * HEAD : (part + 1) * HEAD], grad_scores[:, columns_at]).astype(bf16)

    ahead = start(0)
    for pair in range(HEADS // 2):
        held = ahead
        if pair + 1 < HEADS // 2:
            ahead = start(pair + 1)
        finish(pair, held)
    for quarter in range(4):
        at = slice(quarter * 256, (quarter + 1) * 256)
        out_ref[:, at] = query_t[at, :].T


def block_of(weights, index):
    own = 1024 // weights.shape[0]
    return weights[:, index * own : (index + 1) * own, :].reshape(1024, 1024)


def piece_at(place, step, count, rows):
    return pl.ds(pl.multiple_of(lax.rem(place[0] + step, count) * rows, rows), rows)


def stacked(refs, groups=1):
    per = refs[0].shape[1] // groups
    width = refs[0].shape[-1]
    parts = [ref[:, g * per : (g + 1) * per, :].reshape(-1, width) for g in range(groups) for ref in refs]
    return parts[0] if len(parts) == 1 else jnp.concatenate(parts, axis=0)


def unstack(refs, values, groups=1):
    per = refs[0].shape[1] // groups
    rows = values.shape[0] // (len(refs) * groups)
    for g in range(groups):
        for index, ref in enumerate(refs):
            at = (g * len(refs) + index) * rows
            ref[:, g * per : (g + 1) * per, :] = values[at : at + rows].reshape(ref.shape[0], per, ref.shape[2])


def space_forward(
    place, tok, hot, kmask, qmask, gain, bias, table, weights,
    norm_out, qkv_out, mix_out, lse_out, raised_out, *rest,
):
    after_out, (mixed_t, after) = rest[:-2], rest[-2:]
    embedded = tok[...].astype(f32) + dot(hot[...], table[...])
    hat, _ = standardize(embedded)
    normed = (hat * gain[0:1, :] + bias[0:1, :]).astype(bf16)
    norm_out[...] = normed
    for part in range(3):
        qkv_out[:, part * 1024 : (part + 1) * 1024] = dot(normed, block_of(weights, part)).astype(bf16)
    attend(qkv_out, kmask[...], qmask[...], mixed_t, raised_out, lse_out)
    mixed = mixed_t[...].T
    mix_out[...] = mixed
    after[...] = (embedded + dot(mixed, block_of(weights, 3))).astype(bf16)
    count = len(after_out)
    for step in range(count):
        after_out[step][...] = after[piece_at(place, step, count, ROWS // count), :]


def grad_into_norm(gqkv, weights):
    total = None
    for part in range(3):
        piece = dot(gqkv[:, part * 1024 : (part + 1) * 1024], block_of(weights, part), NT)
        total = piece if total is None else total + piece
    return total


def space_backward(count, *refs):
    grads, refs = refs[:count], refs[count:]
    (
        place, tok, hot, raised, gain, table, weights, qkv, mix, lse,
        gqkv_out, gas_out, tok_out, gain_out, bias_out, table_out, grad_t, mixed_t, query_t, grad_rows,
    ) = refs
    first = pl.program_id(0) == 0
    for step in range(count):
        gas_out[piece_at(place, step, count, ROWS // count), :] = grads[step][...]
    upstream = gas_out[...]
    mixed_t[...] = mix[...].T
    grad_rows[...] = dot(upstream, block_of(weights, 3), NT).astype(bf16)
    grad_t[...] = grad_rows[...].T
    attend_back(qkv, raised, lse, grad_rows, grad_t, mixed_t, gqkv_out, query_t)
    grad_norm = grad_into_norm(gqkv_out, weights)
    embedded = tok[...].astype(f32) + dot(hot[...], table[...])
    hat, rate = standardize(embedded)
    add_row(gain_out, column_sum(grad_norm * hat), first)
    add_row(bias_out, column_sum(grad_norm), first)
    total = upstream.astype(f32) + norm_back(hat, rate, gain[0:1, :], grad_norm)
    tok_out[...] = total
    add_row(table_out, dot(hot[...], total.astype(bf16), TN), first)


def time_forward(count, *refs):
    x, refs = refs[:count], refs[count:]
    kmask, qmask, gain, bias, weights, norm_out, qkv_out, mix_out, lse_out, raised_out, after_out, mixed_t = refs
    after_space = stacked(x).astype(f32)
    hat, _ = standardize(after_space)
    normed = (hat * gain[1:2, :] + bias[1:2, :]).astype(bf16)
    norm_out[...] = normed
    for part in range(3):
        qkv_out[:, part * 1024 : (part + 1) * 1024] = dot(normed, block_of(weights, part)).astype(bf16)
    attend(qkv_out, kmask[...], qmask[...], mixed_t, raised_out, lse_out)
    mixed = mixed_t[...].T
    mix_out[...] = mixed
    after_out[...] = after_space + dot(mixed, block_of(weights, 3))


def feed_forward(count, *refs):
    grad, refs = refs[:count], refs[count:]
    x, gain, bias, hidden_bias, out_bias, weights = refs[:6]
    norm_out, act_out, gpre_out, gat_out, branch_out, gain_out, bias_out, hb_out, ob_out = refs[6:15]
    block_out = refs[15:]
    first = pl.program_id(0) == 0
    clips = weights.shape[0]
    own = 1024 // clips
    groups = x.shape[0]
    width = x.shape[2]
    size = FF_CHUNK
    chunks = 4096 // size
    half = 1024 // size
    share = size * clips // 4096
    branch = stacked(grad, groups)
    branch_out[...] = branch.reshape(branch_out.shape)

    def down_of(chunk):
        if share:
            return weights[chunk * share : (chunk + 1) * share, 4 * own :, :].reshape(size, 1024)
        return None

    def hidden_of(chunk):
        block, column = chunk // half, chunk % half
        return weights[:, block * own : (block + 1) * own, column * size : (column + 1) * size].reshape(1024, size)

    part_at = lambda chunk: slice(chunk * size, (chunk + 1) * size)
    back_act = dot(branch, down_of(0), NT)
    after_time = x[...].reshape(groups * ROWS, width)
    hat, rate = standardize(after_time)
    normed = (hat * gain[2:3, :] + bias[2:3, :]).astype(bf16)
    norm_out[...] = normed.reshape(norm_out.shape)
    pre = dot(normed, hidden_of(0)) + hidden_bias[0:1, part_at(0)]
    result = None
    grad_norm = None
    bias_sums = []
    for chunk in range(chunks):
        at = part_at(chunk)
        u, grad_act = pre, back_act
        if chunk + 1 < chunks:
            pre = dot(normed, hidden_of(chunk + 1)) + hidden_bias[0:1, part_at(chunk + 1)]
            back_act = dot(branch, down_of(chunk + 1), NT)
        c0 = 0.7978845608028654
        square = u * u
        t = jnp.tanh(u * (c0 + (c0 * 0.044715) * square))
        half_plus = 0.5 + 0.5 * t
        act = (u * half_plus).astype(bf16)
        act_out[:, :, at] = act.reshape(groups, ROWS, size)
        slope = half_plus + (0.5 * u) * (1.0 - t * t) * (c0 + (3.0 * c0 * 0.044715) * square)
        gpre = (grad_act * slope).astype(bf16)
        gpre_out[:, :, at] = gpre.reshape(groups, ROWS, size)
        bias_sums.append(column_sum(gpre.astype(f32)))
        down = dot(act, down_of(chunk))
        result = down if result is None else result + down
        back = dot(gpre, hidden_of(chunk), NT)
        grad_norm = back if grad_norm is None else grad_norm + back
    block = (after_time + result + out_bias[0:1, :]).astype(bf16)
    unstack(block_out, block, groups)
    upstream = branch.astype(f32)
    gat = (upstream + norm_back(hat, rate, gain[2:3, :], grad_norm)).astype(bf16)
    gat_out[...] = gat.reshape(gat_out.shape)
    add_row(gain_out, column_sum(grad_norm * hat), first)
    add_row(bias_out, column_sum(grad_norm), first)
    add_row(ob_out, column_sum(upstream), first)
    add_row(hb_out, jnp.concatenate(bias_sums, axis=1), first)


def time_backward(count, *refs):
    x, refs = refs[:count], refs[count:]
    gat, raised, gain, weights, qkv, mix, lse, gqkv_out, gain_out, bias_out = refs[:10]
    gas_out = refs[10 : 10 + count]
    grad_t, mixed_t, query_t, grad_rows = refs[10 + count :]
    first = pl.program_id(0) == 0
    upstream = gat[...]
    mixed_t[...] = mix[...].T
    grad_rows[...] = dot(upstream, block_of(weights, 3), NT).astype(bf16)
    grad_t[...] = grad_rows[...].T
    attend_back(qkv, raised, lse, grad_rows, grad_t, mixed_t, gqkv_out, query_t)
    grad_norm = grad_into_norm(gqkv_out, weights)
    hat, rate = standardize(stacked(x).astype(f32))
    add_row(gain_out, column_sum(grad_norm * hat), first)
    add_row(bias_out, column_sum(grad_norm), first)
    total = upstream.astype(f32) + norm_back(hat, rate, gain[1:2, :], grad_norm)
    unstack(gas_out, total.astype(bf16))


def assemble(count, *refs):
    place, parts, out = refs[0], refs[1:-1], refs[-1]
    for micro in range(out.shape[0]):
        for step in range(count):
            out[micro, piece_at(place, step, count, ROWS // count), :] = parts[micro * count + step][...]


def rows_of(ref):
    value = ref[...]
    return value.reshape(-1, value.shape[-1])


def weight_kernel(pairs, micros, own, by_rows, has_small, *refs):
    out = refs[-1]
    offset = 0
    for pair in range(pairs):
        base = pair * 2 * micros
        total = None
        for index in range(micros):
            piece = dot(rows_of(refs[base + index]), rows_of(refs[base + micros + index]), TN)
            total = piece if total is None else total + piece
        total = total.astype(bf16)
        if by_rows:
            out[...] = total.reshape(out.shape)
            continue
        for block in range(total.shape[1] // 1024):
            for shard in range(out.shape[0]):
                out[shard, offset : offset + own, :] = total[
                    shard * own : (shard + 1) * own, block * 1024 : (block + 1) * 1024
                ]
            offset += own
    if has_small:
        out[:, offset:, :] = refs[pairs * 2 * micros][...]


def params():
    return pltpu.CompilerParams(vmem_limit_bytes=VMEM_LIMIT)


def ordered_call(kernel, behind, in_specs, **options):
    count = len(behind)

    def body(*refs):
        kernel(*refs[count:])

    aliases = options.pop("input_output_aliases", {})
    call = pl.pallas_call(
        body,
        in_specs=[pl.BlockSpec(memory_space=pl.ANY)] * count + in_specs,
        input_output_aliases={count + k: v for k, v in aliases.items()},
        compiler_params=params(),
        **options,
    )
    return lambda *operands: call(*behind, *operands)


def whole(shape):
    rank = len(shape)
    return pl.BlockSpec(shape, lambda i: (0,) * rank, pipeline_mode=pl.Buffered(1))


def total_spec(shape):
    rank = len(shape)
    return pl.BlockSpec(shape, lambda i: (0,) * rank)


def step_spec(shape):
    rank = len(shape)
    return pl.BlockSpec((None,) + shape, lambda i: (i,) + (0,) * rank)


def micro_spec(micro, shape):
    rank = len(shape)
    return pl.BlockSpec((None, None) + shape, lambda i: (micro, i) + (0,) * rank)


def shape_of(shape, kind):
    return jax.ShapeDtypeStruct(shape, kind)


def smem():
    return pl.BlockSpec(memory_space=pltpu.SMEM)


def call_space_forward(behind, micro, place, tok, hot, kmask, qmask, gain, bias, table, weights, count):
    _, frames, slots, width = tok.shape
    per = slots // count
    return ordered_call(
        space_forward,
        behind,
        grid=(frames,),
        in_specs=[smem(), micro_spec(micro, (slots, width)), step_spec(hot.shape[1:])]
        + [whole(a.shape) for a in (kmask, qmask, gain, bias, table, weights)],
        out_specs=[
            step_spec((slots, width)), step_spec((slots, 3 * width)), step_spec((slots, width)),
            step_spec((HEADS, slots)), step_spec(RAISED),
        ]
        + [step_spec((per, width))] * count,
        out_shape=[
            shape_of((frames, slots, width), bf16), shape_of((frames, slots, 3 * width), bf16),
            shape_of((frames, slots, width), bf16), shape_of((frames, HEADS, slots), f32),
            shape_of((frames,) + RAISED, bf16),
        ]
        + [shape_of((frames, per, width), bf16)] * count,
        scratch_shapes=[pltpu.VMEM((width, ROWS), bf16), pltpu.VMEM((ROWS, width), bf16)],
        name="space_forward",
    )(place, tok, hot, kmask, qmask, gain, bias, table, weights)


def back_scratch(width):
    return [
        pltpu.VMEM((width, ROWS), bf16), pltpu.VMEM((width, ROWS), bf16),
        pltpu.VMEM((width, ROWS), bf16), pltpu.VMEM((ROWS, width), bf16),
    ]


def call_space_backward(
    behind, micro, grads, place, tok, hot, raised, gain, table, weights, qkv, mix, lse, buffer
):
    micros, frames, slots, width = tok.shape
    count = len(grads)
    row = shape_of((1, width), f32)
    operands = list(grads) + [place, tok, hot, raised, gain, table, weights, qkv, mix, lse]
    specs = (
        [step_spec((slots // count, width))] * count
        + [smem(), micro_spec(micro, (slots, width)), step_spec(hot.shape[1:]), step_spec(RAISED)]
        + [whole(a.shape) for a in (gain, table, weights)]
        + [step_spec((slots, 3 * width)), step_spec((slots, width)), step_spec((HEADS, slots))]
    )
    before = len(operands)
    kernel = functools.partial(space_backward, count)
    aliases = {}
    if buffer is not None:
        aliases = {before: 2}
        operands.append(buffer)
        specs.append(pl.BlockSpec(memory_space=pl.ANY))
        kernel = lambda *refs: space_backward(count, *refs[:before], *refs[before + 1 :])
    return ordered_call(
        kernel,
        behind,
        grid=(frames,),
        in_specs=specs,
        out_specs=[
            step_spec((slots, 3 * width)), step_spec((slots, width)), micro_spec(micro, (slots, width)),
            total_spec((1, width)), total_spec((1, width)), total_spec((hot.shape[2], width)),
        ],
        out_shape=[
            shape_of((frames, slots, 3 * width), bf16), shape_of((frames, slots, width), bf16),
            shape_of((micros, frames, slots, width), f32), row, row, shape_of((hot.shape[2], width), f32),
        ],
        scratch_shapes=back_scratch(width),
        input_output_aliases=aliases,
        name="space_backward",
    )(*operands)


def group_spec(array, count):
    frames, _, width = array.shape
    return pl.BlockSpec((frames, ROWS // (frames * count), width), lambda i: (0, i, 0))


def call_time_forward(behind, x, kmask, qmask, gain, bias, weights):
    count = len(x)
    frames, slots, width = x[0].shape
    groups = slots * frames * count // ROWS
    return ordered_call(
        functools.partial(time_forward, count),
        behind,
        grid=(groups,),
        in_specs=[group_spec(a, count) for a in x] + [whole(a.shape) for a in (kmask, qmask, gain, bias, weights)],
        out_specs=[
            step_spec((ROWS, width)), step_spec((ROWS, 3 * width)), step_spec((ROWS, width)),
            step_spec((HEADS, ROWS)), step_spec(RAISED), step_spec((ROWS, width)),
        ],
        out_shape=[
            shape_of((groups, ROWS, width), bf16), shape_of((groups, ROWS, 3 * width), bf16),
            shape_of((groups, ROWS, width), bf16), shape_of((groups, HEADS, ROWS), f32),
            shape_of((groups,) + RAISED, bf16), shape_of((groups, ROWS, width), f32),
        ],
        scratch_shapes=[pltpu.VMEM((width, ROWS), bf16)],
        name="time_forward",
    )(*x, kmask, qmask, gain, bias, weights)


def call_feed_forward(behind, grad, x, gain, bias, hidden_bias, out_bias, weights):
    count = len(grad)
    groups, _, width = x.shape
    ff = hidden_bias.shape[1]
    each = FF_GROUPS if groups % FF_GROUPS == 0 else 1
    row = shape_of((1, width), f32)
    rows = lambda cols: shape_of((groups, ROWS, cols), bf16)
    spec = lambda cols: pl.BlockSpec((each, ROWS, cols), lambda i: (i, 0, 0))
    grad_spec = lambda a: pl.BlockSpec(
        (a.shape[0], each * ROWS // (a.shape[0] * count), width), lambda i: (0, i, 0)
    )
    return ordered_call(
        functools.partial(feed_forward, count),
        behind,
        grid=(groups // each,),
        in_specs=[grad_spec(a) for a in grad]
        + [spec(width)]
        + [whole(a.shape) for a in (gain, bias, hidden_bias, out_bias, weights)],
        out_specs=[
            spec(width), spec(ff), spec(ff), spec(width), spec(width),
            total_spec((1, width)), total_spec((1, width)), total_spec((1, ff)), total_spec((1, width)),
        ]
        + [grad_spec(a) for a in grad],
        out_shape=[rows(width), rows(ff), rows(ff), rows(width), rows(width), row, row, shape_of((1, ff), f32), row]
        + [shape_of(a.shape, bf16) for a in grad],
        name="feed_forward",
    )(*grad, x, gain, bias, hidden_bias, out_bias, weights)


def call_time_backward(behind, x, gat, raised, gain, weights, qkv, mix, lse):
    count = len(x)
    groups, _, width = gat.shape
    row = shape_of((1, width), f32)
    return ordered_call(
        functools.partial(time_backward, count),
        behind,
        grid=(groups,),
        in_specs=[group_spec(a, count) for a in x]
        + [step_spec((ROWS, width)), step_spec(RAISED)]
        + [whole(a.shape) for a in (gain, weights)]
        + [step_spec((ROWS, 3 * width)), step_spec((ROWS, width)), step_spec((HEADS, ROWS))],
        out_specs=[step_spec((ROWS, 3 * width)), total_spec((1, width)), total_spec((1, width))]
        + [group_spec(a, count) for a in x],
        out_shape=[shape_of((groups, ROWS, 3 * width), bf16), row, row] + [shape_of(a.shape, bf16) for a in x],
        scratch_shapes=back_scratch(width),
        name="time_backward",
    )(*x, gat, raised, gain, weights, qkv, mix, lse)


def call_assemble(place, parts):
    micros, count = len(parts), len(parts[0])
    frames, per, width = parts[0][0].shape
    flat = [p for pieces in parts for p in pieces]
    return ordered_call(
        functools.partial(assemble, count),
        [],
        grid=(frames,),
        in_specs=[smem()] + [step_spec((per, width))] * len(flat),
        out_specs=pl.BlockSpec((micros, None, per * count, width), lambda i: (0, i, 0, 0)),
        out_shape=shape_of((micros, frames, per * count, width), bf16),
        name="assemble",
    )(place, *flat)


def weight_grad(behind, pairs, clips, rows, name, small=None, down_at=None):
    own = 1024 // clips
    block = 256 if down_at is None else 512
    width = pairs[0][0][0].shape[-1]
    by_rows = down_at is not None

    def left_spec(a):
        rank = a.ndim
        return pl.BlockSpec(a.shape[:-1] + (block,), lambda i: (0,) * (rank - 1) + (i,))

    operands, specs = [], []
    cols = 0
    for lefts, rights in pairs:
        operands += list(lefts) + list(rights)
        specs += [left_spec(a) for a in lefts] + [whole(a.shape) for a in rights]
        cols += rights[0].shape[-1]
    shards = block // own
    if small is not None:
        operands.append(small)
        specs.append(pl.BlockSpec((shards,) + small.shape[1:], lambda i: (i, 0, 0)))
    if by_rows:
        per = width // clips
        out_spec = pl.BlockSpec((block // per, per, 1024), lambda i: (i, down_at // per, 0))
    else:
        out_rows = cols // 1024 * own + (0 if small is None else small.shape[1])
        out_spec = pl.BlockSpec((shards, out_rows, 1024), lambda i: (i, 0, 0))
    return ordered_call(
        functools.partial(weight_kernel, len(pairs), len(pairs[0][0]), own, by_rows, small is not None),
        behind,
        grid=(width // block,),
        in_specs=specs,
        out_specs=out_spec,
        out_shape=shape_of((clips, rows, 1024), bf16),
        name=name,
    )(*operands)


def column_kernel(starts, micros, *refs):
    out = refs[-1]
    step = pl.program_id(0)
    for pair, (start, end) in enumerate(starts):
        lefts = refs[pair * 2 * micros : pair * 2 * micros + micros]
        rights = refs[pair * 2 * micros + micros : (pair + 1) * 2 * micros]

        def fill():
            total = None
            for left, right in zip(lefts, rights):
                piece = dot(rows_of(left), rows_of(right), TN)
                total = piece if total is None else total + piece
            out[...] = total.astype(bf16).reshape(out.shape)

        if len(starts) == 1:
            fill()
        else:
            pl.when(jnp.logical_and(step >= start, step < end))(fill)


def weight_columns(behind, pairs, clips, rows, name, buffer=None):
    own = 1024 // clips
    block = 512
    operands, specs, starts = [], [], []
    step = 0
    for lefts, rights in pairs:
        count = rights[0].shape[-1] // block

        def right_spec(a, start=step, last=count - 1):
            rank = a.ndim
            return pl.BlockSpec(
                a.shape[:-1] + (block,), lambda i: (0,) * (rank - 1) + (jnp.clip(i - start, 0, last),)
            )

        operands += list(lefts) + list(rights)
        specs += [whole(a.shape) for a in lefts] + [right_spec(a) for a in rights]
        starts.append((step, step + count))
        step += count
    kernel = functools.partial(column_kernel, starts, len(pairs[0][0]))
    aliases = {}
    if buffer is not None:
        before = len(operands)
        aliases = {before: 0}
        operands.append(buffer)
        specs.append(pl.BlockSpec(memory_space=pl.ANY))
        inner = kernel
        kernel = lambda *refs: inner(*refs[:before], *refs[before + 1 :])
    return ordered_call(
        kernel,
        behind,
        grid=(step,),
        in_specs=specs,
        out_specs=pl.BlockSpec((clips, own, block), lambda i: (0, i // 2, i % 2)),
        out_shape=shape_of((clips, rows, 1024), bf16),
        input_output_aliases=aliases,
        name=name,
    )(*operands)


def one_hot(index, count, kind=bf16):
    return (index[..., None] == jnp.arange(count)).astype(kind)


def space_masks(labels):
    keys = one_hot(labels, 128)
    queries = jnp.where(labels[None, :] == jnp.arange(128)[:, None], 0.0, MASKED)
    queries = jnp.where(jnp.arange(128)[:, None] < 8, queries, 0.0).astype(bf16)
    return keys, queries


def time_masks(frames, count, me):
    per = ROWS // frames
    row = jnp.arange(ROWS)
    held = frames // count
    frame = jnp.mod(me - row // (held * per), count) * held + row // per % held
    place = row % per
    lane = jnp.arange(128)
    keys = ((lane[None, :] == place[:, None]) | (lane[None, :] == per + frame[:, None])).astype(bf16)
    other = (lane[:, None] < per) & (lane[:, None] != place[None, :])
    later = (lane[:, None] >= per) & (lane[:, None] < per + frames) & (lane[:, None] - per > frame[None, :])
    queries = jnp.where(other | later, MASKED, 0.0).astype(bf16)
    return keys, queries


def action_rows(labels, owners, actions):
    clip_of = jnp.sum(jnp.where(labels[:, None] == jnp.arange(owners.shape[0]), owners[None, :], 0), axis=1)
    hit = clip_of[:, None] == jnp.arange(actions.shape[0])
    chosen = jnp.sum(jnp.where(hit[:, :, None], actions[None], 0), axis=1)
    return jnp.transpose(chosen)


def exchange(values):
    return lax.all_to_all(values, "tm", 0, 0, tiled=True)


def gather(shards):
    own = shards[0].shape[0]
    parts = []
    for shard in shards:
        rows, cols = shard.shape
        parts += [shard[:, at : at + 1024] for at in range(0, cols, 1024)]
    return lax.all_gather(jnp.concatenate(parts, axis=0), "clip", axis=0, tiled=False)


def reduce_clip(total):
    return lax.psum_scatter(total, "clip", scatter_dimension=0, tiled=False)


def shift(values, step):
    count = lax.axis_size("tm")
    return lax.ppermute(values, "tm", [(k, (k + step) % count) for k in range(count)])


def sum_half(part):
    count = lax.axis_size("tm")
    rows = part.shape[0] // count
    me = lax.axis_index("tm")
    piece = lambda step: lax.dynamic_slice_in_dim(part, lax.rem(me + step, count) * rows, rows, axis=0)
    total = piece(0).astype(f32)
    for received in [shift(piece(step), step) for step in range(1, count)]:
        total = total + received.astype(f32)
    return total.astype(bf16)


def share(mine):
    return [mine] + [shift(mine, step) for step in range(1, lax.axis_size("tm"))]


def joined(held):
    count = len(held)
    rows, width = held[0].shape
    me = lax.axis_index("tm")
    values = jnp.zeros((count * rows, width), held[0].dtype)
    for step, piece in enumerate(held):
        values = lax.dynamic_update_slice_in_dim(values, piece, lax.rem(me + count - step, count) * rows, axis=0)
    return values


def mark(values):
    return values.reshape(-1, values.shape[-1])[:8, :128]


def together(*lists):
    flat = lax.optimization_barrier([a for arrays in lists for a in arrays])
    out = []
    for arrays in lists:
        out.append(list(flat[: len(arrays)]))
        flat = flat[len(arrays) :]
    return out


def columns(rows, own, first, count):
    return jnp.concatenate([rows[(first + c) * own : (first + c + 1) * own] for c in range(count)], axis=1).astype(f32)


def local(
    tokens, segments, assignment, actions, norm_gain, norm_bias,
    space_in, space_out, time_in, time_out, hidden, hidden_bias, down, out_bias,
    action_table, out_grad,
):
    micros, frames_here, slots, width = tokens.shape
    pieces = lax.axis_size("tm")
    clips = lax.axis_size("clip")
    frames = frames_here * pieces
    per = slots // pieces
    own = norm_gain.shape[1]
    nact = action_table.shape[0]
    micro = range(micros)
    hb_rows = hidden_bias.shape[0] // own
    small_rows = 6 + nact + hb_rows + 1

    small = jnp.concatenate(
        [norm_gain, norm_bias, action_table, hidden_bias.reshape(-1, own), out_bias.reshape(-1, own)], axis=0
    )
    small_all = lax.all_gather(small, "clip", axis=0, tiled=False)
    w_space = gather([space_in, space_out])
    w_time = gather([time_in, time_out])
    w_ff = gather([hidden, down])

    rows_by = lambda start, count: jnp.transpose(small_all[:, start : start + count], (1, 0, 2)).reshape(count, width)
    gain = rows_by(0, 3).astype(f32)
    bias = rows_by(3, 3).astype(f32)
    table = jnp.pad(rows_by(6, nact), ((0, 128 - nact), (0, 0)))
    hb_all = small_all[:, 6 + nact : 6 + nact + hb_rows].reshape(1, -1).astype(f32)
    ob_all = small_all[:, 6 + nact + hb_rows :].reshape(1, -1).astype(f32)

    me = lax.axis_index("tm").astype(jnp.int32)
    place = me.reshape(1)
    tmasks = time_masks(frames, pieces, me)
    hots = [one_hot(action_rows(segments[m], assignment[m], actions[m]), 128) for m in micro]
    smasks = [space_masks(segments[m]) for m in micro]

    pick = lambda parts, index: [parts[m][index] for m in micro]
    outward = lambda parts: [parts[0]] + [
        lax.ppermute(parts[d], "tm", [(k, (k + d) % pieces) for k in range(pieces)]) for d in range(1, pieces)
    ]
    inward = lambda parts: [parts[0]] + [
        lax.ppermute(parts[d], "tm", [(k, (k - d) % pieces) for k in range(pieces)]) for d in range(1, pieces)
    ]
    marks = lambda parts: [mark(a) for a in parts[1:]]
    rounded = lambda values, d: lax.dynamic_slice_in_dim(values, (me + d) % pieces * per, per, axis=1).astype(bf16)
    sent = [[rounded(out_grad[m], d) for d in range(pieces)] for m in micro]

    branch = [outward(sent[0])]
    forward, after, middle, ahead, pieces_out, back, gas, last = [], [], [], [], [], [], [], []
    behind = []
    for m in micro:
        forward.append(
            call_space_forward(behind, m, place, tokens, hots[m], *smasks[m], gain, bias, table, w_space, pieces)
        )
        after.append(outward(forward[m][5:]))
        behind = [forward[m][3]] + marks(branch[0])
    for m in micro:
        middle.append(list(call_time_forward(behind, after[m], *tmasks, gain, bias, w_time)))
        behind = [middle[m][3]]
    for m in micro[1:]:
        late, (middle[-1][5],) = together(sent[m], [middle[-1][5]])
        branch.append(outward(late))
    for m in micro:
        ahead.append(call_feed_forward(behind, branch[m], middle[m][5], gain, bias, hb_all, ob_all, w_ff))
        pieces_out.append(inward(ahead[m][9:]))
        behind = [ahead[m][5]]
    behind += marks(pieces_out[0])
    ff_grad = weight_grad(behind, [(pick(ahead, 1), pick(ahead, 4))], clips, 8 * own, "down_grad", down_at=4 * own)
    ff_grad = weight_columns([], [(pick(ahead, 0), pick(ahead, 2))], clips, 8 * own, "hidden_grad", buffer=ff_grad)
    (ff_grad,), pieces_out[-1] = together([ff_grad], pieces_out[-1])
    ff_part = reduce_clip(ff_grad)
    behind = [ff_grad]
    for m in micro:
        back.append(
            call_time_backward(
                behind, after[m], ahead[m][3], middle[m][4], gain, w_time, middle[m][1], middle[m][2], middle[m][3]
            )
        )
        gas.append(inward(back[m][3:]))
        behind = [back[m][1]]
    time_grad = weight_columns(
        behind, [(pick(middle, 0), pick(back, 0)), (pick(middle, 2), pick(ahead, 3))], clips, 4 * own, "time_grad"
    )
    (time_grad,), gas[0] = together([time_grad], gas[0])
    time_part = reduce_clip(time_grad)
    behind = [time_grad]
    grad_buffer = None
    for m in micro:
        last.append(
            list(
                call_space_backward(
                    behind, m, gas[m], place, tokens, hots[m], forward[m][4], gain, table, w_space,
                    forward[m][1], forward[m][2], forward[m][3], grad_buffer,
                )
            )
        )
        grad_buffer = last[m][2]
        behind = []
        if m == 0:
            (ff_part,), (last[m][3],), gas[-1] = together([ff_part], [last[m][3]], gas[-1])
            ff_half = sum_half(ff_part)
            behind = [mark(ff_part)]

    total = lambda values: functools.reduce(jnp.add, values)
    gain_grad = jnp.concatenate([total(pick(last, 3)), total(pick(back, 1)), total(pick(ahead, 5))])
    bias_grad = jnp.concatenate([total(pick(last, 4)), total(pick(back, 2)), total(pick(ahead, 6))])
    table_grad = total(pick(last, 5))[:nact]
    hb_grad = total(pick(ahead, 7))
    ob_grad = total(pick(ahead, 8))
    split = lambda a: jnp.transpose(a.reshape(a.shape[0], clips, own), (1, 0, 2))
    small_grads = jnp.concatenate(
        [
            split(gain_grad), split(bias_grad), split(table_grad),
            hb_grad.reshape(clips, hb_rows, own), ob_grad.reshape(clips, 1, own),
        ],
        axis=1,
    ).astype(bf16).reshape(clips, -1)
    extra = 8 * pieces - 4 * own % (8 * pieces)
    small_grads = jnp.pad(small_grads, ((0, 0), (0, extra * 1024 - small_grads.shape[1]))).reshape(clips, extra, 1024)
    space_grad = weight_grad(
        [mark(ff_half)], [(pick(forward, 0), pick(last, 0)), (pick(forward, 2), pick(last, 1))],
        clips, 4 * own + extra, "space_grad", small=small_grads,
    )

    ff_shared = share(ff_half)
    (space_grad,), (time_part,), ff_shared[1::2] = together([space_grad], [time_part], ff_shared[1::2])
    space_part = reduce_clip(space_grad)
    ff_sum = joined(ff_shared)
    time_sum = joined(share(sum_half(time_part)))
    early = (
        call_assemble(place, pieces_out),
        columns(time_sum, own, 0, 3),
        columns(time_sum, own, 3, 1),
        columns(ff_sum, own, 0, 4),
        ff_sum[4 * own :].astype(f32),
    )
    space_part, *early = lax.optimization_barrier((space_part,) + early)
    space_sum = joined(share(sum_half(space_part)))
    mine = space_sum[4 * own :].reshape(-1)[: small_rows * own].reshape(small_rows, own).astype(f32)
    return (
        early[0],
        grad_buffer,
        mine[0:3],
        mine[3:6],
        columns(space_sum, own, 0, 3),
        columns(space_sum, own, 3, 1),
        early[1],
        early[2],
        early[3],
        mine[6 + nact : 6 + nact + hb_rows].reshape(-1),
        early[4],
        mine[6 + nact + hb_rows :].reshape(-1),
        mine[6 : 6 + nact],
    )


def solution(mesh):
    rows = P("clip", None)
    cols = P(None, "clip")
    line = P("clip")
    wide = P(None, "tm", "clip", None)
    return jax.shard_map(
        local,
        mesh=mesh,
        in_specs=(
            wide, cols, cols, P(None, None, "tm"), cols, cols,
            rows, rows, rows, rows, rows, line, rows, line, cols, wide,
        ),
        out_specs=(wide, wide, cols, cols, rows, rows, rows, rows, rows, line, rows, line, cols),
        check_vma=False,
    )
```

```python
import functools

import jax
import jax.numpy as jnp
from jax import lax
from jax.experimental import pallas as pl
from jax.experimental.pallas import tpu as pltpu
from jax.sharding import PartitionSpec as P

HEADS = 16
HEAD = 64
EPS = 1e-05
MASKED = -1e30
ROWS = 256
RAISED = (HEADS // 2, ROWS, 2 * ROWS)
FF_CHUNK = 1024
FF_GROUPS = 1
VMEM_LIMIT = 62 * 1024 * 1024

bf16 = jnp.bfloat16
f32 = jnp.float32

NN = (((1,), (0,)), ((), ()))
NT = (((1,), (1,)), ((), ()))
TN = (((0,), (0,)), ((), ()))


def dot(left, right, form=NN):
    return lax.dot_general(left, right, form, preferred_element_type=f32)


def standardize(values):
    centered = values - jnp.mean(values, axis=-1, keepdims=True)
    rate = lax.rsqrt(jnp.mean(centered * centered, axis=-1, keepdims=True) + EPS)
    return centered * rate, rate


def norm_back(hat, rate, gain, grad):
    scaled = grad * gain
    return rate * (
        scaled
        - jnp.mean(scaled, axis=-1, keepdims=True)
        - hat * jnp.mean(scaled * hat, axis=-1, keepdims=True)
    )


def add_row(ref, row, first):
    @pl.when(first)
    def _():
        ref[...] = row

    @pl.when(jnp.logical_not(first))
    def _():
        ref[...] += row


def column_sum(values):
    return jnp.sum(values, axis=0, keepdims=True)


def pair_slices(pair):
    lane = pair * 128
    return slice(lane, lane + 128), slice(1024 + lane, 1024 + lane + 128), slice(2048 + lane, 2048 + lane + 128)


def attend(qkv_ref, key_mask, query_mask, mixed_t, raised_ref, rate_ref):
    blank = jnp.zeros((HEAD, ROWS), bf16)
    scale = jnp.asarray(HEAD**-0.5, bf16)

    def scores_of(pair):
        q_at, k_at, v_at = pair_slices(pair)
        q_t = (qkv_ref[:, q_at] * scale).T
        keys = jnp.concatenate([qkv_ref[:, k_at], key_mask], axis=1)
        first = jnp.concatenate([q_t[:HEAD], blank, query_mask], axis=0)
        second = jnp.concatenate([blank, q_t[HEAD:], query_mask], axis=0)
        return dot(keys, jnp.concatenate([first, second], axis=1))

    def finish(pair, scores):
        v_t = qkv_ref[:, pair_slices(pair)[2]].T
        top = jnp.max(scores, axis=0, keepdims=True)
        raised = jnp.exp(scores - top)
        total = jnp.sum(raised, axis=0, keepdims=True)
        weights = raised.astype(bf16)
        rate = 1.0 / total
        raised_ref[pair] = weights
        for part in range(2):
            head = pair * 2 + part
            at = slice(part * ROWS, (part + 1) * ROWS)
            mixed = dot(v_t[part * HEAD : (part + 1) * HEAD], weights[:, at])
            mixed_t[head * HEAD : (head + 1) * HEAD, :] = (mixed * rate[:, at]).astype(bf16)
            rate_ref[head : head + 1, :] = rate[:, at]

    queue = [scores_of(0), scores_of(1)]
    for pair in range(HEADS // 2):
        if pair + 2 < HEADS // 2:
            queue.append(scores_of(pair + 2))
        finish(pair, queue.pop(0))


def attend_back(qkv_ref, raised_ref, rate_ref, grad_ref, grad_t, mixed_t, out_ref, query_t):
    blank = jnp.zeros((HEAD, ROWS), bf16)
    scale = jnp.asarray(HEAD**-0.5, bf16)
    low_half = lax.broadcasted_iota(jnp.int32, (ROWS, 128), 1) < HEAD
    zero = jnp.zeros((ROWS, 128), bf16)

    def both(top, bottom):
        first = jnp.concatenate([top, blank], axis=0)
        second = jnp.concatenate([blank, bottom], axis=0)
        return jnp.concatenate([first, second], axis=1)

    def halves(values):
        return jnp.concatenate([jnp.where(low_half, values, zero), jnp.where(low_half, zero, values)], axis=0)

    def start(pair):
        q_at, _, v_at = pair_slices(pair)
        pair_t = grad_t[q_at, :]
        return dot(qkv_ref[:, v_at], both(pair_t[:HEAD], pair_t[HEAD:]))

    def finish(pair, grad_probs):
        q_at, k_at, v_at = pair_slices(pair)
        head = pair * 2
        rate = jnp.concatenate([rate_ref[head : head + 1, :], rate_ref[head + 1 : head + 2, :]], axis=1)
        product = grad_t[q_at, :].astype(f32) * mixed_t[q_at, :].astype(f32)
        along = jnp.concatenate([column_sum(product[:HEAD]), column_sum(product[HEAD:])], axis=1)
        probs = raised_ref[pair].astype(f32) * rate
        grad_scores = (probs * (grad_probs - along)).astype(bf16)
        out_ref[:, v_at] = dot(probs.astype(bf16), halves(grad_ref[:, q_at])).astype(bf16)
        out_ref[:, k_at] = dot(grad_scores, halves(qkv_ref[:, q_at] * scale)).astype(bf16)
        k_t = (qkv_ref[:, k_at] * scale).T
        for part in range(2):
            at = slice((head + part) * HEAD, (head + part + 1) * HEAD)
            columns_at = slice(part * ROWS, (part + 1) * ROWS)
            query_t[at, :] = dot(k_t[part * HEAD : (part + 1) * HEAD], grad_scores[:, columns_at]).astype(bf16)

    ahead = start(0)
    for pair in range(HEADS // 2):
        held = ahead
        if pair + 1 < HEADS // 2:
            ahead = start(pair + 1)
        finish(pair, held)
    for quarter in range(4):
        at = slice(quarter * 256, (quarter + 1) * 256)
        out_ref[:, at] = query_t[at, :].T


def block_of(weights, index):
    own = 1024 // weights.shape[0]
    return weights[:, index * own : (index + 1) * own, :].reshape(1024, 1024)


def piece_at(place, step, count, rows):
    return pl.ds(pl.multiple_of(lax.rem(place[0] + step, count) * rows, rows), rows)


def stacked(refs, groups=1):
    per = refs[0].shape[1] // groups
    width = refs[0].shape[-1]
    parts = [ref[:, g * per : (g + 1) * per, :].reshape(-1, width) for g in range(groups) for ref in refs]
    return parts[0] if len(parts) == 1 else jnp.concatenate(parts, axis=0)


def unstack(refs, values, groups=1):
    per = refs[0].shape[1] // groups
    rows = values.shape[0] // (len(refs) * groups)
    for g in range(groups):
        for index, ref in enumerate(refs):
            at = (g * len(refs) + index) * rows
            ref[:, g * per : (g + 1) * per, :] = values[at : at + rows].reshape(ref.shape[0], per, ref.shape[2])


def space_forward(
    place, tok, hot, kmask, qmask, gain, bias, table, weights,
    norm_out, qkv_out, mix_out, lse_out, raised_out, *rest,
):
    after_out, (mixed_t, after) = rest[:-2], rest[-2:]
    embedded = tok[...].astype(f32) + dot(hot[...], table[...])
    hat, _ = standardize(embedded)
    normed = (hat * gain[0:1, :] + bias[0:1, :]).astype(bf16)
    norm_out[...] = normed
    for part in range(3):
        qkv_out[:, part * 1024 : (part + 1) * 1024] = dot(normed, block_of(weights, part)).astype(bf16)
    attend(qkv_out, kmask[...], qmask[...], mixed_t, raised_out, lse_out)
    mixed = mixed_t[...].T
    mix_out[...] = mixed
    after[...] = (embedded + dot(mixed, block_of(weights, 3))).astype(bf16)
    count = len(after_out)
    for step in range(count):
        after_out[step][...] = after[piece_at(place, step, count, ROWS // count), :]


def grad_into_norm(gqkv, weights):
    total = None
    for part in range(3):
        piece = dot(gqkv[:, part * 1024 : (part + 1) * 1024], block_of(weights, part), NT)
        total = piece if total is None else total + piece
    return total


def space_backward(count, *refs):
    grads, refs = refs[:count], refs[count:]
    (
        place, tok, hot, raised, gain, table, weights, qkv, mix, lse,
        gqkv_out, gas_out, tok_out, gain_out, bias_out, table_out, grad_t, mixed_t, query_t, grad_rows,
    ) = refs
    first = pl.program_id(0) == 0
    for step in range(count):
        gas_out[piece_at(place, step, count, ROWS // count), :] = grads[step][...]
    upstream = gas_out[...]
    mixed_t[...] = mix[...].T
    grad_rows[...] = dot(upstream, block_of(weights, 3), NT).astype(bf16)
    grad_t[...] = grad_rows[...].T
    attend_back(qkv, raised, lse, grad_rows, grad_t, mixed_t, gqkv_out, query_t)
    grad_norm = grad_into_norm(gqkv_out, weights)
    embedded = tok[...].astype(f32) + dot(hot[...], table[...])
    hat, rate = standardize(embedded)
    add_row(gain_out, column_sum(grad_norm * hat), first)
    add_row(bias_out, column_sum(grad_norm), first)
    total = upstream.astype(f32) + norm_back(hat, rate, gain[0:1, :], grad_norm)
    tok_out[...] = total
    add_row(table_out, dot(hot[...], total.astype(bf16), TN), first)


def time_forward(count, *refs):
    x, refs = refs[:count], refs[count:]
    kmask, qmask, gain, bias, weights, norm_out, qkv_out, mix_out, lse_out, raised_out, after_out, mixed_t = refs
    after_space = stacked(x).astype(f32)
    hat, _ = standardize(after_space)
    normed = (hat * gain[1:2, :] + bias[1:2, :]).astype(bf16)
    norm_out[...] = normed
    for part in range(3):
        qkv_out[:, part * 1024 : (part + 1) * 1024] = dot(normed, block_of(weights, part)).astype(bf16)
    attend(qkv_out, kmask[...], qmask[...], mixed_t, raised_out, lse_out)
    mixed = mixed_t[...].T
    mix_out[...] = mixed
    after_out[...] = after_space + dot(mixed, block_of(weights, 3))


def feed_forward(count, *refs):
    grad, refs = refs[:count], refs[count:]
    x, gain, bias, hidden_bias, out_bias, weights = refs[:6]
    norm_out, act_out, gpre_out, gat_out, branch_out, gain_out, bias_out, hb_out, ob_out = refs[6:15]
    block_out = refs[15:]
    first = pl.program_id(0) == 0
    clips = weights.shape[0]
    own = 1024 // clips
    groups = x.shape[0]
    width = x.shape[2]
    size = FF_CHUNK
    chunks = 4096 // size
    half = 1024 // size
    share = size * clips // 4096
    branch = stacked(grad, groups)
    branch_out[...] = branch.reshape(branch_out.shape)

    def down_of(chunk):
        if share:
            return weights[chunk * share : (chunk + 1) * share, 4 * own :, :].reshape(size, 1024)
        return None

    def hidden_of(chunk):
        block, column = chunk // half, chunk % half
        return weights[:, block * own : (block + 1) * own, column * size : (column + 1) * size].reshape(1024, size)

    part_at = lambda chunk: slice(chunk * size, (chunk + 1) * size)
    back_act = dot(branch, down_of(0), NT)
    after_time = x[...].reshape(groups * ROWS, width)
    hat, rate = standardize(after_time)
    normed = (hat * gain[2:3, :] + bias[2:3, :]).astype(bf16)
    norm_out[...] = normed.reshape(norm_out.shape)
    pre = dot(normed, hidden_of(0)) + hidden_bias[0:1, part_at(0)]
    result = None
    grad_norm = None
    bias_sums = []
    for chunk in range(chunks):
        at = part_at(chunk)
        u, grad_act = pre, back_act
        if chunk + 1 < chunks:
            pre = dot(normed, hidden_of(chunk + 1)) + hidden_bias[0:1, part_at(chunk + 1)]
            back_act = dot(branch, down_of(chunk + 1), NT)
        c0 = 0.7978845608028654
        square = u * u
        t = jnp.tanh(u * (c0 + (c0 * 0.044715) * square))
        half_plus = 0.5 + 0.5 * t
        act = (u * half_plus).astype(bf16)
        act_out[:, :, at] = act.reshape(groups, ROWS, size)
        slope = half_plus + (0.5 * u) * (1.0 - t * t) * (c0 + (3.0 * c0 * 0.044715) * square)
        gpre = (grad_act * slope).astype(bf16)
        gpre_out[:, :, at] = gpre.reshape(groups, ROWS, size)
        bias_sums.append(column_sum(gpre.astype(f32)))
        down = dot(act, down_of(chunk))
        result = down if result is None else result + down
        back = dot(gpre, hidden_of(chunk), NT)
        grad_norm = back if grad_norm is None else grad_norm + back
    block = (after_time + result + out_bias[0:1, :]).astype(bf16)
    unstack(block_out, block, groups)
    upstream = branch.astype(f32)
    gat = (upstream + norm_back(hat, rate, gain[2:3, :], grad_norm)).astype(bf16)
    gat_out[...] = gat.reshape(gat_out.shape)
    add_row(gain_out, column_sum(grad_norm * hat), first)
    add_row(bias_out, column_sum(grad_norm), first)
    add_row(ob_out, column_sum(upstream), first)
    add_row(hb_out, jnp.concatenate(bias_sums, axis=1), first)


def time_backward(count, *refs):
    x, refs = refs[:count], refs[count:]
    gat, raised, gain, weights, qkv, mix, lse, gqkv_out, gain_out, bias_out = refs[:10]
    gas_out = refs[10 : 10 + count]
    grad_t, mixed_t, query_t, grad_rows = refs[10 + count :]
    first = pl.program_id(0) == 0
    upstream = gat[...]
    mixed_t[...] = mix[...].T
    grad_rows[...] = dot(upstream, block_of(weights, 3), NT).astype(bf16)
    grad_t[...] = grad_rows[...].T
    attend_back(qkv, raised, lse, grad_rows, grad_t, mixed_t, gqkv_out, query_t)
    grad_norm = grad_into_norm(gqkv_out, weights)
    hat, rate = standardize(stacked(x).astype(f32))
    add_row(gain_out, column_sum(grad_norm * hat), first)
    add_row(bias_out, column_sum(grad_norm), first)
    total = upstream.astype(f32) + norm_back(hat, rate, gain[1:2, :], grad_norm)
    unstack(gas_out, total.astype(bf16))


def assemble(count, *refs):
    place, parts, out = refs[0], refs[1:-1], refs[-1]
    for micro in range(out.shape[0]):
        for step in range(count):
            out[micro, piece_at(place, step, count, ROWS // count), :] = parts[micro * count + step][...]


def rows_of(ref):
    value = ref[...]
    return value.reshape(-1, value.shape[-1])


def weight_kernel(pairs, micros, own, by_rows, has_small, *refs):
    out = refs[-1]
    offset = 0
    for pair in range(pairs):
        base = pair * 2 * micros
        total = None
        for index in range(micros):
            piece = dot(rows_of(refs[base + index]), rows_of(refs[base + micros + index]), TN)
            total = piece if total is None else total + piece
        total = total.astype(bf16)
        if by_rows:
            out[...] = total.reshape(out.shape)
            continue
        for block in range(total.shape[1] // 1024):
            for shard in range(out.shape[0]):
                out[shard, offset : offset + own, :] = total[
                    shard * own : (shard + 1) * own, block * 1024 : (block + 1) * 1024
                ]
            offset += own
    if has_small:
        out[:, offset:, :] = refs[pairs * 2 * micros][...]


def params():
    return pltpu.CompilerParams(vmem_limit_bytes=VMEM_LIMIT)


def ordered_call(kernel, behind, in_specs, **options):
    count = len(behind)

    def body(*refs):
        kernel(*refs[count:])

    aliases = options.pop("input_output_aliases", {})
    call = pl.pallas_call(
        body,
        in_specs=[pl.BlockSpec(memory_space=pl.ANY)] * count + in_specs,
        input_output_aliases={count + k: v for k, v in aliases.items()},
        compiler_params=params(),
        **options,
    )
    return lambda *operands: call(*behind, *operands)


def whole(shape):
    rank = len(shape)
    return pl.BlockSpec(shape, lambda i: (0,) * rank, pipeline_mode=pl.Buffered(1))


def total_spec(shape):
    rank = len(shape)
    return pl.BlockSpec(shape, lambda i: (0,) * rank)


def step_spec(shape):
    rank = len(shape)
    return pl.BlockSpec((None,) + shape, lambda i: (i,) + (0,) * rank)


def micro_spec(micro, shape):
    rank = len(shape)
    return pl.BlockSpec((None, None) + shape, lambda i: (micro, i) + (0,) * rank)


def shape_of(shape, kind):
    return jax.ShapeDtypeStruct(shape, kind)


def smem():
    return pl.BlockSpec(memory_space=pltpu.SMEM)


def call_space_forward(behind, micro, place, tok, hot, kmask, qmask, gain, bias, table, weights, count):
    _, frames, slots, width = tok.shape
    per = slots // count
    return ordered_call(
        space_forward,
        behind,
        grid=(frames,),
        in_specs=[smem(), micro_spec(micro, (slots, width)), step_spec(hot.shape[1:])]
        + [whole(a.shape) for a in (kmask, qmask, gain, bias, table, weights)],
        out_specs=[
            step_spec((slots, width)), step_spec((slots, 3 * width)), step_spec((slots, width)),
            step_spec((HEADS, slots)), step_spec(RAISED),
        ]
        + [step_spec((per, width))] * count,
        out_shape=[
            shape_of((frames, slots, width), bf16), shape_of((frames, slots, 3 * width), bf16),
            shape_of((frames, slots, width), bf16), shape_of((frames, HEADS, slots), f32),
            shape_of((frames,) + RAISED, bf16),
        ]
        + [shape_of((frames, per, width), bf16)] * count,
        scratch_shapes=[pltpu.VMEM((width, ROWS), bf16), pltpu.VMEM((ROWS, width), bf16)],
        name="space_forward",
    )(place, tok, hot, kmask, qmask, gain, bias, table, weights)


def back_scratch(width):
    return [
        pltpu.VMEM((width, ROWS), bf16), pltpu.VMEM((width, ROWS), bf16),
        pltpu.VMEM((width, ROWS), bf16), pltpu.VMEM((ROWS, width), bf16),
    ]


def call_space_backward(
    behind, micro, grads, place, tok, hot, raised, gain, table, weights, qkv, mix, lse, buffer
):
    micros, frames, slots, width = tok.shape
    count = len(grads)
    row = shape_of((1, width), f32)
    operands = list(grads) + [place, tok, hot, raised, gain, table, weights, qkv, mix, lse]
    specs = (
        [step_spec((slots // count, width))] * count
        + [smem(), micro_spec(micro, (slots, width)), step_spec(hot.shape[1:]), step_spec(RAISED)]
        + [whole(a.shape) for a in (gain, table, weights)]
        + [step_spec((slots, 3 * width)), step_spec((slots, width)), step_spec((HEADS, slots))]
    )
    before = len(operands)
    kernel = functools.partial(space_backward, count)
    aliases = {}
    if buffer is not None:
        aliases = {before: 2}
        operands.append(buffer)
        specs.append(pl.BlockSpec(memory_space=pl.ANY))
        kernel = lambda *refs: space_backward(count, *refs[:before], *refs[before + 1 :])
    return ordered_call(
        kernel,
        behind,
        grid=(frames,),
        in_specs=specs,
        out_specs=[
            step_spec((slots, 3 * width)), step_spec((slots, width)), micro_spec(micro, (slots, width)),
            total_spec((1, width)), total_spec((1, width)), total_spec((hot.shape[2], width)),
        ],
        out_shape=[
            shape_of((frames, slots, 3 * width), bf16), shape_of((frames, slots, width), bf16),
            shape_of((micros, frames, slots, width), f32), row, row, shape_of((hot.shape[2], width), f32),
        ],
        scratch_shapes=back_scratch(width),
        input_output_aliases=aliases,
        name="space_backward",
    )(*operands)


def group_spec(array, count):
    frames, _, width = array.shape
    return pl.BlockSpec((frames, ROWS // (frames * count), width), lambda i: (0, i, 0))


def call_time_forward(behind, x, kmask, qmask, gain, bias, weights):
    count = len(x)
    frames, slots, width = x[0].shape
    groups = slots * frames * count // ROWS
    return ordered_call(
        functools.partial(time_forward, count),
        behind,
        grid=(groups,),
        in_specs=[group_spec(a, count) for a in x] + [whole(a.shape) for a in (kmask, qmask, gain, bias, weights)],
        out_specs=[
            step_spec((ROWS, width)), step_spec((ROWS, 3 * width)), step_spec((ROWS, width)),
            step_spec((HEADS, ROWS)), step_spec(RAISED), step_spec((ROWS, width)),
        ],
        out_shape=[
            shape_of((groups, ROWS, width), bf16), shape_of((groups, ROWS, 3 * width), bf16),
            shape_of((groups, ROWS, width), bf16), shape_of((groups, HEADS, ROWS), f32),
            shape_of((groups,) + RAISED, bf16), shape_of((groups, ROWS, width), f32),
        ],
        scratch_shapes=[pltpu.VMEM((width, ROWS), bf16)],
        name="time_forward",
    )(*x, kmask, qmask, gain, bias, weights)


def call_feed_forward(behind, grad, x, gain, bias, hidden_bias, out_bias, weights):
    count = len(grad)
    groups, _, width = x.shape
    ff = hidden_bias.shape[1]
    each = FF_GROUPS if groups % FF_GROUPS == 0 else 1
    row = shape_of((1, width), f32)
    rows = lambda cols: shape_of((groups, ROWS, cols), bf16)
    spec = lambda cols: pl.BlockSpec((each, ROWS, cols), lambda i: (i, 0, 0))
    grad_spec = lambda a: pl.BlockSpec(
        (a.shape[0], each * ROWS // (a.shape[0] * count), width), lambda i: (0, i, 0)
    )
    return ordered_call(
        functools.partial(feed_forward, count),
        behind,
        grid=(groups // each,),
        in_specs=[grad_spec(a) for a in grad]
        + [spec(width)]
        + [whole(a.shape) for a in (gain, bias, hidden_bias, out_bias, weights)],
        out_specs=[
            spec(width), spec(ff), spec(ff), spec(width), spec(width),
            total_spec((1, width)), total_spec((1, width)), total_spec((1, ff)), total_spec((1, width)),
        ]
        + [grad_spec(a) for a in grad],
        out_shape=[rows(width), rows(ff), rows(ff), rows(width), rows(width), row, row, shape_of((1, ff), f32), row]
        + [shape_of(a.shape, bf16) for a in grad],
        name="feed_forward",
    )(*grad, x, gain, bias, hidden_bias, out_bias, weights)


def call_time_backward(behind, x, gat, raised, gain, weights, qkv, mix, lse):
    count = len(x)
    groups, _, width = gat.shape
    row = shape_of((1, width), f32)
    return ordered_call(
        functools.partial(time_backward, count),
        behind,
        grid=(groups,),
        in_specs=[group_spec(a, count) for a in x]
        + [step_spec((ROWS, width)), step_spec(RAISED)]
        + [whole(a.shape) for a in (gain, weights)]
        + [step_spec((ROWS, 3 * width)), step_spec((ROWS, width)), step_spec((HEADS, ROWS))],
        out_specs=[step_spec((ROWS, 3 * width)), total_spec((1, width)), total_spec((1, width))]
        + [group_spec(a, count) for a in x],
        out_shape=[shape_of((groups, ROWS, 3 * width), bf16), row, row] + [shape_of(a.shape, bf16) for a in x],
        scratch_shapes=back_scratch(width),
        name="time_backward",
    )(*x, gat, raised, gain, weights, qkv, mix, lse)


def call_assemble(place, parts):
    micros, count = len(parts), len(parts[0])
    frames, per, width = parts[0][0].shape
    flat = [p for pieces in parts for p in pieces]
    return ordered_call(
        functools.partial(assemble, count),
        [],
        grid=(frames,),
        in_specs=[smem()] + [step_spec((per, width))] * len(flat),
        out_specs=pl.BlockSpec((micros, None, per * count, width), lambda i: (0, i, 0, 0)),
        out_shape=shape_of((micros, frames, per * count, width), bf16),
        name="assemble",
    )(place, *flat)


def weight_grad(behind, pairs, clips, rows, name, small=None, down_at=None):
    own = 1024 // clips
    block = 256 if down_at is None else 512
    width = pairs[0][0][0].shape[-1]
    by_rows = down_at is not None

    def left_spec(a):
        rank = a.ndim
        return pl.BlockSpec(a.shape[:-1] + (block,), lambda i: (0,) * (rank - 1) + (i,))

    operands, specs = [], []
    cols = 0
    for lefts, rights in pairs:
        operands += list(lefts) + list(rights)
        specs += [left_spec(a) for a in lefts] + [whole(a.shape) for a in rights]
        cols += rights[0].shape[-1]
    shards = block // own
    if small is not None:
        operands.append(small)
        specs.append(pl.BlockSpec((shards,) + small.shape[1:], lambda i: (i, 0, 0)))
    if by_rows:
        per = width // clips
        out_spec = pl.BlockSpec((block // per, per, 1024), lambda i: (i, down_at // per, 0))
    else:
        out_rows = cols // 1024 * own + (0 if small is None else small.shape[1])
        out_spec = pl.BlockSpec((shards, out_rows, 1024), lambda i: (i, 0, 0))
    return ordered_call(
        functools.partial(weight_kernel, len(pairs), len(pairs[0][0]), own, by_rows, small is not None),
        behind,
        grid=(width // block,),
        in_specs=specs,
        out_specs=out_spec,
        out_shape=shape_of((clips, rows, 1024), bf16),
        name=name,
    )(*operands)


def column_kernel(starts, micros, *refs):
    out = refs[-1]
    step = pl.program_id(0)
    for pair, (start, end) in enumerate(starts):
        lefts = refs[pair * 2 * micros : pair * 2 * micros + micros]
        rights = refs[pair * 2 * micros + micros : (pair + 1) * 2 * micros]

        def fill():
            total = None
            for left, right in zip(lefts, rights):
                piece = dot(rows_of(left), rows_of(right), TN)
                total = piece if total is None else total + piece
            out[...] = total.astype(bf16).reshape(out.shape)

        if len(starts) == 1:
            fill()
        else:
            pl.when(jnp.logical_and(step >= start, step < end))(fill)


def weight_columns(behind, pairs, clips, rows, name, buffer=None):
    own = 1024 // clips
    block = 512
    operands, specs, starts = [], [], []
    step = 0
    for lefts, rights in pairs:
        count = rights[0].shape[-1] // block

        def right_spec(a, start=step, last=count - 1):
            rank = a.ndim
            return pl.BlockSpec(
                a.shape[:-1] + (block,), lambda i: (0,) * (rank - 1) + (jnp.clip(i - start, 0, last),)
            )

        operands += list(lefts) + list(rights)
        specs += [whole(a.shape) for a in lefts] + [right_spec(a) for a in rights]
        starts.append((step, step + count))
        step += count
    kernel = functools.partial(column_kernel, starts, len(pairs[0][0]))
    aliases = {}
    if buffer is not None:
        before = len(operands)
        aliases = {before: 0}
        operands.append(buffer)
        specs.append(pl.BlockSpec(memory_space=pl.ANY))
        inner = kernel
        kernel = lambda *refs: inner(*refs[:before], *refs[before + 1 :])
    return ordered_call(
        kernel,
        behind,
        grid=(step,),
        in_specs=specs,
        out_specs=pl.BlockSpec((clips, own, block), lambda i: (0, i // 2, i % 2)),
        out_shape=shape_of((clips, rows, 1024), bf16),
        input_output_aliases=aliases,
        name=name,
    )(*operands)


def one_hot(index, count, kind=bf16):
    return (index[..., None] == jnp.arange(count)).astype(kind)


def space_masks(labels):
    keys = one_hot(labels, 128)
    queries = jnp.where(labels[None, :] == jnp.arange(128)[:, None], 0.0, MASKED)
    queries = jnp.where(jnp.arange(128)[:, None] < 8, queries, 0.0).astype(bf16)
    return keys, queries


def time_masks(frames, count, me):
    per = ROWS // frames
    row = jnp.arange(ROWS)
    held = frames // count
    frame = jnp.mod(me - row // (held * per), count) * held + row // per % held
    place = row % per
    lane = jnp.arange(128)
    keys = ((lane[None, :] == place[:, None]) | (lane[None, :] == per + frame[:, None])).astype(bf16)
    other = (lane[:, None] < per) & (lane[:, None] != place[None, :])
    later = (lane[:, None] >= per) & (lane[:, None] < per + frames) & (lane[:, None] - per > frame[None, :])
    queries = jnp.where(other | later, MASKED, 0.0).astype(bf16)
    return keys, queries


def action_rows(labels, owners, actions):
    clip_of = jnp.sum(jnp.where(labels[:, None] == jnp.arange(owners.shape[0]), owners[None, :], 0), axis=1)
    hit = clip_of[:, None] == jnp.arange(actions.shape[0])
    chosen = jnp.sum(jnp.where(hit[:, :, None], actions[None], 0), axis=1)
    return jnp.transpose(chosen)


def exchange(values):
    return lax.all_to_all(values, "tm", 0, 0, tiled=True)


def gather(shards):
    own = shards[0].shape[0]
    parts = []
    for shard in shards:
        rows, cols = shard.shape
        parts += [shard[:, at : at + 1024] for at in range(0, cols, 1024)]
    return lax.all_gather(jnp.concatenate(parts, axis=0), "clip", axis=0, tiled=False)


def reduce_clip(total):
    return lax.psum_scatter(total, "clip", scatter_dimension=0, tiled=False)


def shift(values, step):
    count = lax.axis_size("tm")
    return lax.ppermute(values, "tm", [(k, (k + step) % count) for k in range(count)])


def sum_half(part):
    count = lax.axis_size("tm")
    rows = part.shape[0] // count
    me = lax.axis_index("tm")
    piece = lambda step: lax.dynamic_slice_in_dim(part, lax.rem(me + step, count) * rows, rows, axis=0)
    total = piece(0).astype(f32)
    for received in [shift(piece(step), step) for step in range(1, count)]:
        total = total + received.astype(f32)
    return total.astype(bf16)


def share(mine):
    return [mine] + [shift(mine, step) for step in range(1, lax.axis_size("tm"))]


def joined(held):
    count = len(held)
    rows, width = held[0].shape
    me = lax.axis_index("tm")
    values = jnp.zeros((count * rows, width), held[0].dtype)
    for step, piece in enumerate(held):
        values = lax.dynamic_update_slice_in_dim(values, piece, lax.rem(me + count - step, count) * rows, axis=0)
    return values


def together(*lists):
    flat = lax.optimization_barrier([a for arrays in lists for a in arrays])
    out = []
    for arrays in lists:
        out.append(list(flat[: len(arrays)]))
        flat = flat[len(arrays) :]
    return out


def columns(rows, own, first, count):
    return jnp.concatenate([rows[(first + c) * own : (first + c + 1) * own] for c in range(count)], axis=1).astype(f32)


def local(
    tokens, segments, assignment, actions, norm_gain, norm_bias,
    space_in, space_out, time_in, time_out, hidden, hidden_bias, down, out_bias,
    action_table, out_grad,
):
    micros, frames_here, slots, width = tokens.shape
    pieces = lax.axis_size("tm")
    clips = lax.axis_size("clip")
    frames = frames_here * pieces
    per = slots // pieces
    own = norm_gain.shape[1]
    nact = action_table.shape[0]
    micro = range(micros)
    hb_rows = hidden_bias.shape[0] // own
    small_rows = 6 + nact + hb_rows + 1

    small = jnp.concatenate(
        [norm_gain, norm_bias, action_table, hidden_bias.reshape(-1, own), out_bias.reshape(-1, own)], axis=0
    )
    small_all = lax.all_gather(small, "clip", axis=0, tiled=False)
    w_space = gather([space_in, space_out])
    w_time = gather([time_in, time_out])
    w_ff = gather([hidden, down])

    rows_by = lambda start, count: jnp.transpose(small_all[:, start : start + count], (1, 0, 2)).reshape(count, width)
    gain = rows_by(0, 3).astype(f32)
    bias = rows_by(3, 3).astype(f32)
    table = jnp.pad(rows_by(6, nact), ((0, 128 - nact), (0, 0)))
    hb_all = small_all[:, 6 + nact : 6 + nact + hb_rows].reshape(1, -1).astype(f32)
    ob_all = small_all[:, 6 + nact + hb_rows :].reshape(1, -1).astype(f32)

    me = lax.axis_index("tm").astype(jnp.int32)
    place = me.reshape(1)
    tmasks = time_masks(frames, pieces, me)
    hots = [one_hot(action_rows(segments[m], assignment[m], actions[m]), 128) for m in micro]
    smasks = [space_masks(segments[m]) for m in micro]

    pick = lambda parts, index: [parts[m][index] for m in micro]
    outward = lambda parts: [parts[0]] + [
        lax.ppermute(parts[d], "tm", [(k, (k + d) % pieces) for k in range(pieces)]) for d in range(1, pieces)
    ]
    inward = lambda parts: [parts[0]] + [
        lax.ppermute(parts[d], "tm", [(k, (k - d) % pieces) for k in range(pieces)]) for d in range(1, pieces)
    ]
    marks = lambda parts: parts[1:]
    rounded = lambda values, d: lax.dynamic_slice_in_dim(values, (me + d) % pieces * per, per, axis=1).astype(bf16)
    sent = [[rounded(out_grad[m], d) for d in range(pieces)] for m in micro]

    branch = [outward(sent[0])]
    forward, after, middle, ahead, pieces_out, back, gas, last = [], [], [], [], [], [], [], []
    behind = []
    for m in micro:
        forward.append(
            call_space_forward(behind, m, place, tokens, hots[m], *smasks[m], gain, bias, table, w_space, pieces)
        )
        after.append(outward(forward[m][5:]))
        behind = [forward[m][3]] + marks(branch[0])
    for m in micro:
        middle.append(list(call_time_forward(behind, after[m], *tmasks, gain, bias, w_time)))
        behind = [middle[m][3]]
    for m in micro[1:]:
        late, (middle[-1][5],) = together(sent[m], [middle[-1][5]])
        branch.append(outward(late))
    for m in micro:
        ahead.append(call_feed_forward(behind, branch[m], middle[m][5], gain, bias, hb_all, ob_all, w_ff))
        pieces_out.append(inward(ahead[m][9:]))
        behind = [ahead[m][5]]
    behind += marks(pieces_out[0])
    ff_grad = weight_grad(behind, [(pick(ahead, 1), pick(ahead, 4))], clips, 8 * own, "down_grad", down_at=4 * own)
    ff_grad = weight_columns([], [(pick(ahead, 0), pick(ahead, 2))], clips, 8 * own, "hidden_grad", buffer=ff_grad)
    (ff_grad,), pieces_out[-1] = together([ff_grad], pieces_out[-1])
    ff_part = reduce_clip(ff_grad)
    behind = [ff_grad]
    for m in micro:
        back.append(
            call_time_backward(
                behind, after[m], ahead[m][3], middle[m][4], gain, w_time, middle[m][1], middle[m][2], middle[m][3]
            )
        )
        gas.append(inward(back[m][3:]))
        behind = [back[m][1]]
    time_grad = weight_columns(
        behind, [(pick(middle, 0), pick(back, 0)), (pick(middle, 2), pick(ahead, 3))], clips, 4 * own, "time_grad"
    )
    (time_grad,), gas[0] = together([time_grad], gas[0])
    time_part = reduce_clip(time_grad)
    behind = [time_grad]
    grad_buffer = None
    for m in micro:
        last.append(
            list(
                call_space_backward(
                    behind, m, gas[m], place, tokens, hots[m], forward[m][4], gain, table, w_space,
                    forward[m][1], forward[m][2], forward[m][3], grad_buffer,
                )
            )
        )
        grad_buffer = last[m][2]
        behind = []
        if m == 0:
            (ff_part,), (last[m][3],), gas[-1] = together([ff_part], [last[m][3]], gas[-1])
            ff_half = sum_half(ff_part)
            behind = [ff_part]

    total = lambda values: functools.reduce(jnp.add, values)
    gain_grad = jnp.concatenate([total(pick(last, 3)), total(pick(back, 1)), total(pick(ahead, 5))])
    bias_grad = jnp.concatenate([total(pick(last, 4)), total(pick(back, 2)), total(pick(ahead, 6))])
    table_grad = total(pick(last, 5))[:nact]
    hb_grad = total(pick(ahead, 7))
    ob_grad = total(pick(ahead, 8))
    split = lambda a: jnp.transpose(a.reshape(a.shape[0], clips, own), (1, 0, 2))
    small_grads = jnp.concatenate(
        [
            split(gain_grad), split(bias_grad), split(table_grad),
            hb_grad.reshape(clips, hb_rows, own), ob_grad.reshape(clips, 1, own),
        ],
        axis=1,
    ).astype(bf16).reshape(clips, -1)
    extra = 8 * pieces - 4 * own % (8 * pieces)
    small_grads = jnp.pad(small_grads, ((0, 0), (0, extra * 1024 - small_grads.shape[1]))).reshape(clips, extra, 1024)
    space_grad = weight_grad(
        [ff_half], [(pick(forward, 0), pick(last, 0)), (pick(forward, 2), pick(last, 1))],
        clips, 4 * own + extra, "space_grad", small=small_grads,
    )

    ff_shared = share(ff_half)
    (space_grad,), (time_part,), ff_shared[1::2] = together([space_grad], [time_part], ff_shared[1::2])
    space_part = reduce_clip(space_grad)
    ff_sum = joined(ff_shared)
    time_sum = joined(share(sum_half(time_part)))
    early = (
        call_assemble(place, pieces_out),
        columns(time_sum, own, 0, 3),
        columns(time_sum, own, 3, 1),
        columns(ff_sum, own, 0, 4),
        ff_sum[4 * own :].astype(f32),
    )
    space_part, *early = lax.optimization_barrier((space_part,) + early)
    space_sum = joined(share(sum_half(space_part)))
    mine = space_sum[4 * own :].reshape(-1)[: small_rows * own].reshape(small_rows, own).astype(f32)
    return (
        early[0],
        grad_buffer,
        mine[0:3],
        mine[3:6],
        columns(space_sum, own, 0, 3),
        columns(space_sum, own, 3, 1),
        early[1],
        early[2],
        early[3],
        mine[6 + nact : 6 + nact + hb_rows].reshape(-1),
        early[4],
        mine[6 + nact + hb_rows :].reshape(-1),
        mine[6 : 6 + nact],
    )


def solution(mesh):
    rows = P("clip", None)
    cols = P(None, "clip")
    line = P("clip")
    wide = P(None, "tm", "clip", None)
    return jax.shard_map(
        local,
        mesh=mesh,
        in_specs=(
            wide, cols, cols, P(None, None, "tm"), cols, cols,
            rows, rows, rows, rows, rows, line, rows, line, cols, wide,
        ),
        out_specs=(wide, wide, cols, cols, rows, rows, rows, rows, rows, line, rows, line, cols),
        check_vma=False,
    )
```

```python
import functools

import jax
import jax.numpy as jnp
from jax import lax
from jax.experimental import pallas as pl
from jax.experimental.pallas import tpu as pltpu
from jax.sharding import PartitionSpec as P

HEADS = 16
HEAD = 64
EPS = 1e-05
MASKED = -1e30
ROWS = 256
RAISED = (HEADS // 2, ROWS, 2 * ROWS)
FF_CHUNK = 1024
FF_GROUPS = 1
VMEM_LIMIT = 62 * 1024 * 1024

bf16 = jnp.bfloat16
f32 = jnp.float32

NN = (((1,), (0,)), ((), ()))
NT = (((1,), (1,)), ((), ()))
TN = (((0,), (0,)), ((), ()))


def dot(left, right, form=NN):
    return lax.dot_general(left, right, form, preferred_element_type=f32)


def standardize(values):
    centered = values - jnp.mean(values, axis=-1, keepdims=True)
    rate = lax.rsqrt(jnp.mean(centered * centered, axis=-1, keepdims=True) + EPS)
    return centered * rate, rate


def norm_back(hat, rate, gain, grad):
    scaled = grad * gain
    return rate * (
        scaled
        - jnp.mean(scaled, axis=-1, keepdims=True)
        - hat * jnp.mean(scaled * hat, axis=-1, keepdims=True)
    )


def add_row(ref, row, first):
    @pl.when(first)
    def _():
        ref[...] = row

    @pl.when(jnp.logical_not(first))
    def _():
        ref[...] += row


def column_sum(values):
    return jnp.sum(values, axis=0, keepdims=True)


def pair_slices(pair):
    lane = pair * 128
    return slice(lane, lane + 128), slice(1024 + lane, 1024 + lane + 128), slice(2048 + lane, 2048 + lane + 128)


def attend(qkv_ref, key_mask, query_mask, mixed_t, raised_ref, rate_ref):
    blank = jnp.zeros((HEAD, ROWS), bf16)
    scale = jnp.asarray(HEAD**-0.5, bf16)

    def scores_of(pair):
        q_at, k_at, v_at = pair_slices(pair)
        q_t = (qkv_ref[:, q_at] * scale).T
        keys = jnp.concatenate([qkv_ref[:, k_at], key_mask], axis=1)
        first = jnp.concatenate([q_t[:HEAD], blank, query_mask], axis=0)
        second = jnp.concatenate([blank, q_t[HEAD:], query_mask], axis=0)
        return dot(keys, jnp.concatenate([first, second], axis=1))

    def finish(pair, scores):
        v_t = qkv_ref[:, pair_slices(pair)[2]].T
        top = jnp.max(scores, axis=0, keepdims=True)
        raised = jnp.exp(scores - top)
        total = jnp.sum(raised, axis=0, keepdims=True)
        weights = raised.astype(bf16)
        rate = 1.0 / total
        raised_ref[pair] = weights
        for part in range(2):
            head = pair * 2 + part
            at = slice(part * ROWS, (part + 1) * ROWS)
            mixed = dot(v_t[part * HEAD : (part + 1) * HEAD], weights[:, at])
            mixed_t[head * HEAD : (head + 1) * HEAD, :] = (mixed * rate[:, at]).astype(bf16)
            rate_ref[head : head + 1, :] = rate[:, at]

    queue = [scores_of(0), scores_of(1)]
    for pair in range(HEADS // 2):
        if pair + 2 < HEADS // 2:
            queue.append(scores_of(pair + 2))
        finish(pair, queue.pop(0))


def attend_back(qkv_ref, raised_ref, rate_ref, grad_ref, grad_t, mixed_t, out_ref, query_t):
    blank = jnp.zeros((HEAD, ROWS), bf16)
    scale = jnp.asarray(HEAD**-0.5, bf16)
    low_half = lax.broadcasted_iota(jnp.int32, (ROWS, 128), 1) < HEAD
    zero = jnp.zeros((ROWS, 128), bf16)

    def both(top, bottom):
        first = jnp.concatenate([top, blank], axis=0)
        second = jnp.concatenate([blank, bottom], axis=0)
        return jnp.concatenate([first, second], axis=1)

    def halves(values):
        return jnp.concatenate([jnp.where(low_half, values, zero), jnp.where(low_half, zero, values)], axis=0)

    def start(pair):
        q_at, _, v_at = pair_slices(pair)
        pair_t = grad_t[q_at, :]
        return dot(qkv_ref[:, v_at], both(pair_t[:HEAD], pair_t[HEAD:]))

    def finish(pair, grad_probs):
        q_at, k_at, v_at = pair_slices(pair)
        head = pair * 2
        rate = jnp.concatenate([rate_ref[head : head + 1, :], rate_ref[head + 1 : head + 2, :]], axis=1)
        product = grad_t[q_at, :].astype(f32) * mixed_t[q_at, :].astype(f32)
        along = jnp.concatenate([column_sum(product[:HEAD]), column_sum(product[HEAD:])], axis=1)
        probs = raised_ref[pair].astype(f32) * rate
        grad_scores = (probs * (grad_probs - along)).astype(bf16)
        out_ref[:, v_at] = dot(probs.astype(bf16), halves(grad_ref[:, q_at])).astype(bf16)
        out_ref[:, k_at] = dot(grad_scores, halves(qkv_ref[:, q_at] * scale)).astype(bf16)
        k_t = (qkv_ref[:, k_at] * scale).T
        for part in range(2):
            at = slice((head + part) * HEAD, (head + part + 1) * HEAD)
            columns_at = slice(part * ROWS, (part + 1) * ROWS)
            query_t[at, :] = dot(k_t[part * HEAD : (part + 1) * HEAD], grad_scores[:, columns_at]).astype(bf16)

    ahead = start(0)
    for pair in range(HEADS // 2):
        held = ahead
        if pair + 1 < HEADS // 2:
            ahead = start(pair + 1)
        finish(pair, held)
    for quarter in range(4):
        at = slice(quarter * 256, (quarter + 1) * 256)
        out_ref[:, at] = query_t[at, :].T


def block_of(weights, index):
    own = 1024 // weights.shape[0]
    return weights[:, index * own : (index + 1) * own, :].reshape(1024, 1024)


def piece_at(place, step, count, rows):
    return pl.ds(pl.multiple_of(lax.rem(place[0] + step, count) * rows, rows), rows)


def stacked(refs, groups=1):
    per = refs[0].shape[1] // groups
    width = refs[0].shape[-1]
    parts = [ref[:, g * per : (g + 1) * per, :].reshape(-1, width) for g in range(groups) for ref in refs]
    return parts[0] if len(parts) == 1 else jnp.concatenate(parts, axis=0)


def unstack(refs, values, groups=1):
    per = refs[0].shape[1] // groups
    rows = values.shape[0] // (len(refs) * groups)
    for g in range(groups):
        for index, ref in enumerate(refs):
            at = (g * len(refs) + index) * rows
            ref[:, g * per : (g + 1) * per, :] = values[at : at + rows].reshape(ref.shape[0], per, ref.shape[2])


def space_forward(
    place, tok, hot, kmask, qmask, gain, bias, table, weights,
    norm_out, qkv_out, mix_out, lse_out, raised_out, *rest,
):
    after_out, (mixed_t, after) = rest[:-2], rest[-2:]
    embedded = tok[...].astype(f32) + dot(hot[...], table[...])
    hat, _ = standardize(embedded)
    normed = (hat * gain[0:1, :] + bias[0:1, :]).astype(bf16)
    norm_out[...] = normed
    for part in range(3):
        qkv_out[:, part * 1024 : (part + 1) * 1024] = dot(normed, block_of(weights, part)).astype(bf16)
    attend(qkv_out, kmask[...], qmask[...], mixed_t, raised_out, lse_out)
    mixed = mixed_t[...].T
    mix_out[...] = mixed
    after[...] = (embedded + dot(mixed, block_of(weights, 3))).astype(bf16)
    count = len(after_out)
    for step in range(count):
        after_out[step][...] = after[piece_at(place, step, count, ROWS // count), :]


def grad_into_norm(gqkv, weights):
    total = None
    for part in range(3):
        piece = dot(gqkv[:, part * 1024 : (part + 1) * 1024], block_of(weights, part), NT)
        total = piece if total is None else total + piece
    return total


def space_backward(count, *refs):
    grads, refs = refs[:count], refs[count:]
    (
        place, tok, hot, raised, gain, table, weights, qkv, mix, lse,
        gqkv_out, gas_out, tok_out, gain_out, bias_out, table_out, grad_t, mixed_t, query_t, grad_rows,
    ) = refs
    first = pl.program_id(0) == 0
    for step in range(count):
        gas_out[piece_at(place, step, count, ROWS // count), :] = grads[step][...]
    upstream = gas_out[...]
    mixed_t[...] = mix[...].T
    grad_rows[...] = dot(upstream, block_of(weights, 3), NT).astype(bf16)
    grad_t[...] = grad_rows[...].T
    attend_back(qkv, raised, lse, grad_rows, grad_t, mixed_t, gqkv_out, query_t)
    grad_norm = grad_into_norm(gqkv_out, weights)
    embedded = tok[...].astype(f32) + dot(hot[...], table[...])
    hat, rate = standardize(embedded)
    add_row(gain_out, column_sum(grad_norm * hat), first)
    add_row(bias_out, column_sum(grad_norm), first)
    total = upstream.astype(f32) + norm_back(hat, rate, gain[0:1, :], grad_norm)
    tok_out[...] = total
    add_row(table_out, dot(hot[...], total.astype(bf16), TN), first)


def time_forward(count, *refs):
    x, refs = refs[:count], refs[count:]
    kmask, qmask, gain, bias, weights, norm_out, qkv_out, mix_out, lse_out, raised_out, after_out, mixed_t = refs
    after_space = stacked(x).astype(f32)
    hat, _ = standardize(after_space)
    normed = (hat * gain[1:2, :] + bias[1:2, :]).astype(bf16)
    norm_out[...] = normed
    for part in range(3):
        qkv_out[:, part * 1024 : (part + 1) * 1024] = dot(normed, block_of(weights, part)).astype(bf16)
    attend(qkv_out, kmask[...], qmask[...], mixed_t, raised_out, lse_out)
    mixed = mixed_t[...].T
    mix_out[...] = mixed
    after_out[...] = after_space + dot(mixed, block_of(weights, 3))


def feed_forward(count, *refs):
    grad, refs = refs[:count], refs[count:]
    x, gain, bias, hidden_bias, out_bias, weights = refs[:6]
    norm_out, act_out, gpre_out, gat_out, branch_out, gain_out, bias_out, hb_out, ob_out = refs[6:15]
    block_out = refs[15:]
    first = pl.program_id(0) == 0
    clips = weights.shape[0]
    own = 1024 // clips
    groups = x.shape[0]
    width = x.shape[2]
    size = FF_CHUNK
    chunks = 4096 // size
    half = 1024 // size
    share = size * clips // 4096
    branch = stacked(grad, groups)
    branch_out[...] = branch.reshape(branch_out.shape)

    def down_of(chunk):
        if share:
            return weights[chunk * share : (chunk + 1) * share, 4 * own :, :].reshape(size, 1024)
        return None

    def hidden_of(chunk):
        block, column = chunk // half, chunk % half
        return weights[:, block * own : (block + 1) * own, column * size : (column + 1) * size].reshape(1024, size)

    part_at = lambda chunk: slice(chunk * size, (chunk + 1) * size)
    back_act = dot(branch, down_of(0), NT)
    after_time = x[...].reshape(groups * ROWS, width)
    hat, rate = standardize(after_time)
    normed = (hat * gain[2:3, :] + bias[2:3, :]).astype(bf16)
    norm_out[...] = normed.reshape(norm_out.shape)
    pre = dot(normed, hidden_of(0)) + hidden_bias[0:1, part_at(0)]
    result = None
    grad_norm = None
    bias_sums = []
    for chunk in range(chunks):
        at = part_at(chunk)
        u, grad_act = pre, back_act
        if chunk + 1 < chunks:
            pre = dot(normed, hidden_of(chunk + 1)) + hidden_bias[0:1, part_at(chunk + 1)]
            back_act = dot(branch, down_of(chunk + 1), NT)
        c0 = 0.7978845608028654
        square = u * u
        t = jnp.tanh(u * (c0 + (c0 * 0.044715) * square))
        half_plus = 0.5 + 0.5 * t
        act = (u * half_plus).astype(bf16)
        act_out[:, :, at] = act.reshape(groups, ROWS, size)
        slope = half_plus + (0.5 * u) * (1.0 - t * t) * (c0 + (3.0 * c0 * 0.044715) * square)
        gpre = (grad_act * slope).astype(bf16)
        gpre_out[:, :, at] = gpre.reshape(groups, ROWS, size)
        bias_sums.append(column_sum(gpre.astype(f32)))
        down = dot(act, down_of(chunk))
        result = down if result is None else result + down
        back = dot(gpre, hidden_of(chunk), NT)
        grad_norm = back if grad_norm is None else grad_norm + back
    block = (after_time + result + out_bias[0:1, :]).astype(bf16)
    unstack(block_out, block, groups)
    upstream = branch.astype(f32)
    gat = (upstream + norm_back(hat, rate, gain[2:3, :], grad_norm)).astype(bf16)
    gat_out[...] = gat.reshape(gat_out.shape)
    add_row(gain_out, column_sum(grad_norm * hat), first)
    add_row(bias_out, column_sum(grad_norm), first)
    add_row(ob_out, column_sum(upstream), first)
    add_row(hb_out, jnp.concatenate(bias_sums, axis=1), first)


def time_backward(count, *refs):
    x, refs = refs[:count], refs[count:]
    gat, raised, gain, weights, qkv, mix, lse, gqkv_out, gain_out, bias_out = refs[:10]
    gas_out = refs[10 : 10 + count]
    grad_t, mixed_t, query_t, grad_rows = refs[10 + count :]
    first = pl.program_id(0) == 0
    upstream = gat[...]
    mixed_t[...] = mix[...].T
    grad_rows[...] = dot(upstream, block_of(weights, 3), NT).astype(bf16)
    grad_t[...] = grad_rows[...].T
    attend_back(qkv, raised, lse, grad_rows, grad_t, mixed_t, gqkv_out, query_t)
    grad_norm = grad_into_norm(gqkv_out, weights)
    hat, rate = standardize(stacked(x).astype(f32))
    add_row(gain_out, column_sum(grad_norm * hat), first)
    add_row(bias_out, column_sum(grad_norm), first)
    total = upstream.astype(f32) + norm_back(hat, rate, gain[1:2, :], grad_norm)
    unstack(gas_out, total.astype(bf16))


def assemble(count, *refs):
    place, parts, out = refs[0], refs[1:-1], refs[-1]
    for micro in range(out.shape[0]):
        for step in range(count):
            out[micro, piece_at(place, step, count, ROWS // count), :] = parts[micro * count + step][...]


def rows_of(ref):
    value = ref[...]
    return value.reshape(-1, value.shape[-1])


def weight_kernel(pairs, micros, own, by_rows, has_small, *refs):
    out = refs[-1]
    offset = 0
    for pair in range(pairs):
        base = pair * 2 * micros
        total = None
        for index in range(micros):
            piece = dot(rows_of(refs[base + index]), rows_of(refs[base + micros + index]), TN)
            total = piece if total is None else total + piece
        total = total.astype(bf16)
        if by_rows:
            out[...] = total.reshape(out.shape)
            continue
        for block in range(total.shape[1] // 1024):
            for shard in range(out.shape[0]):
                out[shard, offset : offset + own, :] = total[
                    shard * own : (shard + 1) * own, block * 1024 : (block + 1) * 1024
                ]
            offset += own
    if has_small:
        out[:, offset:, :] = refs[pairs * 2 * micros][...]


def params():
    return pltpu.CompilerParams(vmem_limit_bytes=VMEM_LIMIT)


def ordered_call(kernel, behind, in_specs, **options):
    count = len(behind)

    def body(*refs):
        kernel(*refs[count:])

    aliases = options.pop("input_output_aliases", {})
    call = pl.pallas_call(
        body,
        in_specs=[pl.BlockSpec(memory_space=pl.ANY)] * count + in_specs,
        input_output_aliases={count + k: v for k, v in aliases.items()},
        compiler_params=params(),
        **options,
    )
    return lambda *operands: call(*behind, *operands)


def whole(shape):
    rank = len(shape)
    return pl.BlockSpec(shape, lambda i: (0,) * rank, pipeline_mode=pl.Buffered(1))


def total_spec(shape):
    rank = len(shape)
    return pl.BlockSpec(shape, lambda i: (0,) * rank)


def step_spec(shape):
    rank = len(shape)
    return pl.BlockSpec((None,) + shape, lambda i: (i,) + (0,) * rank)


def micro_spec(micro, shape):
    rank = len(shape)
    return pl.BlockSpec((None, None) + shape, lambda i: (micro, i) + (0,) * rank)


def shape_of(shape, kind):
    return jax.ShapeDtypeStruct(shape, kind)


def smem():
    return pl.BlockSpec(memory_space=pltpu.SMEM)


def call_space_forward(behind, micro, place, tok, hot, kmask, qmask, gain, bias, table, weights, count):
    _, frames, slots, width = tok.shape
    per = slots // count
    return ordered_call(
        space_forward,
        behind,
        grid=(frames,),
        in_specs=[smem(), micro_spec(micro, (slots, width)), step_spec(hot.shape[1:])]
        + [whole(a.shape) for a in (kmask, qmask, gain, bias, table, weights)],
        out_specs=[
            step_spec((slots, width)), step_spec((slots, 3 * width)), step_spec((slots, width)),
            step_spec((HEADS, slots)), step_spec(RAISED),
        ]
        + [step_spec((per, width))] * count,
        out_shape=[
            shape_of((frames, slots, width), bf16), shape_of((frames, slots, 3 * width), bf16),
            shape_of((frames, slots, width), bf16), shape_of((frames, HEADS, slots), f32),
            shape_of((frames,) + RAISED, bf16),
        ]
        + [shape_of((frames, per, width), bf16)] * count,
        scratch_shapes=[pltpu.VMEM((width, ROWS), bf16), pltpu.VMEM((ROWS, width), bf16)],
        name="space_forward",
    )(place, tok, hot, kmask, qmask, gain, bias, table, weights)


def back_scratch(width):
    return [
        pltpu.VMEM((width, ROWS), bf16), pltpu.VMEM((width, ROWS), bf16),
        pltpu.VMEM((width, ROWS), bf16), pltpu.VMEM((ROWS, width), bf16),
    ]


def call_space_backward(
    behind, micro, grads, place, tok, hot, raised, gain, table, weights, qkv, mix, lse, buffer
):
    micros, frames, slots, width = tok.shape
    count = len(grads)
    row = shape_of((1, width), f32)
    operands = list(grads) + [place, tok, hot, raised, gain, table, weights, qkv, mix, lse]
    specs = (
        [step_spec((slots // count, width))] * count
        + [smem(), micro_spec(micro, (slots, width)), step_spec(hot.shape[1:]), step_spec(RAISED)]
        + [whole(a.shape) for a in (gain, table, weights)]
        + [step_spec((slots, 3 * width)), step_spec((slots, width)), step_spec((HEADS, slots))]
    )
    before = len(operands)
    kernel = functools.partial(space_backward, count)
    aliases = {}
    if buffer is not None:
        aliases = {before: 2}
        operands.append(buffer)
        specs.append(pl.BlockSpec(memory_space=pl.ANY))
        kernel = lambda *refs: space_backward(count, *refs[:before], *refs[before + 1 :])
    return ordered_call(
        kernel,
        behind,
        grid=(frames,),
        in_specs=specs,
        out_specs=[
            step_spec((slots, 3 * width)), step_spec((slots, width)), micro_spec(micro, (slots, width)),
            total_spec((1, width)), total_spec((1, width)), total_spec((hot.shape[2], width)),
        ],
        out_shape=[
            shape_of((frames, slots, 3 * width), bf16), shape_of((frames, slots, width), bf16),
            shape_of((micros, frames, slots, width), f32), row, row, shape_of((hot.shape[2], width), f32),
        ],
        scratch_shapes=back_scratch(width),
        input_output_aliases=aliases,
        name="space_backward",
    )(*operands)


def group_spec(array, count):
    frames, _, width = array.shape
    return pl.BlockSpec((frames, ROWS // (frames * count), width), lambda i: (0, i, 0))


def call_time_forward(behind, x, kmask, qmask, gain, bias, weights):
    count = len(x)
    frames, slots, width = x[0].shape
    groups = slots * frames * count // ROWS
    return ordered_call(
        functools.partial(time_forward, count),
        behind,
        grid=(groups,),
        in_specs=[group_spec(a, count) for a in x] + [whole(a.shape) for a in (kmask, qmask, gain, bias, weights)],
        out_specs=[
            step_spec((ROWS, width)), step_spec((ROWS, 3 * width)), step_spec((ROWS, width)),
            step_spec((HEADS, ROWS)), step_spec(RAISED), step_spec((ROWS, width)),
        ],
        out_shape=[
            shape_of((groups, ROWS, width), bf16), shape_of((groups, ROWS, 3 * width), bf16),
            shape_of((groups, ROWS, width), bf16), shape_of((groups, HEADS, ROWS), f32),
            shape_of((groups,) + RAISED, bf16), shape_of((groups, ROWS, width), f32),
        ],
        scratch_shapes=[pltpu.VMEM((width, ROWS), bf16)],
        name="time_forward",
    )(*x, kmask, qmask, gain, bias, weights)


def call_feed_forward(behind, grad, x, gain, bias, hidden_bias, out_bias, weights):
    count = len(grad)
    groups, _, width = x.shape
    ff = hidden_bias.shape[1]
    each = FF_GROUPS if groups % FF_GROUPS == 0 else 1
    row = shape_of((1, width), f32)
    rows = lambda cols: shape_of((groups, ROWS, cols), bf16)
    spec = lambda cols: pl.BlockSpec((each, ROWS, cols), lambda i: (i, 0, 0))
    grad_spec = lambda a: pl.BlockSpec(
        (a.shape[0], each * ROWS // (a.shape[0] * count), width), lambda i: (0, i, 0)
    )
    return ordered_call(
        functools.partial(feed_forward, count),
        behind,
        grid=(groups // each,),
        in_specs=[grad_spec(a) for a in grad]
        + [spec(width)]
        + [whole(a.shape) for a in (gain, bias, hidden_bias, out_bias, weights)],
        out_specs=[
            spec(width), spec(ff), spec(ff), spec(width), spec(width),
            total_spec((1, width)), total_spec((1, width)), total_spec((1, ff)), total_spec((1, width)),
        ]
        + [grad_spec(a) for a in grad],
        out_shape=[rows(width), rows(ff), rows(ff), rows(width), rows(width), row, row, shape_of((1, ff), f32), row]
        + [shape_of(a.shape, bf16) for a in grad],
        name="feed_forward",
    )(*grad, x, gain, bias, hidden_bias, out_bias, weights)


def call_time_backward(behind, x, gat, raised, gain, weights, qkv, mix, lse):
    count = len(x)
    groups, _, width = gat.shape
    row = shape_of((1, width), f32)
    return ordered_call(
        functools.partial(time_backward, count),
        behind,
        grid=(groups,),
        in_specs=[group_spec(a, count) for a in x]
        + [step_spec((ROWS, width)), step_spec(RAISED)]
        + [whole(a.shape) for a in (gain, weights)]
        + [step_spec((ROWS, 3 * width)), step_spec((ROWS, width)), step_spec((HEADS, ROWS))],
        out_specs=[step_spec((ROWS, 3 * width)), total_spec((1, width)), total_spec((1, width))]
        + [group_spec(a, count) for a in x],
        out_shape=[shape_of((groups, ROWS, 3 * width), bf16), row, row] + [shape_of(a.shape, bf16) for a in x],
        scratch_shapes=back_scratch(width),
        name="time_backward",
    )(*x, gat, raised, gain, weights, qkv, mix, lse)


def call_assemble(place, parts):
    micros, count = len(parts), len(parts[0])
    frames, per, width = parts[0][0].shape
    flat = [p for pieces in parts for p in pieces]
    return ordered_call(
        functools.partial(assemble, count),
        [],
        grid=(frames,),
        in_specs=[smem()] + [step_spec((per, width))] * len(flat),
        out_specs=pl.BlockSpec((micros, None, per * count, width), lambda i: (0, i, 0, 0)),
        out_shape=shape_of((micros, frames, per * count, width), bf16),
        name="assemble",
    )(place, *flat)


def weight_grad(behind, pairs, clips, rows, name, small=None, down_at=None):
    own = 1024 // clips
    block = 256 if down_at is None else 512
    width = pairs[0][0][0].shape[-1]
    by_rows = down_at is not None

    def left_spec(a):
        rank = a.ndim
        return pl.BlockSpec(a.shape[:-1] + (block,), lambda i: (0,) * (rank - 1) + (i,))

    operands, specs = [], []
    cols = 0
    for lefts, rights in pairs:
        operands += list(lefts) + list(rights)
        specs += [left_spec(a) for a in lefts] + [whole(a.shape) for a in rights]
        cols += rights[0].shape[-1]
    shards = block // own
    if small is not None:
        operands.append(small)
        specs.append(pl.BlockSpec((shards,) + small.shape[1:], lambda i: (i, 0, 0)))
    if by_rows:
        per = width // clips
        out_spec = pl.BlockSpec((block // per, per, 1024), lambda i: (i, down_at // per, 0))
    else:
        out_rows = cols // 1024 * own + (0 if small is None else small.shape[1])
        out_spec = pl.BlockSpec((shards, out_rows, 1024), lambda i: (i, 0, 0))
    return ordered_call(
        functools.partial(weight_kernel, len(pairs), len(pairs[0][0]), own, by_rows, small is not None),
        behind,
        grid=(width // block,),
        in_specs=specs,
        out_specs=out_spec,
        out_shape=shape_of((clips, rows, 1024), bf16),
        name=name,
    )(*operands)


def column_kernel(starts, micros, *refs):
    out = refs[-1]
    step = pl.program_id(0)
    for pair, (start, end) in enumerate(starts):
        lefts = refs[pair * 2 * micros : pair * 2 * micros + micros]
        rights = refs[pair * 2 * micros + micros : (pair + 1) * 2 * micros]

        def fill():
            total = None
            for left, right in zip(lefts, rights):
                piece = dot(rows_of(left), rows_of(right), TN)
                total = piece if total is None else total + piece
            out[...] = total.astype(bf16).reshape(out.shape)

        if len(starts) == 1:
            fill()
        else:
            pl.when(jnp.logical_and(step >= start, step < end))(fill)


def weight_columns(behind, pairs, clips, rows, name, buffer=None):
    own = 1024 // clips
    block = 512
    operands, specs, starts = [], [], []
    step = 0
    for lefts, rights in pairs:
        count = rights[0].shape[-1] // block

        def right_spec(a, start=step, last=count - 1):
            rank = a.ndim
            return pl.BlockSpec(
                a.shape[:-1] + (block,), lambda i: (0,) * (rank - 1) + (jnp.clip(i - start, 0, last),)
            )

        operands += list(lefts) + list(rights)
        specs += [whole(a.shape) for a in lefts] + [right_spec(a) for a in rights]
        starts.append((step, step + count))
        step += count
    kernel = functools.partial(column_kernel, starts, len(pairs[0][0]))
    aliases = {}
    if buffer is not None:
        before = len(operands)
        aliases = {before: 0}
        operands.append(buffer)
        specs.append(pl.BlockSpec(memory_space=pl.ANY))
        inner = kernel
        kernel = lambda *refs: inner(*refs[:before], *refs[before + 1 :])
    return ordered_call(
        kernel,
        behind,
        grid=(step,),
        in_specs=specs,
        out_specs=pl.BlockSpec((clips, own, block), lambda i: (0, i // 2, i % 2)),
        out_shape=shape_of((clips, rows, 1024), bf16),
        input_output_aliases=aliases,
        name=name,
    )(*operands)


def one_hot(index, count, kind=bf16):
    return (index[..., None] == jnp.arange(count)).astype(kind)


def space_masks(labels):
    keys = one_hot(labels, 128)
    queries = jnp.where(labels[None, :] == jnp.arange(128)[:, None], 0.0, MASKED)
    queries = jnp.where(jnp.arange(128)[:, None] < 8, queries, 0.0).astype(bf16)
    return keys, queries


def time_masks(frames, count, me):
    per = ROWS // frames
    row = jnp.arange(ROWS)
    held = frames // count
    frame = jnp.mod(me - row // (held * per), count) * held + row // per % held
    place = row % per
    lane = jnp.arange(128)
    keys = ((lane[None, :] == place[:, None]) | (lane[None, :] == per + frame[:, None])).astype(bf16)
    other = (lane[:, None] < per) & (lane[:, None] != place[None, :])
    later = (lane[:, None] >= per) & (lane[:, None] < per + frames) & (lane[:, None] - per > frame[None, :])
    queries = jnp.where(other | later, MASKED, 0.0).astype(bf16)
    return keys, queries


def action_rows(labels, owners, actions):
    clip_of = jnp.sum(jnp.where(labels[:, None] == jnp.arange(owners.shape[0]), owners[None, :], 0), axis=1)
    hit = clip_of[:, None] == jnp.arange(actions.shape[0])
    chosen = jnp.sum(jnp.where(hit[:, :, None], actions[None], 0), axis=1)
    return jnp.transpose(chosen)


def exchange(values):
    return lax.all_to_all(values, "tm", 0, 0, tiled=True)


def gather(shards):
    own = shards[0].shape[0]
    parts = []
    for shard in shards:
        rows, cols = shard.shape
        parts += [shard[:, at : at + 1024] for at in range(0, cols, 1024)]
    return lax.all_gather(jnp.concatenate(parts, axis=0), "clip", axis=0, tiled=False)


def reduce_clip(total):
    return lax.psum_scatter(total, "clip", scatter_dimension=0, tiled=False)


def shift(values, step):
    count = lax.axis_size("tm")
    return lax.ppermute(values, "tm", [(k, (k + step) % count) for k in range(count)])


def sum_half(part):
    count = lax.axis_size("tm")
    rows = part.shape[0] // count
    me = lax.axis_index("tm")
    piece = lambda step: lax.dynamic_slice_in_dim(part, lax.rem(me + step, count) * rows, rows, axis=0)
    total = piece(0).astype(f32)
    for received in [shift(piece(step), step) for step in range(1, count)]:
        total = total + received.astype(f32)
    return total.astype(bf16)


def share(mine):
    return [mine] + [shift(mine, step) for step in range(1, lax.axis_size("tm"))]


def joined(held):
    count = len(held)
    rows, width = held[0].shape
    me = lax.axis_index("tm")
    values = jnp.zeros((count * rows, width), held[0].dtype)
    for step, piece in enumerate(held):
        values = lax.dynamic_update_slice_in_dim(values, piece, lax.rem(me + count - step, count) * rows, axis=0)
    return values


def together(*lists):
    flat = lax.optimization_barrier([a for arrays in lists for a in arrays])
    out = []
    for arrays in lists:
        out.append(list(flat[: len(arrays)]))
        flat = flat[len(arrays) :]
    return out


def columns(rows, own, first, count):
    return jnp.concatenate([rows[(first + c) * own : (first + c + 1) * own] for c in range(count)], axis=1).astype(f32)


def local(
    tokens, segments, assignment, actions, norm_gain, norm_bias,
    space_in, space_out, time_in, time_out, hidden, hidden_bias, down, out_bias,
    action_table, out_grad,
):
    micros, frames_here, slots, width = tokens.shape
    pieces = lax.axis_size("tm")
    clips = lax.axis_size("clip")
    frames = frames_here * pieces
    per = slots // pieces
    own = norm_gain.shape[1]
    nact = action_table.shape[0]
    micro = range(micros)
    hb_rows = hidden_bias.shape[0] // own
    small_rows = 6 + nact + hb_rows + 1

    small = jnp.concatenate(
        [norm_gain, norm_bias, action_table, hidden_bias.reshape(-1, own), out_bias.reshape(-1, own)], axis=0
    )
    small_all = lax.all_gather(small, "clip", axis=0, tiled=False)
    w_space = gather([space_in, space_out])
    w_time = gather([time_in, time_out])
    w_ff = gather([hidden, down])

    rows_by = lambda start, count: jnp.transpose(small_all[:, start : start + count], (1, 0, 2)).reshape(count, width)
    gain = rows_by(0, 3).astype(f32)
    bias = rows_by(3, 3).astype(f32)
    table = jnp.pad(rows_by(6, nact), ((0, 128 - nact), (0, 0)))
    hb_all = small_all[:, 6 + nact : 6 + nact + hb_rows].reshape(1, -1).astype(f32)
    ob_all = small_all[:, 6 + nact + hb_rows :].reshape(1, -1).astype(f32)

    me = lax.axis_index("tm").astype(jnp.int32)
    place = me.reshape(1)
    tmasks = time_masks(frames, pieces, me)
    hots = [one_hot(action_rows(segments[m], assignment[m], actions[m]), 128) for m in micro]
    smasks = [space_masks(segments[m]) for m in micro]

    pick = lambda parts, index: [parts[m][index] for m in micro]
    outward = lambda parts: [parts[0]] + [
        lax.ppermute(parts[d], "tm", [(k, (k + d) % pieces) for k in range(pieces)]) for d in range(1, pieces)
    ]
    inward = lambda parts: [parts[0]] + [
        lax.ppermute(parts[d], "tm", [(k, (k - d) % pieces) for k in range(pieces)]) for d in range(1, pieces)
    ]
    marks = lambda parts: parts[1:]
    rounded = lambda values, d: lax.dynamic_slice_in_dim(values, (me + d) % pieces * per, per, axis=1).astype(bf16)
    sent = [[rounded(out_grad[m], d) for d in range(pieces)] for m in micro]

    branch = [outward(sent[0])]
    forward, after, middle, ahead, pieces_out, back, gas, last = [], [], [], [], [], [], [], []
    behind = []
    for m in micro:
        forward.append(
            call_space_forward(behind, m, place, tokens, hots[m], *smasks[m], gain, bias, table, w_space, pieces)
        )
        after.append(outward(forward[m][5:]))
        behind = [forward[m][3]] + marks(branch[0])
    for m in micro:
        middle.append(list(call_time_forward(behind, after[m], *tmasks, gain, bias, w_time)))
        behind = [middle[m][3]]
    for m in micro[1:]:
        late, (middle[-1][5],) = together(sent[m], [middle[-1][5]])
        branch.append(outward(late))
    for m in micro:
        ahead.append(call_feed_forward(behind, branch[m], middle[m][5], gain, bias, hb_all, ob_all, w_ff))
        pieces_out.append(inward(ahead[m][9:]))
        behind = [ahead[m][5]]
    behind += marks(pieces_out[0])
    ff_grad = weight_grad(behind, [(pick(ahead, 1), pick(ahead, 4))], clips, 8 * own, "down_grad", down_at=4 * own)
    ff_grad = weight_columns([], [(pick(ahead, 0), pick(ahead, 2))], clips, 8 * own, "hidden_grad", buffer=ff_grad)
    (ff_grad,), pieces_out[-1] = together([ff_grad], pieces_out[-1])
    ff_part = reduce_clip(ff_grad)
    behind = [ff_grad]
    for m in micro:
        back.append(
            call_time_backward(
                behind, after[m], ahead[m][3], middle[m][4], gain, w_time, middle[m][1], middle[m][2], middle[m][3]
            )
        )
        gas.append(inward(back[m][3:]))
        behind = [back[m][1]]
    time_grad = weight_columns(
        behind, [(pick(middle, 0), pick(back, 0)), (pick(middle, 2), pick(ahead, 3))], clips, 4 * own, "time_grad"
    )
    (time_grad,), gas[0] = together([time_grad], gas[0])
    time_part = reduce_clip(time_grad)
    behind = [time_grad]
    grad_buffer = None
    for m in micro:
        last.append(
            list(
                call_space_backward(
                    behind, m, gas[m], place, tokens, hots[m], forward[m][4], gain, table, w_space,
                    forward[m][1], forward[m][2], forward[m][3], grad_buffer,
                )
            )
        )
        grad_buffer = last[m][2]
        behind = []
        if m == 0:
            (ff_part,), (last[m][3],), gas[-1] = together([ff_part], [last[m][3]], gas[-1])
            ff_half = sum_half(ff_part)
            behind = [ff_part]

    total = lambda values: functools.reduce(jnp.add, values)
    gain_grad = jnp.concatenate([total(pick(last, 3)), total(pick(back, 1)), total(pick(ahead, 5))])
    bias_grad = jnp.concatenate([total(pick(last, 4)), total(pick(back, 2)), total(pick(ahead, 6))])
    table_grad = total(pick(last, 5))[:nact]
    hb_grad = total(pick(ahead, 7))
    ob_grad = total(pick(ahead, 8))
    split = lambda a: jnp.transpose(a.reshape(a.shape[0], clips, own), (1, 0, 2))
    small_grads = jnp.concatenate(
        [
            split(gain_grad), split(bias_grad), split(table_grad),
            hb_grad.reshape(clips, hb_rows, own), ob_grad.reshape(clips, 1, own),
        ],
        axis=1,
    ).astype(bf16).reshape(clips, -1)
    extra = 8 * pieces - 4 * own % (8 * pieces)
    small_grads = jnp.pad(small_grads, ((0, 0), (0, extra * 1024 - small_grads.shape[1]))).reshape(clips, extra, 1024)
    block_out = call_assemble(place, pieces_out)
    space_grad = weight_grad(
        [ff_half, block_out], [(pick(forward, 0), pick(last, 0)), (pick(forward, 2), pick(last, 1))],
        clips, 4 * own + extra, "space_grad", small=small_grads,
    )

    ff_shared = share(ff_half)
    (space_grad,), (time_part,), ff_shared[1::2] = together([space_grad], [time_part], ff_shared[1::2])
    space_part = reduce_clip(space_grad)
    ff_sum = joined(ff_shared)
    time_sum = joined(share(sum_half(time_part)))
    early = (
        block_out,
        columns(time_sum, own, 0, 3),
        columns(time_sum, own, 3, 1),
        columns(ff_sum, own, 0, 4),
        ff_sum[4 * own :].astype(f32),
    )
    space_part, *early = lax.optimization_barrier((space_part,) + early)
    space_sum = joined(share(sum_half(space_part)))
    mine = space_sum[4 * own :].reshape(-1)[: small_rows * own].reshape(small_rows, own).astype(f32)
    return (
        early[0],
        grad_buffer,
        mine[0:3],
        mine[3:6],
        columns(space_sum, own, 0, 3),
        columns(space_sum, own, 3, 1),
        early[1],
        early[2],
        early[3],
        mine[6 + nact : 6 + nact + hb_rows].reshape(-1),
        early[4],
        mine[6 + nact + hb_rows :].reshape(-1),
        mine[6 : 6 + nact],
    )


def solution(mesh):
    rows = P("clip", None)
    cols = P(None, "clip")
    line = P("clip")
    wide = P(None, "tm", "clip", None)
    return jax.shard_map(
        local,
        mesh=mesh,
        in_specs=(
            wide, cols, cols, P(None, None, "tm"), cols, cols,
            rows, rows, rows, rows, rows, line, rows, line, cols, wide,
        ),
        out_specs=(wide, wide, cols, cols, rows, rows, rows, rows, rows, line, rows, line, cols),
        check_vma=False,
    )
```

```python
import functools

import jax
import jax.numpy as jnp
from jax import lax
from jax.experimental import pallas as pl
from jax.experimental.pallas import tpu as pltpu
from jax.sharding import PartitionSpec as P

HEADS = 16
HEAD = 64
EPS = 1e-05
MASKED = -1e30
ROWS = 256
RAISED = (HEADS // 2, ROWS, 2 * ROWS)
VMEM_LIMIT = 62 * 1024 * 1024

bf16 = jnp.bfloat16
f32 = jnp.float32

NN = (((1,), (0,)), ((), ()))
NT = (((1,), (1,)), ((), ()))
TN = (((0,), (0,)), ((), ()))


def dot(left, right, form=NN):
    return lax.dot_general(left, right, form, preferred_element_type=f32)


def standardize(values):
    centered = values - jnp.mean(values, axis=-1, keepdims=True)
    rate = lax.rsqrt(jnp.mean(centered * centered, axis=-1, keepdims=True) + EPS)
    return centered * rate, rate


def norm_back(hat, rate, gain, grad):
    scaled = grad * gain
    return rate * (
        scaled
        - jnp.mean(scaled, axis=-1, keepdims=True)
        - hat * jnp.mean(scaled * hat, axis=-1, keepdims=True)
    )


def add_row(ref, row, first):
    @pl.when(first)
    def _():
        ref[...] = row

    @pl.when(jnp.logical_not(first))
    def _():
        ref[...] += row


def column_sum(values):
    return jnp.sum(values, axis=0, keepdims=True)


def pair_slices(pair):
    lane = pair * 128
    return slice(lane, lane + 128), slice(1024 + lane, 1024 + lane + 128), slice(2048 + lane, 2048 + lane + 128)


def attend(qkv_ref, key_mask, query_mask, mixed_t, raised_ref, rate_ref):
    blank = jnp.zeros((HEAD, ROWS), bf16)
    scale = jnp.asarray(HEAD**-0.5, bf16)

    def scores_of(pair):
        q_at, k_at, v_at = pair_slices(pair)
        q_t = (qkv_ref[:, q_at] * scale).T
        keys = jnp.concatenate([qkv_ref[:, k_at], key_mask], axis=1)
        first = jnp.concatenate([q_t[:HEAD], blank, query_mask], axis=0)
        second = jnp.concatenate([blank, q_t[HEAD:], query_mask], axis=0)
        return dot(keys, jnp.concatenate([first, second], axis=1))

    def finish(pair, scores):
        v_t = qkv_ref[:, pair_slices(pair)[2]].T
        top = jnp.max(scores, axis=0, keepdims=True)
        raised = jnp.exp(scores - top)
        total = jnp.sum(raised, axis=0, keepdims=True)
        weights = raised.astype(bf16)
        rate = 1.0 / total
        raised_ref[pair] = weights
        for part in range(2):
            head = pair * 2 + part
            at = slice(part * ROWS, (part + 1) * ROWS)
            mixed = dot(v_t[part * HEAD : (part + 1) * HEAD], weights[:, at])
            mixed_t[head * HEAD : (head + 1) * HEAD, :] = (mixed * rate[:, at]).astype(bf16)
            rate_ref[head : head + 1, :] = rate[:, at]

    queue = [scores_of(0), scores_of(1)]
    for pair in range(HEADS // 2):
        if pair + 2 < HEADS // 2:
            queue.append(scores_of(pair + 2))
        finish(pair, queue.pop(0))


def attend_back(qkv_ref, raised_ref, rate_ref, grad_ref, grad_t, mixed_t, out_ref, query_t):
    blank = jnp.zeros((HEAD, ROWS), bf16)
    scale = jnp.asarray(HEAD**-0.5, bf16)
    low_half = lax.broadcasted_iota(jnp.int32, (ROWS, 128), 1) < HEAD
    zero = jnp.zeros((ROWS, 128), bf16)

    def both(top, bottom):
        first = jnp.concatenate([top, blank], axis=0)
        second = jnp.concatenate([blank, bottom], axis=0)
        return jnp.concatenate([first, second], axis=1)

    def halves(values):
        return jnp.concatenate([jnp.where(low_half, values, zero), jnp.where(low_half, zero, values)], axis=0)

    def start(pair):
        q_at, _, v_at = pair_slices(pair)
        pair_t = grad_t[q_at, :]
        return dot(qkv_ref[:, v_at], both(pair_t[:HEAD], pair_t[HEAD:]))

    def finish(pair, grad_probs):
        q_at, k_at, v_at = pair_slices(pair)
        head = pair * 2
        rate = jnp.concatenate([rate_ref[head : head + 1, :], rate_ref[head + 1 : head + 2, :]], axis=1)
        product = grad_t[q_at, :].astype(f32) * mixed_t[q_at, :].astype(f32)
        along = jnp.concatenate([column_sum(product[:HEAD]), column_sum(product[HEAD:])], axis=1)
        probs = raised_ref[pair].astype(f32) * rate
        grad_scores = (probs * (grad_probs - along)).astype(bf16)
        out_ref[:, v_at] = dot(probs.astype(bf16), halves(grad_ref[:, q_at])).astype(bf16)
        out_ref[:, k_at] = dot(grad_scores, halves(qkv_ref[:, q_at] * scale)).astype(bf16)
        k_t = (qkv_ref[:, k_at] * scale).T
        for part in range(2):
            at = slice((head + part) * HEAD, (head + part + 1) * HEAD)
            columns_at = slice(part * ROWS, (part + 1) * ROWS)
            query_t[at, :] = dot(k_t[part * HEAD : (part + 1) * HEAD], grad_scores[:, columns_at]).astype(bf16)

    ahead = start(0)
    for pair in range(HEADS // 2):
        held = ahead
        if pair + 1 < HEADS // 2:
            ahead = start(pair + 1)
        finish(pair, held)
    for quarter in range(4):
        at = slice(quarter * 256, (quarter + 1) * 256)
        out_ref[:, at] = query_t[at, :].T


def block_of(weights, index):
    own = 1024 // weights.shape[0]
    return weights[:, index * own : (index + 1) * own, :].reshape(1024, 1024)


def piece_at(place, step, count, rows):
    return pl.ds(pl.multiple_of(lax.rem(place[0] + step, count) * rows, rows), rows)


def stacked(refs, groups=1):
    per = refs[0].shape[1] // groups
    width = refs[0].shape[-1]
    parts = [ref[:, g * per : (g + 1) * per, :].reshape(-1, width) for g in range(groups) for ref in refs]
    return parts[0] if len(parts) == 1 else jnp.concatenate(parts, axis=0)


def unstack(refs, values, groups=1):
    per = refs[0].shape[1] // groups
    rows = values.shape[0] // (len(refs) * groups)
    for g in range(groups):
        for index, ref in enumerate(refs):
            at = (g * len(refs) + index) * rows
            ref[:, g * per : (g + 1) * per, :] = values[at : at + rows].reshape(ref.shape[0], per, ref.shape[2])


def space_forward(
    place, tok, hot, kmask, qmask, gain, bias, table, weights,
    norm_out, qkv_out, mix_out, lse_out, raised_out, *rest,
):
    after_out, (mixed_t, after) = rest[:-2], rest[-2:]
    embedded = tok[...].astype(f32) + dot(hot[...], table[...])
    hat, _ = standardize(embedded)
    normed = (hat * gain[0:1, :] + bias[0:1, :]).astype(bf16)
    norm_out[...] = normed
    for part in range(3):
        qkv_out[:, part * 1024 : (part + 1) * 1024] = dot(normed, block_of(weights, part)).astype(bf16)
    attend(qkv_out, kmask[...], qmask[...], mixed_t, raised_out, lse_out)
    mixed = mixed_t[...].T
    mix_out[...] = mixed
    after[...] = (embedded + dot(mixed, block_of(weights, 3))).astype(bf16)
    count = len(after_out)
    for step in range(count):
        after_out[step][...] = after[piece_at(place, step, count, ROWS // count), :]


def grad_into_norm(gqkv, weights):
    total = None
    for part in range(3):
        piece = dot(gqkv[:, part * 1024 : (part + 1) * 1024], block_of(weights, part), NT)
        total = piece if total is None else total + piece
    return total


def space_backward(count, *refs):
    grads, refs = refs[:count], refs[count:]
    (
        place, tok, hot, raised, gain, table, weights, qkv, mix, lse,
        gqkv_out, gas_out, tok_out, gain_out, bias_out, table_out, grad_t, mixed_t, query_t, grad_rows,
    ) = refs
    first = pl.program_id(0) == 0
    for step in range(count):
        gas_out[piece_at(place, step, count, ROWS // count), :] = grads[step][...]
    upstream = gas_out[...]
    mixed_t[...] = mix[...].T
    grad_rows[...] = dot(upstream, block_of(weights, 3), NT).astype(bf16)
    grad_t[...] = grad_rows[...].T
    attend_back(qkv, raised, lse, grad_rows, grad_t, mixed_t, gqkv_out, query_t)
    grad_norm = grad_into_norm(gqkv_out, weights)
    embedded = tok[...].astype(f32) + dot(hot[...], table[...])
    hat, rate = standardize(embedded)
    add_row(gain_out, column_sum(grad_norm * hat), first)
    add_row(bias_out, column_sum(grad_norm), first)
    total = upstream.astype(f32) + norm_back(hat, rate, gain[0:1, :], grad_norm)
    tok_out[...] = total
    add_row(table_out, dot(hot[...], total.astype(bf16), TN), first)


def time_forward(count, *refs):
    x, refs = refs[:count], refs[count:]
    kmask, qmask, gain, bias, weights, norm_out, qkv_out, mix_out, lse_out, raised_out, after_out, mixed_t = refs
    after_space = stacked(x).astype(f32)
    hat, _ = standardize(after_space)
    normed = (hat * gain[1:2, :] + bias[1:2, :]).astype(bf16)
    norm_out[...] = normed
    for part in range(3):
        qkv_out[:, part * 1024 : (part + 1) * 1024] = dot(normed, block_of(weights, part)).astype(bf16)
    attend(qkv_out, kmask[...], qmask[...], mixed_t, raised_out, lse_out)
    mixed = mixed_t[...].T
    mix_out[...] = mixed
    after_out[...] = after_space + dot(mixed, block_of(weights, 3))


def feed_forward(count, *refs):
    grad, refs = refs[:count], refs[count:]
    x, gain, bias, hidden_bias, out_bias, weights_hbm = refs[:6]
    norm_out, act_out, gpre_out, gat_out, branch_out, gain_out, bias_out, hb_out, ob_out = refs[6:15]
    block_out = refs[15 : 15 + count]
    weights, arrived = refs[15 + count :]
    clips = weights.shape[0]
    own = 1024 // clips
    share = clips // 4

    def part_of(ref, index):
        if index < 4:
            return ref.at[:, index * own : (index + 1) * own, :]
        return ref.at[(index - 4) * share : (index - 3) * share, 4 * own :, :]

    def load(index):
        return pltpu.make_async_copy(part_of(weights_hbm, index), part_of(weights, index), arrived.at[index])

    def run(fresh):
        def part(index):
            if fresh and index not in here:
                load(index).wait()
                here.add(index)
            return part_of(weights, index)[...].reshape(1024, 1024)

        def note(ref, row):
            if fresh:
                ref[...] = row
            else:
                ref[...] += row

        here = set()
        if fresh:
            for index in (4, 0, 1, 5, 2, 6, 3, 7):
                load(index).start()
        part_at = lambda chunk: slice(chunk * 1024, (chunk + 1) * 1024)
        branch = stacked(grad)
        branch_out[...] = branch
        after_time = x[...]
        hat, rate = standardize(after_time)
        normed = (hat * gain[2:3, :] + bias[2:3, :]).astype(bf16)
        norm_out[...] = normed
        back_act = dot(branch, part(4), NT)
        pre = dot(normed, part(0)) + hidden_bias[0:1, part_at(0)]
        result = None
        grad_norm = None
        for chunk in range(4):
            at = part_at(chunk)
            u, grad_act = pre, back_act
            if chunk < 3:
                pre = dot(normed, part(chunk + 1)) + hidden_bias[0:1, part_at(chunk + 1)]
                back_act = dot(branch, part(chunk + 5), NT)
            c0 = 0.7978845608028654
            square = u * u
            t = jnp.tanh(u * (c0 + (c0 * 0.044715) * square))
            half_plus = 0.5 + 0.5 * t
            act = (u * half_plus).astype(bf16)
            act_out[:, at] = act
            slope = half_plus + (0.5 * u) * (1.0 - t * t) * (c0 + (3.0 * c0 * 0.044715) * square)
            gpre = (grad_act * slope).astype(bf16)
            gpre_out[:, at] = gpre
            if fresh:
                hb_out[0:1, at] = column_sum(gpre.astype(f32))
            else:
                hb_out[0:1, at] += column_sum(gpre.astype(f32))
            down = dot(act, part(chunk + 4))
            result = down if result is None else result + down
            back = dot(gpre, part(chunk), NT)
            grad_norm = back if grad_norm is None else grad_norm + back
        unstack(block_out, (after_time + result + out_bias[0:1, :]).astype(bf16))
        upstream = branch.astype(f32)
        gat_out[...] = (upstream + norm_back(hat, rate, gain[2:3, :], grad_norm)).astype(bf16)
        note(gain_out, column_sum(grad_norm * hat))
        note(bias_out, column_sum(grad_norm))
        note(ob_out, column_sum(upstream))

    first = pl.program_id(0) == 0
    pl.when(first)(lambda: run(True))
    pl.when(jnp.logical_not(first))(lambda: run(False))


def time_backward(count, *refs):
    x, refs = refs[:count], refs[count:]
    gat, raised, gain, weights, qkv, mix, lse, gqkv_out, gain_out, bias_out = refs[:10]
    gas_out = refs[10 : 10 + count]
    grad_t, mixed_t, query_t, grad_rows = refs[10 + count :]
    first = pl.program_id(0) == 0
    upstream = gat[...]
    mixed_t[...] = mix[...].T
    grad_rows[...] = dot(upstream, block_of(weights, 3), NT).astype(bf16)
    grad_t[...] = grad_rows[...].T
    attend_back(qkv, raised, lse, grad_rows, grad_t, mixed_t, gqkv_out, query_t)
    grad_norm = grad_into_norm(gqkv_out, weights)
    hat, rate = standardize(stacked(x).astype(f32))
    add_row(gain_out, column_sum(grad_norm * hat), first)
    add_row(bias_out, column_sum(grad_norm), first)
    total = upstream.astype(f32) + norm_back(hat, rate, gain[1:2, :], grad_norm)
    unstack(gas_out, total.astype(bf16))


def assemble(count, *refs):
    place, parts, out = refs[0], refs[1:-1], refs[-1]
    for micro in range(out.shape[0]):
        for step in range(count):
            out[micro, piece_at(place, step, count, ROWS // count), :] = parts[micro * count + step][...]


def rows_of(ref):
    value = ref[...]
    return value.reshape(-1, value.shape[-1])


def weight_kernel(pairs, micros, own, by_rows, has_small, *refs):
    out = refs[-1]
    offset = 0
    for pair in range(pairs):
        base = pair * 2 * micros
        total = None
        for index in range(micros):
            piece = dot(rows_of(refs[base + index]), rows_of(refs[base + micros + index]), TN)
            total = piece if total is None else total + piece
        total = total.astype(bf16)
        if by_rows:
            out[...] = total.reshape(out.shape)
            continue
        for block in range(total.shape[1] // 1024):
            for shard in range(out.shape[0]):
                out[shard, offset : offset + own, :] = total[
                    shard * own : (shard + 1) * own, block * 1024 : (block + 1) * 1024
                ]
            offset += own
    if has_small:
        out[:, offset:, :] = refs[pairs * 2 * micros][...]


def params():
    return pltpu.CompilerParams(vmem_limit_bytes=VMEM_LIMIT)


def ordered_call(kernel, behind, in_specs, **options):
    count = len(behind)

    def body(*refs):
        kernel(*refs[count:])

    aliases = options.pop("input_output_aliases", {})
    call = pl.pallas_call(
        body,
        in_specs=[pl.BlockSpec(memory_space=pl.ANY)] * count + in_specs,
        input_output_aliases={count + k: v for k, v in aliases.items()},
        compiler_params=params(),
        **options,
    )
    return lambda *operands: call(*behind, *operands)


def whole(shape):
    rank = len(shape)
    return pl.BlockSpec(shape, lambda i: (0,) * rank, pipeline_mode=pl.Buffered(1))


def total_spec(shape):
    rank = len(shape)
    return pl.BlockSpec(shape, lambda i: (0,) * rank)


def step_spec(shape):
    rank = len(shape)
    return pl.BlockSpec((None,) + shape, lambda i: (i,) + (0,) * rank)


def micro_spec(micro, shape):
    rank = len(shape)
    return pl.BlockSpec((None, None) + shape, lambda i: (micro, i) + (0,) * rank)


def shape_of(shape, kind):
    return jax.ShapeDtypeStruct(shape, kind)


def smem():
    return pl.BlockSpec(memory_space=pltpu.SMEM)


def call_space_forward(behind, micro, place, tok, hot, kmask, qmask, gain, bias, table, weights, count):
    _, frames, slots, width = tok.shape
    per = slots // count
    return ordered_call(
        space_forward,
        behind,
        grid=(frames,),
        in_specs=[smem(), micro_spec(micro, (slots, width)), step_spec(hot.shape[1:])]
        + [whole(a.shape) for a in (kmask, qmask, gain, bias, table, weights)],
        out_specs=[
            step_spec((slots, width)), step_spec((slots, 3 * width)), step_spec((slots, width)),
            step_spec((HEADS, slots)), step_spec(RAISED),
        ]
        + [step_spec((per, width))] * count,
        out_shape=[
            shape_of((frames, slots, width), bf16), shape_of((frames, slots, 3 * width), bf16),
            shape_of((frames, slots, width), bf16), shape_of((frames, HEADS, slots), f32),
            shape_of((frames,) + RAISED, bf16),
        ]
        + [shape_of((frames, per, width), bf16)] * count,
        scratch_shapes=[pltpu.VMEM((width, ROWS), bf16), pltpu.VMEM((ROWS, width), bf16)],
        name="space_forward",
    )(place, tok, hot, kmask, qmask, gain, bias, table, weights)


def back_scratch(width):
    return [
        pltpu.VMEM((width, ROWS), bf16), pltpu.VMEM((width, ROWS), bf16),
        pltpu.VMEM((width, ROWS), bf16), pltpu.VMEM((ROWS, width), bf16),
    ]


def call_space_backward(
    behind, micro, grads, place, tok, hot, raised, gain, table, weights, qkv, mix, lse, buffer
):
    micros, frames, slots, width = tok.shape
    count = len(grads)
    row = shape_of((1, width), f32)
    operands = list(grads) + [place, tok, hot, raised, gain, table, weights, qkv, mix, lse]
    specs = (
        [step_spec((slots // count, width))] * count
        + [smem(), micro_spec(micro, (slots, width)), step_spec(hot.shape[1:]), step_spec(RAISED)]
        + [whole(a.shape) for a in (gain, table, weights)]
        + [step_spec((slots, 3 * width)), step_spec((slots, width)), step_spec((HEADS, slots))]
    )
    before = len(operands)
    kernel = functools.partial(space_backward, count)
    aliases = {}
    if buffer is not None:
        aliases = {before: 2}
        operands.append(buffer)
        specs.append(pl.BlockSpec(memory_space=pl.ANY))
        kernel = lambda *refs: space_backward(count, *refs[:before], *refs[before + 1 :])
    return ordered_call(
        kernel,
        behind,
        grid=(frames,),
        in_specs=specs,
        out_specs=[
            step_spec((slots, 3 * width)), step_spec((slots, width)), micro_spec(micro, (slots, width)),
            total_spec((1, width)), total_spec((1, width)), total_spec((hot.shape[2], width)),
        ],
        out_shape=[
            shape_of((frames, slots, 3 * width), bf16), shape_of((frames, slots, width), bf16),
            shape_of((micros, frames, slots, width), f32), row, row, shape_of((hot.shape[2], width), f32),
        ],
        scratch_shapes=back_scratch(width),
        input_output_aliases=aliases,
        name="space_backward",
    )(*operands)


def group_spec(array, count):
    frames, _, width = array.shape
    return pl.BlockSpec((frames, ROWS // (frames * count), width), lambda i: (0, i, 0))


def call_time_forward(behind, x, kmask, qmask, gain, bias, weights):
    count = len(x)
    frames, slots, width = x[0].shape
    groups = slots * frames * count // ROWS
    return ordered_call(
        functools.partial(time_forward, count),
        behind,
        grid=(groups,),
        in_specs=[group_spec(a, count) for a in x] + [whole(a.shape) for a in (kmask, qmask, gain, bias, weights)],
        out_specs=[
            step_spec((ROWS, width)), step_spec((ROWS, 3 * width)), step_spec((ROWS, width)),
            step_spec((HEADS, ROWS)), step_spec(RAISED), step_spec((ROWS, width)),
        ],
        out_shape=[
            shape_of((groups, ROWS, width), bf16), shape_of((groups, ROWS, 3 * width), bf16),
            shape_of((groups, ROWS, width), bf16), shape_of((groups, HEADS, ROWS), f32),
            shape_of((groups,) + RAISED, bf16), shape_of((groups, ROWS, width), f32),
        ],
        scratch_shapes=[pltpu.VMEM((width, ROWS), bf16)],
        name="time_forward",
    )(*x, kmask, qmask, gain, bias, weights)


def call_feed_forward(behind, grad, x, gain, bias, hidden_bias, out_bias, weights):
    count = len(grad)
    groups, _, width = x.shape
    ff = hidden_bias.shape[1]
    row = shape_of((1, width), f32)
    rows = lambda cols: shape_of((groups, ROWS, cols), bf16)
    return ordered_call(
        functools.partial(feed_forward, count),
        behind,
        grid=(groups,),
        in_specs=[group_spec(a, count) for a in grad]
        + [step_spec((ROWS, width))]
        + [whole(a.shape) for a in (gain, bias, hidden_bias, out_bias)]
        + [pl.BlockSpec(memory_space=pl.ANY)],
        out_specs=[
            step_spec((ROWS, width)), step_spec((ROWS, ff)), step_spec((ROWS, ff)),
            step_spec((ROWS, width)), step_spec((ROWS, width)),
            total_spec((1, width)), total_spec((1, width)), total_spec((1, ff)), total_spec((1, width)),
        ]
        + [group_spec(a, count) for a in grad],
        out_shape=[rows(width), rows(ff), rows(ff), rows(width), rows(width), row, row, shape_of((1, ff), f32), row]
        + [shape_of(a.shape, bf16) for a in grad],
        scratch_shapes=[pltpu.VMEM(weights.shape, bf16), pltpu.SemaphoreType.DMA((8,))],
        name="feed_forward",
    )(*grad, x, gain, bias, hidden_bias, out_bias, weights)


def call_time_backward(behind, x, gat, raised, gain, weights, qkv, mix, lse):
    count = len(x)
    groups, _, width = gat.shape
    row = shape_of((1, width), f32)
    return ordered_call(
        functools.partial(time_backward, count),
        behind,
        grid=(groups,),
        in_specs=[group_spec(a, count) for a in x]
        + [step_spec((ROWS, width)), step_spec(RAISED)]
        + [whole(a.shape) for a in (gain, weights)]
        + [step_spec((ROWS, 3 * width)), step_spec((ROWS, width)), step_spec((HEADS, ROWS))],
        out_specs=[step_spec((ROWS, 3 * width)), total_spec((1, width)), total_spec((1, width))]
        + [group_spec(a, count) for a in x],
        out_shape=[shape_of((groups, ROWS, 3 * width), bf16), row, row] + [shape_of(a.shape, bf16) for a in x],
        scratch_shapes=back_scratch(width),
        name="time_backward",
    )(*x, gat, raised, gain, weights, qkv, mix, lse)


def call_assemble(place, parts):
    micros, count = len(parts), len(parts[0])
    frames, per, width = parts[0][0].shape
    flat = [p for pieces in parts for p in pieces]
    return ordered_call(
        functools.partial(assemble, count),
        [],
        grid=(frames,),
        in_specs=[smem()] + [step_spec((per, width))] * len(flat),
        out_specs=pl.BlockSpec((micros, None, per * count, width), lambda i: (0, i, 0, 0)),
        out_shape=shape_of((micros, frames, per * count, width), bf16),
        name="assemble",
    )(place, *flat)


def weight_grad(behind, pairs, clips, rows, name, small=None, down_at=None):
    own = 1024 // clips
    block = 256 if down_at is None else 512
    width = pairs[0][0][0].shape[-1]
    by_rows = down_at is not None

    def left_spec(a):
        rank = a.ndim
        return pl.BlockSpec(a.shape[:-1] + (block,), lambda i: (0,) * (rank - 1) + (i,))

    operands, specs = [], []
    cols = 0
    for lefts, rights in pairs:
        operands += list(lefts) + list(rights)
        specs += [left_spec(a) for a in lefts] + [whole(a.shape) for a in rights]
        cols += rights[0].shape[-1]
    shards = block // own
    if small is not None:
        operands.append(small)
        specs.append(pl.BlockSpec((shards,) + small.shape[1:], lambda i: (i, 0, 0)))
    if by_rows:
        per = width // clips
        out_spec = pl.BlockSpec((block // per, per, 1024), lambda i: (i, down_at // per, 0))
    else:
        out_rows = cols // 1024 * own + (0 if small is None else small.shape[1])
        out_spec = pl.BlockSpec((shards, out_rows, 1024), lambda i: (i, 0, 0))
    return ordered_call(
        functools.partial(weight_kernel, len(pairs), len(pairs[0][0]), own, by_rows, small is not None),
        behind,
        grid=(width // block,),
        in_specs=specs,
        out_specs=out_spec,
        out_shape=shape_of((clips, rows, 1024), bf16),
        name=name,
    )(*operands)


def column_kernel(starts, micros, *refs):
    out = refs[-1]
    step = pl.program_id(0)
    for pair, (start, end) in enumerate(starts):
        lefts = refs[pair * 2 * micros : pair * 2 * micros + micros]
        rights = refs[pair * 2 * micros + micros : (pair + 1) * 2 * micros]

        def fill():
            total = None
            for left, right in zip(lefts, rights):
                piece = dot(rows_of(left), rows_of(right), TN)
                total = piece if total is None else total + piece
            out[...] = total.astype(bf16).reshape(out.shape)

        if len(starts) == 1:
            fill()
        else:
            pl.when(jnp.logical_and(step >= start, step < end))(fill)


def weight_columns(behind, pairs, clips, rows, name, buffer=None):
    own = 1024 // clips
    block = 512
    operands, specs, starts = [], [], []
    step = 0
    for lefts, rights in pairs:
        count = rights[0].shape[-1] // block

        def right_spec(a, start=step, last=count - 1):
            rank = a.ndim
            return pl.BlockSpec(
                a.shape[:-1] + (block,), lambda i: (0,) * (rank - 1) + (jnp.clip(i - start, 0, last),)
            )

        operands += list(lefts) + list(rights)
        specs += [whole(a.shape) for a in lefts] + [right_spec(a) for a in rights]
        starts.append((step, step + count))
        step += count
    kernel = functools.partial(column_kernel, starts, len(pairs[0][0]))
    aliases = {}
    if buffer is not None:
        before = len(operands)
        aliases = {before: 0}
        operands.append(buffer)
        specs.append(pl.BlockSpec(memory_space=pl.ANY))
        inner = kernel
        kernel = lambda *refs: inner(*refs[:before], *refs[before + 1 :])
    return ordered_call(
        kernel,
        behind,
        grid=(step,),
        in_specs=specs,
        out_specs=pl.BlockSpec((clips, own, block), lambda i: (0, i // 2, i % 2)),
        out_shape=shape_of((clips, rows, 1024), bf16),
        input_output_aliases=aliases,
        name=name,
    )(*operands)


def one_hot(index, count, kind=bf16):
    return (index[..., None] == jnp.arange(count)).astype(kind)


def space_masks(labels):
    keys = one_hot(labels, 128)
    queries = jnp.where(labels[None, :] == jnp.arange(128)[:, None], 0.0, MASKED)
    queries = jnp.where(jnp.arange(128)[:, None] < 8, queries, 0.0).astype(bf16)
    return keys, queries


def time_masks(frames, count, me):
    per = ROWS // frames
    row = jnp.arange(ROWS)
    held = frames // count
    frame = jnp.mod(me - row // (held * per), count) * held + row // per % held
    place = row % per
    lane = jnp.arange(128)
    keys = ((lane[None, :] == place[:, None]) | (lane[None, :] == per + frame[:, None])).astype(bf16)
    other = (lane[:, None] < per) & (lane[:, None] != place[None, :])
    later = (lane[:, None] >= per) & (lane[:, None] < per + frames) & (lane[:, None] - per > frame[None, :])
    queries = jnp.where(other | later, MASKED, 0.0).astype(bf16)
    return keys, queries


def action_rows(labels, owners, actions):
    clip_of = jnp.sum(jnp.where(labels[:, None] == jnp.arange(owners.shape[0]), owners[None, :], 0), axis=1)
    hit = clip_of[:, None] == jnp.arange(actions.shape[0])
    chosen = jnp.sum(jnp.where(hit[:, :, None], actions[None], 0), axis=1)
    return jnp.transpose(chosen)


def exchange(values):
    return lax.all_to_all(values, "tm", 0, 0, tiled=True)


def gather(shards):
    own = shards[0].shape[0]
    parts = []
    for shard in shards:
        rows, cols = shard.shape
        parts += [shard[:, at : at + 1024] for at in range(0, cols, 1024)]
    return lax.all_gather(jnp.concatenate(parts, axis=0), "clip", axis=0, tiled=False)


def reduce_clip(total):
    return lax.psum_scatter(total, "clip", scatter_dimension=0, tiled=False)


def shift(values, step):
    count = lax.axis_size("tm")
    return lax.ppermute(values, "tm", [(k, (k + step) % count) for k in range(count)])


def sum_half(part):
    count = lax.axis_size("tm")
    rows = part.shape[0] // count
    me = lax.axis_index("tm")
    piece = lambda step: lax.dynamic_slice_in_dim(part, lax.rem(me + step, count) * rows, rows, axis=0)
    total = piece(0).astype(f32)
    for received in [shift(piece(step), step) for step in range(1, count)]:
        total = total + received.astype(f32)
    return total.astype(bf16)


def share(mine):
    return [mine] + [shift(mine, step) for step in range(1, lax.axis_size("tm"))]


def joined(held):
    count = len(held)
    rows, width = held[0].shape
    me = lax.axis_index("tm")
    values = jnp.zeros((count * rows, width), held[0].dtype)
    for step, piece in enumerate(held):
        values = lax.dynamic_update_slice_in_dim(values, piece, lax.rem(me + count - step, count) * rows, axis=0)
    return values


def together(*lists):
    flat = lax.optimization_barrier([a for arrays in lists for a in arrays])
    out = []
    for arrays in lists:
        out.append(list(flat[: len(arrays)]))
        flat = flat[len(arrays) :]
    return out


def columns(rows, own, first, count):
    return jnp.concatenate([rows[(first + c) * own : (first + c + 1) * own] for c in range(count)], axis=1).astype(f32)


def local(
    tokens, segments, assignment, actions, norm_gain, norm_bias,
    space_in, space_out, time_in, time_out, hidden, hidden_bias, down, out_bias,
    action_table, out_grad,
):
    micros, frames_here, slots, width = tokens.shape
    pieces = lax.axis_size("tm")
    clips = lax.axis_size("clip")
    frames = frames_here * pieces
    per = slots // pieces
    own = norm_gain.shape[1]
    nact = action_table.shape[0]
    micro = range(micros)
    hb_rows = hidden_bias.shape[0] // own
    small_rows = 6 + nact + hb_rows + 1

    small = jnp.concatenate(
        [norm_gain, norm_bias, action_table, hidden_bias.reshape(-1, own), out_bias.reshape(-1, own)], axis=0
    )
    small_all = lax.all_gather(small, "clip", axis=0, tiled=False)
    w_space = gather([space_in, space_out])
    w_time = gather([time_in, time_out])
    w_ff = gather([hidden, down])

    rows_by = lambda start, count: jnp.transpose(small_all[:, start : start + count], (1, 0, 2)).reshape(count, width)
    gain = rows_by(0, 3).astype(f32)
    bias = rows_by(3, 3).astype(f32)
    table = jnp.pad(rows_by(6, nact), ((0, 128 - nact), (0, 0)))
    hb_all = small_all[:, 6 + nact : 6 + nact + hb_rows].reshape(1, -1).astype(f32)
    ob_all = small_all[:, 6 + nact + hb_rows :].reshape(1, -1).astype(f32)

    me = lax.axis_index("tm").astype(jnp.int32)
    place = me.reshape(1)
    tmasks = time_masks(frames, pieces, me)
    hots = [one_hot(action_rows(segments[m], assignment[m], actions[m]), 128) for m in micro]
    smasks = [space_masks(segments[m]) for m in micro]

    pick = lambda parts, index: [parts[m][index] for m in micro]
    outward = lambda parts: [parts[0]] + [
        lax.ppermute(parts[d], "tm", [(k, (k + d) % pieces) for k in range(pieces)]) for d in range(1, pieces)
    ]
    inward = lambda parts: [parts[0]] + [
        lax.ppermute(parts[d], "tm", [(k, (k - d) % pieces) for k in range(pieces)]) for d in range(1, pieces)
    ]
    marks = lambda parts: parts[1:]
    rounded = lambda values, d: lax.dynamic_slice_in_dim(values, (me + d) % pieces * per, per, axis=1).astype(bf16)
    sent = [[rounded(out_grad[m], d) for d in range(pieces)] for m in micro]

    branch = [outward(sent[0])]
    forward, after, middle, ahead, pieces_out, back, gas, last = [], [], [], [], [], [], [], []
    behind = []
    for m in micro:
        forward.append(
            call_space_forward(behind, m, place, tokens, hots[m], *smasks[m], gain, bias, table, w_space, pieces)
        )
        after.append(outward(forward[m][5:]))
        behind = [forward[m][3]] + marks(branch[0])
    for m in micro:
        middle.append(list(call_time_forward(behind, after[m], *tmasks, gain, bias, w_time)))
        behind = [middle[m][3]]
    for m in micro[1:]:
        late, (middle[-1][5],) = together(sent[m], [middle[-1][5]])
        branch.append(outward(late))
    for m in micro:
        ahead.append(call_feed_forward(behind, branch[m], middle[m][5], gain, bias, hb_all, ob_all, w_ff))
        pieces_out.append(inward(ahead[m][9:]))
        behind = [ahead[m][5]]
    behind += marks(pieces_out[0])
    ff_grad = weight_grad(behind, [(pick(ahead, 1), pick(ahead, 4))], clips, 8 * own, "down_grad", down_at=4 * own)
    ff_grad = weight_columns([], [(pick(ahead, 0), pick(ahead, 2))], clips, 8 * own, "hidden_grad", buffer=ff_grad)
    (ff_grad,), pieces_out[-1] = together([ff_grad], pieces_out[-1])
    ff_part = reduce_clip(ff_grad)
    behind = [ff_grad]
    for m in micro:
        back.append(
            call_time_backward(
                behind, after[m], ahead[m][3], middle[m][4], gain, w_time, middle[m][1], middle[m][2], middle[m][3]
            )
        )
        gas.append(inward(back[m][3:]))
        behind = [back[m][1]]
    time_grad = weight_columns(
        behind, [(pick(middle, 0), pick(back, 0)), (pick(middle, 2), pick(ahead, 3))], clips, 4 * own, "time_grad"
    )
    (time_grad,), gas[0] = together([time_grad], gas[0])
    time_part = reduce_clip(time_grad)
    behind = [time_grad]
    grad_buffer = None
    for m in micro:
        last.append(
            list(
                call_space_backward(
                    behind, m, gas[m], place, tokens, hots[m], forward[m][4], gain, table, w_space,
                    forward[m][1], forward[m][2], forward[m][3], grad_buffer,
                )
            )
        )
        grad_buffer = last[m][2]
        behind = []
        if m == 0:
            (ff_part,), (last[m][3],), gas[-1] = together([ff_part], [last[m][3]], gas[-1])
            ff_half = sum_half(ff_part)
            behind = [ff_part]

    total = lambda values: functools.reduce(jnp.add, values)
    gain_grad = jnp.concatenate([total(pick(last, 3)), total(pick(back, 1)), total(pick(ahead, 5))])
    bias_grad = jnp.concatenate([total(pick(last, 4)), total(pick(back, 2)), total(pick(ahead, 6))])
    table_grad = total(pick(last, 5))[:nact]
    hb_grad = total(pick(ahead, 7))
    ob_grad = total(pick(ahead, 8))
    split = lambda a: jnp.transpose(a.reshape(a.shape[0], clips, own), (1, 0, 2))
    small_grads = jnp.concatenate(
        [
            split(gain_grad), split(bias_grad), split(table_grad),
            hb_grad.reshape(clips, hb_rows, own), ob_grad.reshape(clips, 1, own),
        ],
        axis=1,
    ).astype(bf16).reshape(clips, -1)
    extra = 8 * pieces - 4 * own % (8 * pieces)
    small_grads = jnp.pad(small_grads, ((0, 0), (0, extra * 1024 - small_grads.shape[1]))).reshape(clips, extra, 1024)
    block_out = call_assemble(place, pieces_out)
    space_grad = weight_grad(
        [ff_half, block_out], [(pick(forward, 0), pick(last, 0)), (pick(forward, 2), pick(last, 1))],
        clips, 4 * own + extra, "space_grad", small=small_grads,
    )

    ff_shared = share(ff_half)
    (space_grad,), (time_part,), ff_shared[1::2] = together([space_grad], [time_part], ff_shared[1::2])
    space_part = reduce_clip(space_grad)
    ff_sum = joined(ff_shared)
    time_sum = joined(share(sum_half(time_part)))
    early = (
        block_out,
        columns(time_sum, own, 0, 3),
        columns(time_sum, own, 3, 1),
        columns(ff_sum, own, 0, 4),
        ff_sum[4 * own :].astype(f32),
    )
    space_part, *early = lax.optimization_barrier((space_part,) + early)
    space_sum = joined(share(sum_half(space_part)))
    mine = space_sum[4 * own :].reshape(-1)[: small_rows * own].reshape(small_rows, own).astype(f32)
    return (
        early[0],
        grad_buffer,
        mine[0:3],
        mine[3:6],
        columns(space_sum, own, 0, 3),
        columns(space_sum, own, 3, 1),
        early[1],
        early[2],
        early[3],
        mine[6 + nact : 6 + nact + hb_rows].reshape(-1),
        early[4],
        mine[6 + nact + hb_rows :].reshape(-1),
        mine[6 : 6 + nact],
    )


def solution(mesh):
    rows = P("clip", None)
    cols = P(None, "clip")
    line = P("clip")
    wide = P(None, "tm", "clip", None)
    return jax.shard_map(
        local,
        mesh=mesh,
        in_specs=(
            wide, cols, cols, P(None, None, "tm"), cols, cols,
            rows, rows, rows, rows, rows, line, rows, line, cols, wide,
        ),
        out_specs=(wide, wide, cols, cols, rows, rows, rows, rows, rows, line, rows, line, cols),
        check_vma=False,
    )
```
